256 devices in a mesh: gx: 4 (over x), gy: 8 (over z), gz: 8 (over y, core).
Axes of the slice: x: 4, y: 4, z: 8, core: 2. Of those that a mesh axis runs over, the one named last changes fastest.
Arguments:
- rhs: float32 [7, 7, 7, 4, 32, 1024], P(None, None, None, 'gx', 'gy', 'gz'), may hold values from -6 to 6
- orders: int32 [4, 32, 1024], P('gx', 'gy', 'gz'), may hold values from 3 to 6
Outputs:
- smoothed: float32 [7, 7, 7, 4, 32, 1024], P(None, None, None, 'gx', 'gy', 'gz')
- coarse_residual: float32 [4, 32, 1024], P('gx', 'gy')
The draws below stay inside these ranges and needn't reach their ends.
All inputs are finite; a program needn't handle non-finite values.
Results may differ from the reference program's by a relative error of at most 0.00016.
Values sent between devices are 32-bit elements; how exact they have to be, the bound alone decides.
No kernel may reach another device: no remote copies, remote signals or barrier semaphores. Data moves between devices by JAX's collectives and lax.ppermute only.
A program may use at most 64 MiB of HBM per device.

```python
import jax
import jax.numpy as jnp
import numpy as np
from jax import lax

MODES = 7
NX = 4
NY = 32
NZ = 1024


def set_ends(drawn, own_key, smallest, largest):
    dims = drawn.shape
    spot = [jax.random.randint(jax.random.fold_in(own_key, axis), (), 0, dims[axis]) for axis in range(len(dims))]
    drawn = drawn.at[tuple(spot)].set(smallest)
    longest = dims.index(max(dims))
    spot[longest] = (spot[longest] + 1) % dims[longest]
    return drawn.at[tuple(spot)].set(largest)


def block_levels(key, dims, pieces, smallest, largest):
    factor_of, own = 1.0, jax.random.fold_in(key, 6)
    for dim, blocks in pieces:
        draws = jnp.exp(jax.random.uniform(jax.random.fold_in(own, dim), (blocks,), jnp.float32, smallest / len(pieces), largest / len(pieces)))
        factor_of = factor_of * jnp.repeat(draws, dims[dim] // blocks).reshape([-1 if axis == dim else 1 for axis in range(len(dims))])
    return factor_of


def scatter_about(stream_key, shape, width, most, shards=(), dtype=jnp.bfloat16):
    values = jax.random.normal(stream_key, shape, jnp.float32) * width
    if len(shards) > 0:
        values = block_levels(stream_key, shape, shards, -0.22, 0.18) * values
    return jnp.clip(values, min=-most, max=most).astype(dtype)


def setup_inputs(seed: int = 0) -> dict:
    key_list = jax.random.split(jax.random.key(seed), 3)
    return {
        "rhs": scatter_about(key_list[0], (MODES, MODES, MODES, NX, NY, NZ), 1.0, 6.0, ((3, 4), (4, 8), (5, 8)), jnp.float32),
        "orders": set_ends(jax.random.randint(key_list[1], (NX, NY, NZ), 3, 7), jax.random.fold_in(key_list[1], 1), 3, 6).astype(jnp.int32),
    }


PENALTY = 49.0
EIGEN_HIGH = 2.4
EIGEN_LOW = 0.24
PRECISE = lax.Precision.HIGHEST

def basis_tables():
    degree = np.arange(7)
    normed = np.sqrt((2.0 * degree + 1.0) / 2.0)
    smaller = np.minimum(degree[:, None], degree[None, :])
    parity = (degree[:, None] + degree[None, :]) % 2 == 0
    stiffness = np.where(parity, normed[:, None] * normed[None, :] * smaller * (smaller + 1), 0.0)
    signs = (-1.0) ** degree
    slope = normed * degree * (degree + 1) / 2.0
    traces = np.stack([normed * signs, -slope * signs, normed, slope])
    stiff_diag = normed * normed * degree * (degree + 1)
    one_axis = stiff_diag + 2.0 * (PENALTY * normed * normed - normed * slope)
    diagonal = (one_axis[:, None, None] + one_axis[None, :, None] + one_axis[None, None, :]) / PENALTY
    highest = np.maximum(np.maximum(degree[:, None, None], degree[None, :, None]), degree[None, None, :])
    third = np.sqrt(1.5) / 3.0
    vertex = np.array([[np.sqrt(0.5), np.sqrt(0.5)], [-third, third]])
    return (stiffness, traces, diagonal, highest, vertex)

def face_stack(field, direction, traces):
    return jnp.stack([jnp.tensordot(traces[row], field, axes=(0, direction), precision=PRECISE) for row in range(4)])

def place(vector, plane, direction):
    return jnp.moveaxis(vector.reshape((7,) + (1,) * plane.ndim) * plane[None], 0, direction)

def middle(array, axis_cells, start):
    return lax.slice_in_dim(array, start, start + array.shape[axis_cells] - 2, axis=axis_cells)

def flux(extended, direction, traces):
    axis_cells = 3 + direction
    own = middle(extended, axis_cells, 1)
    lower = middle(extended, axis_cells, 0)
    upper = middle(extended, axis_cells, 2)
    jump_up = own[2] - upper[0]
    mean_up = 0.5 * (own[3] + upper[1])
    jump_low = lower[2] - own[0]
    mean_low = 0.5 * (lower[3] + own[1])
    result = place(traces[2], PENALTY * jump_up - mean_up, direction) - 0.5 * place(traces[3], jump_up, direction)
    return result + place(traces[0], mean_low - PENALTY * jump_low, direction) - 0.5 * place(traces[1], jump_low, direction)

def rim_stacks(padded, traces):
    stacks = []
    for direction in range(3):
        index = [slice(None)] * 6
        for other in range(3):
            if other != direction:
                index[3 + other] = slice(1, -1)
        stacks.append(face_stack(padded[tuple(index)], direction, traces))
    return stacks

def operate(field, mask, stacks, stiffness, traces):
    total = jnp.zeros_like(field)
    for direction in range(3):
        total = total + jnp.moveaxis(jnp.tensordot(stiffness, field, axes=(1, direction), precision=PRECISE), 0, direction)
        total = total + flux(stacks[direction], direction, traces)
    return mask * total / PENALTY

def carry_global(pair, axis_cells):
    leading = pair[1]
    count = leading.shape[axis_cells]
    moved = jnp.concatenate([jnp.zeros_like(lax.slice_in_dim(leading, 0, 1, axis=axis_cells)), lax.slice_in_dim(leading, 0, count - 1, axis=axis_cells)], axis=axis_cells)
    return pair[0] + moved

def reference(rhs, orders):
    tables = basis_tables()
    stiffness = jnp.asarray(tables[0], jnp.float32)
    traces = jnp.asarray(tables[1], jnp.float32)
    diagonal = jnp.asarray(tables[2], jnp.float32)
    highest = jnp.asarray(tables[3], jnp.int32)
    vertex = jnp.asarray(tables[4], jnp.float32)
    mask = (highest[:, :, :, None, None, None] <= orders[None, None, None]).astype(jnp.float32)
    inv_diag = mask / diagonal[:, :, :, None, None, None]

    def apply(field):
        padded = jnp.pad(field, ((0, 0),) * 3 + ((1, 1),) * 3)
        return operate(field, mask, rim_stacks(padded, traces), stiffness, traces)
    theta = 0.5 * (EIGEN_HIGH + EIGEN_LOW)
    delta = 0.5 * (EIGEN_HIGH - EIGEN_LOW)
    rho_first = delta / theta
    rho_second = 1.0 / (2.0 * theta / delta - rho_first)
    forcing = mask * rhs
    first = inv_diag * forcing / theta
    resid_one = forcing - apply(first)
    smoothed = first + (rho_second * rho_first * first + 2.0 * rho_second / delta * (inv_diag * resid_one))
    resid_two = forcing - apply(smoothed)
    corner = jnp.einsum('ai,bj,ck,abcxyz->ijkxyz', vertex, vertex, vertex, resid_two[:2, :2, :2], precision=PRECISE)
    along_x = carry_global(corner, 2)
    along_y = carry_global(along_x, 2)
    along_z = carry_global(along_y, 2)
    inside_x = (jnp.arange(NX) > 0).astype(jnp.float32)
    inside_y = (jnp.arange(NY) > 0).astype(jnp.float32)
    inside_z = (jnp.arange(NZ) > 0).astype(jnp.float32)
    interior = inside_x[:, None, None] * inside_y[None, :, None] * inside_z[None, None, :]
    return (smoothed, along_z * interior)
```

```python
import jax
import jax.numpy as jnp
import numpy as np
from jax import lax
from jax.experimental import pallas as pl
from jax.experimental.pallas import tpu as pltpu
from jax.sharding import PartitionSpec as P

PENALTY = 49.0
EIGEN_HIGH = 2.4
EIGEN_LOW = 0.24
THETA = 0.5 * (EIGEN_HIGH + EIGEN_LOW)
DELTA = 0.5 * (EIGEN_HIGH - EIGEN_LOW)
RHO_FIRST = DELTA / THETA
RHO_SECOND = 1.0 / (2.0 * THETA / DELTA - RHO_FIRST)
MODES = 7
PAIRS = 4
FACE_ROWS = 14


def basis_tables():
    degree = np.arange(MODES)
    normed = np.sqrt((2.0 * degree + 1.0) / 2.0)
    smaller = np.minimum(degree[:, None], degree[None, :])
    parity = (degree[:, None] + degree[None, :]) % 2 == 0
    stiffness = np.where(parity, normed[:, None] * normed[None, :] * smaller * (smaller + 1), 0.0)
    signs = (-1.0) ** degree
    slope = normed * degree * (degree + 1) / 2.0
    high, high_slope = normed, slope
    low, low_slope = normed * signs, -slope * signs
    own = (
        stiffness
        + PENALTY * (np.outer(high, high) + np.outer(low, low))
        - 0.5 * (np.outer(high, high_slope) + np.outer(high_slope, high))
        + 0.5 * (np.outer(low, low_slope) + np.outer(low_slope, low))
    )
    own = np.where(parity, own, 0.0)
    to_next = np.outer(low, 0.5 * high_slope - PENALTY * high) - 0.5 * np.outer(low_slope, high)
    to_last = np.outer(high, -PENALTY * low - 0.5 * low_slope) + 0.5 * np.outer(high_slope, low)
    one_axis = normed * normed * degree * (degree + 1) + 2.0 * (
        PENALTY * normed * normed - normed * slope
    )
    third = np.sqrt(1.5) / 3.0
    vertex = np.zeros((MODES, 2))
    vertex[0] = np.sqrt(0.5)
    vertex[1] = -third, third
    spread = np.stack(
        [
            vertex[:, 0] @ to_last,
            vertex[:, 1] @ to_last + vertex[:, 0] @ own,
            vertex[:, 1] @ own + vertex[:, 0] @ to_next,
            vertex[:, 1] @ to_next,
        ]
    )
    return normed, slope, own, one_axis, spread, third


NORMED, SLOPE, OWN, ONE_AXIS, SPREAD, THIRD = basis_tables()
ROOT_HALF = float(np.sqrt(0.5))


def diag(a, b, e):
    return float((ONE_AXIS[a] + ONE_AXIS[b] + ONE_AXIS[e]) / PENALTY)


def half_mask():
    return lax.broadcasted_iota(jnp.int32, (8, 128), 0) < 4


def row_in_half():
    return lax.broadcasted_iota(jnp.int32, (8, 128), 0) % 4


def lanes():
    return lax.broadcasted_iota(jnp.int32, (8, 128), 1)


def swap(value):
    return pltpu.roll(value, 4, 0)


class Pairs:
    def __init__(self):
        self.top = half_mask()
        self.known = {}

    def __call__(self, upper, lower):
        key = (float(upper), float(lower))
        if key[0] == key[1]:
            return jnp.float32(key[0])
        if key not in self.known:
            self.known[key] = jnp.where(self.top, jnp.float32(key[0]), jnp.float32(key[1]))
        return self.known[key]

    def once(self, upper, lower):
        if float(upper) == float(lower):
            return jnp.float32(upper)
        return jnp.where(self.top, jnp.float32(upper), jnp.float32(lower))


def total(terms):
    terms = list(terms)
    while len(terms) > 1:
        terms = [
            terms[k] + terms[k + 1] if k + 1 < len(terms) else terms[k]
            for k in range(0, len(terms), 2)
        ]
    return terms[0]


def keep_masks(orders, top):
    both = jnp.concatenate([orders, orders], axis=0)
    known = {}

    def get(upper, lower):
        if (upper, lower) not in known:
            if upper == lower:
                bound = jnp.int32(upper)
            else:
                bound = jnp.where(top, jnp.int32(upper), jnp.int32(lower))
            known[upper, lower] = (both >= bound).astype(jnp.float32)
        return known[upper, lower]

    return get


def odd_of(pair):
    return min(2 * pair + 1, MODES - 1)


def line_traces(line):
    even = total(float(NORMED[n]) * line[n] for n in range(0, MODES, 2))
    odd = total(float(NORMED[n]) * line[n] for n in range(1, MODES, 2))
    even_slope = total(float(SLOPE[n]) * line[n] for n in range(2, MODES, 2))
    odd_slope = total(float(SLOPE[n]) * line[n] for n in range(1, MODES, 2))
    return even + odd, even_slope + odd_slope, even - odd, odd_slope - even_slope


def trace_kernel(
    rhs, orders, first, x_up, x_down, y_up, y_down, z_up, z_down, y_low, y_high, z_low, z_high
):
    pairs = Pairs()
    top = pairs.top
    keep = keep_masks(orders[0], top)
    row, lane = row_in_half(), lanes()
    for b in range(MODES):
        for e in range(MODES):
            column = []
            for i in range(PAIRS):
                upper = rhs[2 * i, b, e, 0]
                lower = rhs[2 * i + 1, b, e, 0] if 2 * i + 1 < MODES else jnp.zeros_like(upper)
                cell = jnp.concatenate([upper, lower], axis=0)
                mask = keep(max(2 * i, b, e), max(odd_of(i), b, e))
                scale = pairs.once(
                    1.0 / (THETA * diag(2 * i, b, e)), 1.0 / (THETA * diag(odd_of(i), b, e))
                )
                cell = cell * mask * scale
                first[i, b, e] = cell
                column.append(cell)
            odd = [odd_of(i) if 2 * i + 1 < MODES else None for i in range(PAIRS)]
            value = total(
                pairs(NORMED[2 * i], NORMED[odd[i]] if odd[i] else 0.0) * column[i]
                for i in range(PAIRS)
            )
            slope = total(
                pairs(SLOPE[2 * i], SLOPE[odd[i]] if odd[i] else 0.0) * column[i]
                for i in range(PAIRS)
            )
            sign = pairs(1.0, -1.0)
            both_value = sign * value + swap(value)
            both_value = jnp.where(top, value + swap(value), swap(value) - value)
            both_slope = jnp.where(top, slope + swap(slope), slope - swap(slope))
            x_up[b * MODES + e] = jnp.where(top, both_value, swap(both_slope))
            x_down[b * MODES + e] = jnp.where(top, swap(both_value), both_slope)
    packed_up = packed_down = None
    for kind in range(2):
        for i in range(PAIRS):
            for e in range(MODES):
                m = i * MODES + e
                q = m % 4
                line = [first[i, b, e] for b in range(MODES)]
                traces = line_traces(line)
                high, low = traces[kind], traces[2 + kind]
                y_high[kind, m] = high
                y_low[kind, m] = low
                up, down = pltpu.roll(high, 5 + q, 0), pltpu.roll(low, q, 0) if q else low
                packed_up = up if q == 0 else jnp.where(row == q, up, packed_up)
                packed_down = down if q == 0 else jnp.where(row == q, down, packed_down)
                if q == 3:
                    y_up[kind * 7 + m // 4] = packed_up
                    y_down[kind * 7 + m // 4] = packed_down
    packed_up = packed_down = jnp.zeros((8, 128), jnp.float32)
    for i in range(PAIRS):
        for b in range(MODES):
            m = i * MODES + b
            line = [first[i, b, e] for e in range(MODES)]
            traces = line_traces(line)
            for kind in range(2):
                high, low = traces[kind], traces[2 + kind]
                z_high[kind, m] = high
                z_low[kind, m] = low
                place = 2 * m + kind
                packed_up = jnp.where(lane == place, pltpu.roll(high, 1 + place, 1), packed_up)
                down = pltpu.roll(low, place, 1) if place else low
                packed_down = jnp.where(lane == place, down, packed_down)
    z_up[...] = packed_up
    z_down[...] = packed_down


def own_kernel(first, out):
    pairs = Pairs()
    for b in range(MODES):
        for e in range(MODES):
            column = [first[i, b, e] for i in range(PAIRS)]
            for i in range(PAIRS):
                terms = []
                for j in range(PAIRS):
                    lower = OWN[2 * i + 1, 2 * j + 1] if max(i, j) < 3 else 0.0
                    terms.append(pairs(OWN[2 * i, 2 * j], lower) * column[j])
                out[i, b, e] = total(terms)
    for i in range(PAIRS):
        for b in range(MODES):
            line = [first[i, b, e] for e in range(MODES)]
            for n in range(MODES):
                out[i, b, n] += total(
                    float(OWN[n, k]) * line[k] for k in range(n % 2, MODES, 2)
                )
        for e in range(MODES):
            line = [first[i, b, e] for b in range(MODES)]
            for n in range(MODES):
                out[i, n, e] += total(
                    float(OWN[n, k]) * line[k] for k in range(n % 2, MODES, 2)
                )


def neighbour_line(low_value, low_slope, high_value, high_slope):
    plus, minus = high_value + low_value, high_value - low_value
    even = 0.5 * (low_slope - high_slope) - PENALTY * plus
    odd = -0.5 * (low_slope + high_slope) - PENALTY * minus
    return (even, 0.5 * plus), (odd, 0.5 * minus)


def vertex_pair(first_mode, second_mode):
    base, tilt = ROOT_HALF * first_mode, THIRD * second_mode
    return base - tilt, base + tilt


def sum_to_vertices(grid, pairs, row, lane):
    top = pairs.top
    rows = {}
    for (dy, dz), value in grid.items():
        rows.setdefault(dy, []).append((dz, value))
    result = [[[], []], [[], []]]
    for dy, entries in rows.items():
        inner, outer = [], []
        for dz, value in entries:
            if dz == 0:
                inner.append(value)
                continue
            moved = pltpu.roll(value, dz % 128, 1)
            inside = lane >= dz if dz > 0 else lane < 128 + dz
            inner.append(jnp.where(inside, moved, 0.0))
            outer.append(jnp.where(inside, 0.0, moved))
        for beyond, terms in ((0, inner), (1, outer)):
            if not terms:
                continue
            value = total(terms)
            if dy == 0:
                result[0][beyond].append(value)
                continue
            moved = pltpu.roll(value, dy % 8, 0)
            inside = row >= dy if dy > 0 else row < 4 + dy
            result[0][beyond].append(jnp.where(inside, moved, 0.0))
            result[1][beyond].append(jnp.where(inside, 0.0, swap(moved)))
    return [[total(result[r][z]) for z in range(2)] for r in range(2)]


def finish_kernel(
    first, local, orders, x_low, x_high, y_low, y_high, z_low, z_high,
    y_below, y_above, z_below, z_above, smoothed, here, ahead, behind, far, field,
):
    pairs = Pairs()
    top = pairs.top
    row, lane = row_in_half(), lanes()
    keep = keep_masks(orders[0], top)

    def inside(axis, distance):
        place = lax.axis_index(axis) + distance
        return jnp.where((place >= 0) & (place < lax.axis_size(axis)), 1.0, 0.0).astype(
            jnp.float32
        )

    x_has_low, x_has_high = inside("gx", -1), inside("gx", 1)
    y_has_low, y_has_high = inside("gy", -1), inside("gy", 1)
    z_has_low, z_has_high = inside("gz", -1), inside("gz", 1)
    for b in range(MODES):
        for e in range(MODES):
            below = x_has_low * x_low[b * MODES + e]
            above = x_has_high * x_high[b * MODES + e]
            plus, minus = above + below, swap(above - below)
            slope = 0.5 * jnp.where(top, plus, minus)
            value = (-2.0 * PENALTY) * slope - 0.5 * jnp.where(top, minus, plus)
            for i in range(PAIRS):
                last = 2 * i + 1 >= MODES
                k = odd_of(i)
                local[i, b, e] += (
                    pairs(NORMED[2 * i], 0.0 if last else NORMED[k]) * value
                    + pairs(SLOPE[2 * i], 0.0 if last else SLOPE[k]) * slope
                )
    for i in range(PAIRS):
        for e in range(MODES):
            m = i * MODES + e
            q = m % 4
            seen = []
            for kind in range(2):
                halo = y_has_low * y_low[kind * 7 + m // 4]
                halo = pltpu.roll(halo, 8 - q, 0) if q else halo
                moved = pltpu.roll(y_below[kind, m], 1, 0)
                seen.append(jnp.where(row == 0, halo, moved))
            for kind in range(2):
                halo = y_has_high * y_high[kind * 7 + m // 4]
                halo = pltpu.roll(halo, 3 - q, 0) if q < 3 else halo
                moved = pltpu.roll(y_above[kind, m], 7, 0)
                seen.append(jnp.where(row == 3, halo, moved))
            parts = neighbour_line(*seen)
            for n in range(MODES):
                value, slope = parts[n % 2]
                add = float(NORMED[n]) * value
                local[i, n, e] += add + float(SLOPE[n]) * slope if n else add
    z_low_halo, z_high_halo = z_has_low * z_low[...], z_has_high * z_high[...]
    for i in range(PAIRS):
        for b in range(MODES):
            m = i * MODES + b
            seen = []
            for kind in range(2):
                place = 2 * m + kind
                halo = pltpu.roll(z_low_halo, 128 - place, 1) if place else z_low_halo
                moved = pltpu.roll(z_below[kind, m], 1, 1)
                seen.append(jnp.where(lane == 0, halo, moved))
            for kind in range(2):
                place = 2 * m + kind
                halo = pltpu.roll(z_high_halo, 127 - place, 1)
                moved = pltpu.roll(z_above[kind, m], 127, 1)
                seen.append(jnp.where(lane == 127, halo, moved))
            parts = neighbour_line(*seen)
            for e in range(MODES):
                value, slope = parts[e % 2]
                add = float(NORMED[e]) * value
                if e:
                    add = add + float(SLOPE[e]) * slope
                applied = local[i, b, e] + add
                one = 2.0 * RHO_SECOND / (DELTA * PENALTY)
                scale = pairs.once(one / diag(2 * i, b, e), one / diag(odd_of(i), b, e))
                mask = keep(max(2 * i, b, e), max(odd_of(i), b, e))
                kappa = 1.0 + RHO_SECOND * RHO_FIRST + 2.0 * RHO_SECOND * THETA / DELTA
                after = kappa * first[i, b, e] - (mask * scale) * applied
                field[i, b, e] = after
                smoothed[2 * i, b, e, 0] = after[:4]
                if 2 * i + 1 < MODES:
                    smoothed[2 * i + 1, b, e, 0] = after[4:]

    grid = {}

    def add(key, value):
        grid[key] = grid[key] + value if key in grid else value

    spread = -SPREAD / PENALTY
    for e in range(MODES):
        low, high = vertex_pair(field[0, 0, e], field[0, 1, e])
        for dz in range(-1, 3):
            add((0, dz), float(spread[dz + 1, e]) * low)
            add((1, dz), float(spread[dz + 1, e]) * high)
    for b in range(MODES):
        low, high = vertex_pair(field[0, b, 0], field[0, b, 1])
        for dy in range(-1, 3):
            add((dy, 0), float(spread[dy + 1, b]) * low)
            add((dy, 1), float(spread[dy + 1, b]) * high)
    force = [
        [
            pairs.once(THETA * diag(0, b, e), THETA * diag(1, b, e)) * first[0, b, e]
            for e in range(2)
        ]
        for b in range(2)
    ]
    force = [vertex_pair(force[0][e], force[1][e]) for e in range(2)]
    for dy in range(2):
        low, high = vertex_pair(force[0][dy], force[1][dy])
        add((dy, 0), low)
        add((dy, 1), high)
    kept, turned = pairs(ROOT_HALF, THIRD), pairs(-THIRD, ROOT_HALF)
    near = {key: kept * value + turned * swap(value) for key, value in grid.items()}
    outer = {}
    corners = []
    for i in range(PAIRS):
        line = [vertex_pair(field[i, 0, e], field[i, 1, e]) for e in range(2)]
        corners.append([vertex_pair(line[0][dy], line[1][dy]) for dy in range(2)])
    for dy in range(2):
        for dz in range(2):
            sums = []
            for dx in range(-1, 3):
                part = total(
                    pairs(
                        spread[dx + 1, 2 * i],
                        spread[dx + 1, 2 * i + 1] if 2 * i + 1 < MODES else 0.0,
                    )
                    * corners[i][dy][dz]
                    for i in range(PAIRS)
                )
                sums.append(part + swap(part))
            near[dy, dz] += jnp.where(top, sums[1], sums[2])
            outer[dy, dz] = jnp.where(top, sums[0], sums[3])
    near = sum_to_vertices(near, pairs, row, lane)
    outer = sum_to_vertices(outer, pairs, row, lane)
    for z in range(2):
        here[z] = jnp.where(top, near[0][z], swap(near[1][z]))
        ahead[z] = jnp.where(top, swap(near[0][z]), near[1][z])
        behind[z] = jnp.where(top, outer[0][z], swap(outer[1][z]))
        far[z] = jnp.where(top, swap(outer[0][z]), outer[1][z])


def shape(*dims):
    return jax.ShapeDtypeStruct(dims, jnp.float32)


def in_vmem(count):
    return [pl.BlockSpec(memory_space=pltpu.VMEM)] * count


def call(kernel, name, inputs, outputs, flops, scratch=(), alias=None):
    size = sum(4 * int(np.prod(o.shape)) for o in outputs) + sum(
        4 * int(np.prod(v.shape)) for v in inputs
    )
    return pl.pallas_call(
        kernel,
        out_shape=outputs,
        in_specs=in_vmem(len(inputs)),
        out_specs=in_vmem(len(outputs)),
        scratch_shapes=list(scratch),
        input_output_aliases=alias or {},
        name=name,
        cost_estimate=pl.CostEstimate(flops=flops, bytes_accessed=size, transcendentals=0),
        compiler_params=pltpu.CompilerParams(vmem_limit_bytes=24 * 1024 * 1024),
    )(*inputs)


def shift(value, axis, distance):
    count = lax.axis_size(axis)
    return lax.ppermute(value, axis, [(i, (i + distance) % count) for i in range(count)])


def inside(axis, distance):
    place = lax.axis_index(axis) + distance
    return ((place >= 0) & (place < lax.axis_size(axis))).astype(jnp.float32)


def per_device(rhs, orders):
    cells = (PAIRS, MODES, MODES, 8, 128)
    first, x_up, x_down, y_up, y_down, z_up, z_down, y_low, y_high, z_low, z_high = call(
        trace_kernel,
        "face_traces",
        (rhs, orders),
        (
            shape(*cells), shape(49, 8, 128), shape(49, 8, 128),
            shape(FACE_ROWS, 8, 128), shape(FACE_ROWS, 8, 128), shape(8, 128), shape(8, 128),
            shape(2, 28, 8, 128), shape(2, 28, 8, 128), shape(2, 28, 8, 128), shape(2, 28, 8, 128),
        ),
        4_000_000,
    )
    x_from_low, x_from_high = shift(x_up, "gx", 1), shift(x_down, "gx", -1)
    y_from_low, y_from_high = shift(y_up, "gy", 1), shift(y_down, "gy", -1)
    z_from_low, z_from_high = shift(z_up, "gz", 1), shift(z_down, "gz", -1)
    (local,) = call(own_kernel, "own_cells", (first,), (shape(*cells),), 4_000_000)
    smoothed, here, ahead, behind, far = call(
        finish_in_place,
        "smooth_and_restrict",
        (
            first, local, orders, x_from_low, x_from_high, y_from_low, y_from_high,
            z_from_low, z_from_high, y_high, y_low, z_high, z_low,
        ),
        (shape(*rhs.shape),) + (shape(2, 8, 128),) * 4,
        5_000_000,
        scratch=(pltpu.VMEM(cells, jnp.float32), pltpu.VMEM(cells, jnp.float32)),
    )
    sums = (
        here
        + inside("gx", -1) * shift(ahead, "gx", 1)
        + inside("gx", 1) * shift(behind, "gx", -1)
        + inside("gx", -2) * shift(far, "gx", 2)
    )
    from_low, from_high = shift(sums, "gy", 1), shift(sums, "gy", -1)
    row = lax.broadcasted_iota(jnp.int32, (1, 4, 1), 1)
    owned = (
        sums[:, :4]
        + jnp.where(row < 2, from_low[:, 4:], 0.0) * inside("gy", -1)
        + jnp.where(row == 3, from_high[:, 4:], 0.0) * inside("gy", 1)
    )
    return smoothed, gather_columns(owned)


def finish_in_place(
    first, local, orders, x_low, x_high, y_low, y_high, z_low, z_high,
    y_below, y_above, z_below, z_above, smoothed, here, ahead, behind, far, field, work,
):
    work[...] = local[...]
    finish_kernel(
        first, work, orders, x_low, x_high, y_low, y_high, z_low, z_high,
        y_below, y_above, z_below, z_above, smoothed, here, ahead, behind, far, field,
    )


def gather_columns(owned):
    count = lax.axis_size("gz")
    packed = owned.reshape(8, 128)
    me = lax.axis_index("gz")
    other = lax.ppermute(packed, "gz", [(i, i ^ 1) for i in range(count)])
    even = me % 2 == 0
    chip = jnp.stack([jnp.where(even, packed, other), jnp.where(even, other, packed)])
    chips = [chip] + [shift(chip, "gz", -2 * k) for k in range(1, count // 2)]
    blocks = jnp.concatenate(chips)
    blocks = jnp.roll(blocks, me - me % 2, axis=0)
    lane = lax.broadcasted_iota(jnp.int32, (1, 1, 128), 2)
    inner, outer = blocks[:, :4], blocks[:, 4:]
    zero = jnp.zeros_like(outer[:1])
    before = jnp.concatenate([zero, outer[:-1]])
    after = jnp.concatenate([outer[1:], zero])
    column = inner + jnp.where(lane < 2, before, 0.0) + jnp.where(lane == 127, after, 0.0)
    column = column.transpose(1, 0, 2).reshape(1, 4, 128 * count)
    place_y = lax.axis_index("gy") * 4 + jnp.arange(4)
    place_z = jnp.arange(128 * count)
    interior = (
        (lax.axis_index("gx") > 0) & (place_y > 0)[:, None] & (place_z > 0)[None, :]
    )
    return jnp.where(interior[None], column, 0.0)


def solution(mesh):
    return jax.shard_map(
        per_device,
        mesh=mesh,
        in_specs=(P(None, None, None, "gx", "gy", "gz"), P("gx", "gy", "gz")),
        out_specs=(P(None, None, None, "gx", "gy", "gz"), P("gx", "gy", None)),
        check_vma=False,
    )
```

```python
import jax
import jax.numpy as jnp
import numpy as np
from jax import lax
from jax.experimental import pallas as pl
from jax.experimental.pallas import tpu as pltpu
from jax.sharding import PartitionSpec as P

PENALTY = 49.0
EIGEN_HIGH = 2.4
EIGEN_LOW = 0.24
THETA = 0.5 * (EIGEN_HIGH + EIGEN_LOW)
DELTA = 0.5 * (EIGEN_HIGH - EIGEN_LOW)
RHO_FIRST = DELTA / THETA
RHO_SECOND = 1.0 / (2.0 * THETA / DELTA - RHO_FIRST)
MODES = 7
PAIRS = 4
FACE_ROWS = 14


def basis_tables():
    degree = np.arange(MODES)
    normed = np.sqrt((2.0 * degree + 1.0) / 2.0)
    smaller = np.minimum(degree[:, None], degree[None, :])
    parity = (degree[:, None] + degree[None, :]) % 2 == 0
    stiffness = np.where(parity, normed[:, None] * normed[None, :] * smaller * (smaller + 1), 0.0)
    signs = (-1.0) ** degree
    slope = normed * degree * (degree + 1) / 2.0
    high, high_slope = normed, slope
    low, low_slope = normed * signs, -slope * signs
    own = (
        stiffness
        + PENALTY * (np.outer(high, high) + np.outer(low, low))
        - 0.5 * (np.outer(high, high_slope) + np.outer(high_slope, high))
        + 0.5 * (np.outer(low, low_slope) + np.outer(low_slope, low))
    )
    own = np.where(parity, own, 0.0)
    to_next = np.outer(low, 0.5 * high_slope - PENALTY * high) - 0.5 * np.outer(low_slope, high)
    to_last = np.outer(high, -PENALTY * low - 0.5 * low_slope) + 0.5 * np.outer(high_slope, low)
    one_axis = normed * normed * degree * (degree + 1) + 2.0 * (
        PENALTY * normed * normed - normed * slope
    )
    third = np.sqrt(1.5) / 3.0
    vertex = np.zeros((MODES, 2))
    vertex[0] = np.sqrt(0.5)
    vertex[1] = -third, third
    spread = np.stack(
        [
            vertex[:, 0] @ to_last,
            vertex[:, 1] @ to_last + vertex[:, 0] @ own,
            vertex[:, 1] @ own + vertex[:, 0] @ to_next,
            vertex[:, 1] @ to_next,
        ]
    )
    return normed, slope, own, one_axis, spread, third


NORMED, SLOPE, OWN, ONE_AXIS, SPREAD, THIRD = basis_tables()
ROOT_HALF = float(np.sqrt(0.5))


def diag(a, b, e):
    return float((ONE_AXIS[a] + ONE_AXIS[b] + ONE_AXIS[e]) / PENALTY)


def half_mask():
    return lax.broadcasted_iota(jnp.int32, (8, 128), 0) < 4


def row_in_half():
    return lax.broadcasted_iota(jnp.int32, (8, 128), 0) % 4


def lanes():
    return lax.broadcasted_iota(jnp.int32, (8, 128), 1)


def swap(value):
    return pltpu.roll(value, 4, 0)


class Pairs:
    def __init__(self):
        self.top = half_mask()
        self.known = {}

    def __call__(self, upper, lower):
        key = (float(upper), float(lower))
        if key[0] == key[1]:
            return jnp.float32(key[0])
        if key not in self.known:
            self.known[key] = jnp.where(self.top, jnp.float32(key[0]), jnp.float32(key[1]))
        return self.known[key]

    def once(self, upper, lower):
        if float(upper) == float(lower):
            return jnp.float32(upper)
        return jnp.where(self.top, jnp.float32(upper), jnp.float32(lower))


def total(terms):
    terms = list(terms)
    while len(terms) > 1:
        terms = [
            terms[k] + terms[k + 1] if k + 1 < len(terms) else terms[k]
            for k in range(0, len(terms), 2)
        ]
    return terms[0]


def keep_masks(orders, top):
    both = jnp.concatenate([orders, orders], axis=0)
    known = {}

    def get(upper, lower):
        if (upper, lower) not in known:
            if upper == lower:
                bound = jnp.int32(upper)
            else:
                bound = jnp.where(top, jnp.int32(upper), jnp.int32(lower))
            known[upper, lower] = (both >= bound).astype(jnp.float32)
        return known[upper, lower]

    return get


def odd_of(pair):
    return min(2 * pair + 1, MODES - 1)


def line_traces(line):
    even = total(float(NORMED[n]) * line[n] for n in range(0, MODES, 2))
    odd = total(float(NORMED[n]) * line[n] for n in range(1, MODES, 2))
    even_slope = total(float(SLOPE[n]) * line[n] for n in range(2, MODES, 2))
    odd_slope = total(float(SLOPE[n]) * line[n] for n in range(1, MODES, 2))
    return even + odd, even_slope + odd_slope, even - odd, odd_slope - even_slope


def trace_kernel(
    rhs_hbm, orders_hbm, first, x_up, x_down, y_up, y_down, z_up, z_down, y_low, y_high, z_low,
    z_high, orders, rhs, arrived,
):
    copies = [pltpu.make_async_copy(orders_hbm, orders, arrived.at[MODES])]
    for b in range(MODES):
        copies.append(pltpu.make_async_copy(rhs_hbm.at[:, b], rhs.at[:, b], arrived.at[b]))
    for copy in copies:
        copy.start()
    pairs = Pairs()
    top = pairs.top
    row, lane = row_in_half(), lanes()
    copies[0].wait()
    keep = keep_masks(orders[0], top)
    for b in range(MODES):
        copies[1 + b].wait()
        for e in range(MODES):
            column = []
            for i in range(PAIRS):
                upper = rhs[2 * i, b, e, 0]
                lower = rhs[2 * i + 1, b, e, 0] if 2 * i + 1 < MODES else jnp.zeros_like(upper)
                cell = jnp.concatenate([upper, lower], axis=0)
                mask = keep(max(2 * i, b, e), max(odd_of(i), b, e))
                scale = pairs.once(
                    1.0 / (THETA * diag(2 * i, b, e)), 1.0 / (THETA * diag(odd_of(i), b, e))
                )
                cell = cell * mask * scale
                first[i, b, e] = cell
                column.append(cell)
            odd = [odd_of(i) if 2 * i + 1 < MODES else None for i in range(PAIRS)]
            value = total(
                pairs(NORMED[2 * i], NORMED[odd[i]] if odd[i] else 0.0) * column[i]
                for i in range(PAIRS)
            )
            slope = total(
                pairs(SLOPE[2 * i], SLOPE[odd[i]] if odd[i] else 0.0) * column[i]
                for i in range(PAIRS)
            )
            both_value = jnp.where(top, value + swap(value), swap(value) - value)
            both_slope = jnp.where(top, slope + swap(slope), slope - swap(slope))
            x_up[b * MODES + e] = jnp.where(top, both_value, swap(both_slope))
            x_down[b * MODES + e] = jnp.where(top, swap(both_value), both_slope)
    packed_up = packed_down = None
    for kind in range(2):
        for i in range(PAIRS):
            for e in range(MODES):
                m = i * MODES + e
                q = m % 4
                line = [first[i, b, e] for b in range(MODES)]
                traces = line_traces(line)
                high, low = traces[kind], traces[2 + kind]
                y_high[kind, m] = high
                y_low[kind, m] = low
                up, down = pltpu.roll(high, 5 + q, 0), pltpu.roll(low, q, 0) if q else low
                packed_up = up if q == 0 else jnp.where(row == q, up, packed_up)
                packed_down = down if q == 0 else jnp.where(row == q, down, packed_down)
                if q == 3:
                    y_up[kind * 7 + m // 4] = packed_up
                    y_down[kind * 7 + m // 4] = packed_down
    packed_up = packed_down = jnp.zeros((8, 128), jnp.float32)
    for i in range(PAIRS):
        for b in range(MODES):
            m = i * MODES + b
            line = [first[i, b, e] for e in range(MODES)]
            traces = line_traces(line)
            for kind in range(2):
                high, low = traces[kind], traces[2 + kind]
                z_high[kind, m] = high
                z_low[kind, m] = low
                place = 2 * m + kind
                packed_up = jnp.where(lane == place, pltpu.roll(high, 1 + place, 1), packed_up)
                down = pltpu.roll(low, place, 1) if place else low
                packed_down = jnp.where(lane == place, down, packed_down)
    z_up[...] = packed_up
    z_down[...] = packed_down


def own_kernel(first, out):
    pairs = Pairs()
    for b in range(MODES):
        for e in range(MODES):
            column = [first[i, b, e] for i in range(PAIRS)]
            for i in range(PAIRS):
                terms = []
                for j in range(PAIRS):
                    lower = OWN[2 * i + 1, 2 * j + 1] if max(i, j) < 3 else 0.0
                    terms.append(pairs(OWN[2 * i, 2 * j], lower) * column[j])
                out[i, b, e] = total(terms)
    for i in range(PAIRS):
        for b in range(MODES):
            line = [first[i, b, e] for e in range(MODES)]
            for n in range(MODES):
                out[i, b, n] += total(
                    float(OWN[n, k]) * line[k] for k in range(n % 2, MODES, 2)
                )
        for e in range(MODES):
            line = [first[i, b, e] for b in range(MODES)]
            for n in range(MODES):
                out[i, n, e] += total(
                    float(OWN[n, k]) * line[k] for k in range(n % 2, MODES, 2)
                )


def neighbour_line(low_value, low_slope, high_value, high_slope):
    plus, minus = high_value + low_value, high_value - low_value
    even = 0.5 * (low_slope - high_slope) - PENALTY * plus
    odd = -0.5 * (low_slope + high_slope) - PENALTY * minus
    return (even, 0.5 * plus), (odd, 0.5 * minus)


def vertex_pair(first_mode, second_mode):
    base, tilt = ROOT_HALF * first_mode, THIRD * second_mode
    return base - tilt, base + tilt


def sum_to_vertices(grid, pairs, row, lane):
    top = pairs.top
    rows = {}
    for (dy, dz), value in grid.items():
        rows.setdefault(dy, []).append((dz, value))
    result = [[[], []], [[], []]]
    for dy, entries in rows.items():
        inner, outer = [], []
        for dz, value in entries:
            if dz == 0:
                inner.append(value)
                continue
            moved = pltpu.roll(value, dz % 128, 1)
            inside = lane >= dz if dz > 0 else lane < 128 + dz
            inner.append(jnp.where(inside, moved, 0.0))
            outer.append(jnp.where(inside, 0.0, moved))
        for beyond, terms in ((0, inner), (1, outer)):
            if not terms:
                continue
            value = total(terms)
            if dy == 0:
                result[0][beyond].append(value)
                continue
            moved = pltpu.roll(value, dy % 8, 0)
            inside = row >= dy if dy > 0 else row < 4 + dy
            result[0][beyond].append(jnp.where(inside, moved, 0.0))
            result[1][beyond].append(jnp.where(inside, 0.0, swap(moved)))
    return [[total(result[r][z]) for z in range(2)] for r in range(2)]


def finish_kernel(
    first, local, orders, x_low, x_high, y_low, y_high, z_low, z_high,
    y_below, y_above, z_below, z_above, field, here, ahead, behind, far,
):
    pairs = Pairs()
    top = pairs.top
    row, lane = row_in_half(), lanes()
    keep = keep_masks(orders[0], top)

    def inside(axis, distance):
        place = lax.axis_index(axis) + distance
        return jnp.where((place >= 0) & (place < lax.axis_size(axis)), 1.0, 0.0).astype(
            jnp.float32
        )

    x_has_low, x_has_high = inside("gx", -1), inside("gx", 1)
    y_has_low, y_has_high = inside("gy", -1), inside("gy", 1)
    z_has_low, z_has_high = inside("gz", -1), inside("gz", 1)
    for b in range(MODES):
        for e in range(MODES):
            below = x_has_low * x_low[b * MODES + e]
            above = x_has_high * x_high[b * MODES + e]
            plus, minus = above + below, swap(above - below)
            slope = 0.5 * jnp.where(top, plus, minus)
            value = (-2.0 * PENALTY) * slope - 0.5 * jnp.where(top, minus, plus)
            for i in range(PAIRS):
                last = 2 * i + 1 >= MODES
                k = odd_of(i)
                local[i, b, e] += (
                    pairs(NORMED[2 * i], 0.0 if last else NORMED[k]) * value
                    + pairs(SLOPE[2 * i], 0.0 if last else SLOPE[k]) * slope
                )
    for i in range(PAIRS):
        for e in range(MODES):
            m = i * MODES + e
            q = m % 4
            seen = []
            for kind in range(2):
                halo = y_has_low * y_low[kind * 7 + m // 4]
                halo = pltpu.roll(halo, 8 - q, 0) if q else halo
                moved = pltpu.roll(y_below[kind, m], 1, 0)
                seen.append(jnp.where(row == 0, halo, moved))
            for kind in range(2):
                halo = y_has_high * y_high[kind * 7 + m // 4]
                halo = pltpu.roll(halo, 3 - q, 0) if q < 3 else halo
                moved = pltpu.roll(y_above[kind, m], 7, 0)
                seen.append(jnp.where(row == 3, halo, moved))
            parts = neighbour_line(*seen)
            for n in range(MODES):
                value, slope = parts[n % 2]
                add = float(NORMED[n]) * value
                local[i, n, e] += add + float(SLOPE[n]) * slope if n else add
    z_low_halo, z_high_halo = z_has_low * z_low[...], z_has_high * z_high[...]
    for i in range(PAIRS):
        for b in range(MODES):
            m = i * MODES + b
            seen = []
            for kind in range(2):
                place = 2 * m + kind
                halo = pltpu.roll(z_low_halo, 128 - place, 1) if place else z_low_halo
                moved = pltpu.roll(z_below[kind, m], 1, 1)
                seen.append(jnp.where(lane == 0, halo, moved))
            for kind in range(2):
                place = 2 * m + kind
                halo = pltpu.roll(z_high_halo, 127 - place, 1)
                moved = pltpu.roll(z_above[kind, m], 127, 1)
                seen.append(jnp.where(lane == 127, halo, moved))
            parts = neighbour_line(*seen)
            for e in range(MODES):
                value, slope = parts[e % 2]
                add = float(NORMED[e]) * value
                if e:
                    add = add + float(SLOPE[e]) * slope
                applied = local[i, b, e] + add
                one = 2.0 * RHO_SECOND / (DELTA * PENALTY)
                scale = pairs.once(one / diag(2 * i, b, e), one / diag(odd_of(i), b, e))
                mask = keep(max(2 * i, b, e), max(odd_of(i), b, e))
                kappa = 1.0 + RHO_SECOND * RHO_FIRST + 2.0 * RHO_SECOND * THETA / DELTA
                after = kappa * first[i, b, e] - (mask * scale) * applied
                field[i, b, e] = after

    grid = {}

    def add(key, value):
        grid[key] = grid[key] + value if key in grid else value

    spread = -SPREAD / PENALTY
    for e in range(MODES):
        low, high = vertex_pair(field[0, 0, e], field[0, 1, e])
        for dz in range(-1, 3):
            add((0, dz), float(spread[dz + 1, e]) * low)
            add((1, dz), float(spread[dz + 1, e]) * high)
    for b in range(MODES):
        low, high = vertex_pair(field[0, b, 0], field[0, b, 1])
        for dy in range(-1, 3):
            add((dy, 0), float(spread[dy + 1, b]) * low)
            add((dy, 1), float(spread[dy + 1, b]) * high)
    force = [
        [
            pairs.once(THETA * diag(0, b, e), THETA * diag(1, b, e)) * first[0, b, e]
            for e in range(2)
        ]
        for b in range(2)
    ]
    force = [vertex_pair(force[0][e], force[1][e]) for e in range(2)]
    for dy in range(2):
        low, high = vertex_pair(force[0][dy], force[1][dy])
        add((dy, 0), low)
        add((dy, 1), high)
    kept, turned = pairs(ROOT_HALF, THIRD), pairs(-THIRD, ROOT_HALF)
    near = {key: kept * value + turned * swap(value) for key, value in grid.items()}
    outer = {}
    corners = []
    for i in range(PAIRS):
        line = [vertex_pair(field[i, 0, e], field[i, 1, e]) for e in range(2)]
        corners.append([vertex_pair(line[0][dy], line[1][dy]) for dy in range(2)])
    for dy in range(2):
        for dz in range(2):
            sums = []
            for dx in range(-1, 3):
                part = total(
                    pairs(
                        spread[dx + 1, 2 * i],
                        spread[dx + 1, 2 * i + 1] if 2 * i + 1 < MODES else 0.0,
                    )
                    * corners[i][dy][dz]
                    for i in range(PAIRS)
                )
                sums.append(part + swap(part))
            near[dy, dz] += jnp.where(top, sums[1], sums[2])
            outer[dy, dz] = jnp.where(top, sums[0], sums[3])
    near = sum_to_vertices(near, pairs, row, lane)
    outer = sum_to_vertices(outer, pairs, row, lane)
    for z in range(2):
        here[z] = jnp.where(top, near[0][z], swap(near[1][z]))
        ahead[z] = jnp.where(top, swap(near[0][z]), near[1][z])
        behind[z] = jnp.where(top, outer[0][z], swap(outer[1][z]))
        far[z] = jnp.where(top, swap(outer[0][z]), outer[1][z])


def unpack_kernel(field, smoothed):
    for b in range(MODES):
        for e in range(MODES):
            for i in range(PAIRS):
                value = field[i, b, e]
                smoothed[2 * i, b, e, 0] = value[:4]
                if 2 * i + 1 < MODES:
                    smoothed[2 * i + 1, b, e, 0] = value[4:]


def column_kernel(own, other, next_chip, over_chip, last_chip, column, blocks):
    count = lax.axis_size("gz")
    me = lax.axis_index("gz")
    mate = me + 1 - 2 * lax.rem(me, 2)
    zero = jnp.zeros((8, 128), jnp.float32)
    blocks[0] = zero
    blocks[count + 1] = zero
    blocks[me + 1] = own[...]
    blocks[mate + 1] = other[...]
    for k, chip in ((1, next_chip), (2, over_chip), (3, last_chip)):
        blocks[lax.rem(me + 2 * k, count) + 1] = chip[0]
        blocks[lax.rem(mate + 2 * k, count) + 1] = chip[1]
    lane = lax.broadcasted_iota(jnp.int32, (4, 128), 1)
    row = lax.broadcasted_iota(jnp.int32, (4, 128), 0)
    interior = (lax.axis_index("gx") > 0) & (lax.axis_index("gy") * 4 + row > 0)
    for k in range(count):
        value = (
            blocks[k + 1, :4]
            + jnp.where(lane < 2, blocks[k, 4:], 0.0)
            + jnp.where(lane == 127, blocks[k + 2, 4:], 0.0)
        )
        here = interior & (lane > 0) if k == 0 else interior
        column[0, :, k * 128 : (k + 1) * 128] = jnp.where(here, value, 0.0)


def shape(*dims):
    return jax.ShapeDtypeStruct(dims, jnp.float32)


def in_vmem(count):
    return [pl.BlockSpec(memory_space=pltpu.VMEM)] * count


def call(kernel, name, inputs, outputs, flops, scratch=(), in_hbm=False):
    size = sum(4 * int(np.prod(v.shape)) for v in (*inputs, *outputs))
    space = pltpu.HBM if in_hbm else pltpu.VMEM
    return pl.pallas_call(
        kernel,
        out_shape=outputs,
        in_specs=[pl.BlockSpec(memory_space=space)] * len(inputs),
        out_specs=[pl.BlockSpec(memory_space=pltpu.VMEM)] * len(outputs),
        scratch_shapes=list(scratch),
        name=name,
        cost_estimate=pl.CostEstimate(flops=flops, bytes_accessed=size, transcendentals=0),
        compiler_params=pltpu.CompilerParams(vmem_limit_bytes=24 * 1024 * 1024),
    )(*inputs)


def shift(value, axis, distance):
    count = lax.axis_size(axis)
    return lax.ppermute(value, axis, [(i, (i + distance) % count) for i in range(count)])


def inside(axis, distance):
    place = lax.axis_index(axis) + distance
    return ((place >= 0) & (place < lax.axis_size(axis))).astype(jnp.float32)


def per_device(rhs, orders):
    cells = (PAIRS, MODES, MODES, 8, 128)
    first, x_up, x_down, y_up, y_down, z_up, z_down, y_low, y_high, z_low, z_high, held = call(
        trace_kernel,
        "face_traces",
        tuple(pltpu.with_memory_space_constraint(v, pltpu.HBM) for v in (rhs, orders)),
        (
            shape(*cells), shape(49, 8, 128), shape(49, 8, 128),
            shape(FACE_ROWS, 8, 128), shape(FACE_ROWS, 8, 128), shape(8, 128), shape(8, 128),
            shape(2, 28, 8, 128), shape(2, 28, 8, 128), shape(2, 28, 8, 128), shape(2, 28, 8, 128),
            jax.ShapeDtypeStruct(orders.shape, jnp.int32),
        ),
        4_000_000,
        scratch=(
            pltpu.VMEM(rhs.shape, jnp.float32),
            pltpu.SemaphoreType.DMA((MODES + 1,)),
        ),
        in_hbm=True,
    )
    x_from_low, x_from_high = shift(x_up, "gx", 1), shift(x_down, "gx", -1)
    y_from_low, y_from_high = shift(y_up, "gy", 1), shift(y_down, "gy", -1)
    z_from_low, z_from_high = shift(z_up, "gz", 1), shift(z_down, "gz", -1)
    (local,) = call(own_kernel, "own_cells", (first,), (shape(*cells),), 4_000_000_000)
    field, here, ahead, behind, far = call(
        finish_in_place,
        "smooth_and_restrict",
        (
            first, local, held, x_from_low, x_from_high, y_from_low, y_from_high,
            z_from_low, z_from_high, y_high, y_low, z_high, z_low,
        ),
        (shape(*cells),) + (shape(2, 8, 128),) * 4,
        5_000_000,
        scratch=(pltpu.VMEM(cells, jnp.float32),),
    )
    (smoothed,) = call(unpack_kernel, "unpack_modes", (field,), (shape(*rhs.shape),), 200_000)
    sums = (
        here
        + inside("gx", -1) * shift(ahead, "gx", 1)
        + inside("gx", 1) * shift(behind, "gx", -1)
        + inside("gx", -2) * shift(far, "gx", 2)
    )
    from_low, from_high = shift(sums, "gy", 1), shift(sums, "gy", -1)
    row = lax.broadcasted_iota(jnp.int32, (1, 4, 1), 1)
    owned = (
        sums[:, :4]
        + jnp.where(row < 2, from_low[:, 4:], 0.0) * inside("gy", -1)
        + jnp.where(row == 3, from_high[:, 4:], 0.0) * inside("gy", 1)
    ).reshape(8, 128)
    count = lax.axis_size("gz")
    other = lax.ppermute(owned, "gz", [(i, i ^ 1) for i in range(count)])
    chip = jnp.stack([owned, other])
    chips = [shift(chip, "gz", -2 * k) for k in range(1, count // 2)]
    (column,) = call(
        column_kernel,
        "column",
        (owned, other, *chips),
        (shape(1, 4, 128 * count),),
        20_000,
        scratch=(pltpu.VMEM((count + 2, 8, 128), jnp.float32),),
    )
    return smoothed, column


def finish_in_place(
    first, local, orders, x_low, x_high, y_low, y_high, z_low, z_high,
    y_below, y_above, z_below, z_above, field, here, ahead, behind, far, work,
):
    work[...] = local[...]
    finish_kernel(
        first, work, orders, x_low, x_high, y_low, y_high, z_low, z_high,
        y_below, y_above, z_below, z_above, field, here, ahead, behind, far,
    )


def solution(mesh):
    return jax.shard_map(
        per_device,
        mesh=mesh,
        in_specs=(P(None, None, None, "gx", "gy", "gz"), P("gx", "gy", "gz")),
        out_specs=(P(None, None, None, "gx", "gy", "gz"), P("gx", "gy", None)),
        check_vma=False,
    )
```

```python
import jax
import jax.numpy as jnp
import numpy as np
from jax import lax
from jax.experimental import pallas as pl
from jax.experimental.pallas import tpu as pltpu
from jax.sharding import PartitionSpec as P

PENALTY = 49.0
EIGEN_HIGH = 2.4
EIGEN_LOW = 0.24
THETA = 0.5 * (EIGEN_HIGH + EIGEN_LOW)
DELTA = 0.5 * (EIGEN_HIGH - EIGEN_LOW)
RHO_FIRST = DELTA / THETA
RHO_SECOND = 1.0 / (2.0 * THETA / DELTA - RHO_FIRST)
MODES = 7
PAIRS = 4
FACE_ROWS = 14


def basis_tables():
    degree = np.arange(MODES)
    normed = np.sqrt((2.0 * degree + 1.0) / 2.0)
    smaller = np.minimum(degree[:, None], degree[None, :])
    parity = (degree[:, None] + degree[None, :]) % 2 == 0
    stiffness = np.where(parity, normed[:, None] * normed[None, :] * smaller * (smaller + 1), 0.0)
    signs = (-1.0) ** degree
    slope = normed * degree * (degree + 1) / 2.0
    high, high_slope = normed, slope
    low, low_slope = normed * signs, -slope * signs
    own = (
        stiffness
        + PENALTY * (np.outer(high, high) + np.outer(low, low))
        - 0.5 * (np.outer(high, high_slope) + np.outer(high_slope, high))
        + 0.5 * (np.outer(low, low_slope) + np.outer(low_slope, low))
    )
    own = np.where(parity, own, 0.0)
    to_next = np.outer(low, 0.5 * high_slope - PENALTY * high) - 0.5 * np.outer(low_slope, high)
    to_last = np.outer(high, -PENALTY * low - 0.5 * low_slope) + 0.5 * np.outer(high_slope, low)
    one_axis = normed * normed * degree * (degree + 1) + 2.0 * (
        PENALTY * normed * normed - normed * slope
    )
    third = np.sqrt(1.5) / 3.0
    vertex = np.zeros((MODES, 2))
    vertex[0] = np.sqrt(0.5)
    vertex[1] = -third, third
    spread = np.stack(
        [
            vertex[:, 0] @ to_last,
            vertex[:, 1] @ to_last + vertex[:, 0] @ own,
            vertex[:, 1] @ own + vertex[:, 0] @ to_next,
            vertex[:, 1] @ to_next,
        ]
    )
    return normed, slope, own, one_axis, spread, third


NORMED, SLOPE, OWN, ONE_AXIS, SPREAD, THIRD = basis_tables()
ROOT_HALF = float(np.sqrt(0.5))


def diag(a, b, e):
    return float((ONE_AXIS[a] + ONE_AXIS[b] + ONE_AXIS[e]) / PENALTY)


def half_mask():
    return lax.broadcasted_iota(jnp.int32, (8, 128), 0) < 4


def row_in_half():
    return lax.broadcasted_iota(jnp.int32, (8, 128), 0) % 4


def lanes():
    return lax.broadcasted_iota(jnp.int32, (8, 128), 1)


def swap(value):
    return pltpu.roll(value, 4, 0)


class Pairs:
    def __init__(self):
        self.top = half_mask()
        self.known = {}

    def __call__(self, upper, lower):
        key = (float(upper), float(lower))
        if key[0] == key[1]:
            return jnp.float32(key[0])
        if key not in self.known:
            self.known[key] = jnp.where(self.top, jnp.float32(key[0]), jnp.float32(key[1]))
        return self.known[key]

    def once(self, upper, lower):
        if float(upper) == float(lower):
            return jnp.float32(upper)
        return jnp.where(self.top, jnp.float32(upper), jnp.float32(lower))


def total(terms):
    terms = list(terms)
    while len(terms) > 1:
        terms = [
            terms[k] + terms[k + 1] if k + 1 < len(terms) else terms[k]
            for k in range(0, len(terms), 2)
        ]
    return terms[0]


def keep_masks(orders, top):
    both = jnp.concatenate([orders, orders], axis=0)
    known = {}

    def get(upper, lower):
        if (upper, lower) not in known:
            if upper == lower:
                bound = jnp.int32(upper)
            else:
                bound = jnp.where(top, jnp.int32(upper), jnp.int32(lower))
            known[upper, lower] = (both >= bound).astype(jnp.float32)
        return known[upper, lower]

    return get


def odd_of(pair):
    return min(2 * pair + 1, MODES - 1)


def line_traces(line):
    even = total(float(NORMED[n]) * line[n] for n in range(0, MODES, 2))
    odd = total(float(NORMED[n]) * line[n] for n in range(1, MODES, 2))
    even_slope = total(float(SLOPE[n]) * line[n] for n in range(2, MODES, 2))
    odd_slope = total(float(SLOPE[n]) * line[n] for n in range(1, MODES, 2))
    return even + odd, even_slope + odd_slope, even - odd, odd_slope - even_slope


def trace_kernel(
    rhs_hbm, orders_hbm, first, x_a, x_b, y_a, y_b, z_a, z_b, y_low, y_high, z_low, z_high,
    orders, rhs, arrived,
):
    copies = [pltpu.make_async_copy(orders_hbm, orders, arrived.at[MODES])]
    for b in range(MODES):
        copies.append(pltpu.make_async_copy(rhs_hbm.at[:, b], rhs.at[:, b], arrived.at[b]))
    for copy in copies:
        copy.start()
    pairs = Pairs()
    top = pairs.top
    row, lane = row_in_half(), lanes()

    def put(ref, other_ref, index, axis, up, down):
        even = jnp.full((8, 128), lax.rem(lax.axis_index(axis), 2), jnp.int32) == 0
        ref[index] = jnp.where(even, up, down)
        other_ref[index] = jnp.where(even, down, up)

    copies[0].wait()
    keep = keep_masks(orders[0], top)
    for b in range(MODES):
        copies[1 + b].wait()
        for e in range(MODES):
            column = []
            for i in range(PAIRS):
                upper = rhs[2 * i, b, e, 0]
                lower = rhs[2 * i + 1, b, e, 0] if 2 * i + 1 < MODES else jnp.zeros_like(upper)
                cell = jnp.concatenate([upper, lower], axis=0)
                mask = keep(max(2 * i, b, e), max(odd_of(i), b, e))
                scale = pairs.once(
                    1.0 / (THETA * diag(2 * i, b, e)), 1.0 / (THETA * diag(odd_of(i), b, e))
                )
                cell = cell * mask * scale
                first[i, b, e] = cell
                column.append(cell)
            odd = [odd_of(i) if 2 * i + 1 < MODES else None for i in range(PAIRS)]
            value = total(
                pairs(NORMED[2 * i], NORMED[odd[i]] if odd[i] else 0.0) * column[i]
                for i in range(PAIRS)
            )
            slope = total(
                pairs(SLOPE[2 * i], SLOPE[odd[i]] if odd[i] else 0.0) * column[i]
                for i in range(PAIRS)
            )
            both_value = jnp.where(top, value + swap(value), swap(value) - value)
            both_slope = jnp.where(top, slope + swap(slope), slope - swap(slope))
            up = jnp.where(top, both_value, swap(both_slope))
            down = jnp.where(top, swap(both_value), both_slope)
            put(x_a, x_b, b * MODES + e, "gx", up, down)
    packed_up = packed_down = None
    for kind in range(2):
        for i in range(PAIRS):
            for e in range(MODES):
                m = i * MODES + e
                q = m % 4
                line = [first[i, b, e] for b in range(MODES)]
                traces = line_traces(line)
                high, low = traces[kind], traces[2 + kind]
                y_high[kind, m] = high
                y_low[kind, m] = low
                up, down = pltpu.roll(high, 5 + q, 0), pltpu.roll(low, q, 0) if q else low
                packed_up = up if q == 0 else jnp.where(row == q, up, packed_up)
                packed_down = down if q == 0 else jnp.where(row == q, down, packed_down)
                if q == 3:
                    put(y_a, y_b, kind * 7 + m // 4, "gy", packed_up, packed_down)
    packed_up = packed_down = jnp.zeros((8, 128), jnp.float32)
    for i in range(PAIRS):
        for b in range(MODES):
            m = i * MODES + b
            line = [first[i, b, e] for e in range(MODES)]
            traces = line_traces(line)
            for kind in range(2):
                high, low = traces[kind], traces[2 + kind]
                z_high[kind, m] = high
                z_low[kind, m] = low
                place = 2 * m + kind
                packed_up = jnp.where(lane == place, pltpu.roll(high, 1 + place, 1), packed_up)
                down = pltpu.roll(low, place, 1) if place else low
                packed_down = jnp.where(lane == place, down, packed_down)
    put(z_a, z_b, ..., "gz", packed_up, packed_down)


def own_kernel(first, out):
    pairs = Pairs()
    for b in range(MODES):
        for e in range(MODES):
            column = [first[i, b, e] for i in range(PAIRS)]
            for i in range(PAIRS):
                terms = []
                for j in range(PAIRS):
                    lower = OWN[2 * i + 1, 2 * j + 1] if max(i, j) < 3 else 0.0
                    terms.append(pairs(OWN[2 * i, 2 * j], lower) * column[j])
                out[i, b, e] = total(terms)
    for i in range(PAIRS):
        for b in range(MODES):
            line = [first[i, b, e] for e in range(MODES)]
            for n in range(MODES):
                out[i, b, n] += total(
                    float(OWN[n, k]) * line[k] for k in range(n % 2, MODES, 2)
                )
        for e in range(MODES):
            line = [first[i, b, e] for b in range(MODES)]
            for n in range(MODES):
                out[i, n, e] += total(
                    float(OWN[n, k]) * line[k] for k in range(n % 2, MODES, 2)
                )


def neighbour_line(low_value, low_slope, high_value, high_slope):
    plus, minus = high_value + low_value, high_value - low_value
    even = 0.5 * (low_slope - high_slope) - PENALTY * plus
    odd = -0.5 * (low_slope + high_slope) - PENALTY * minus
    return (even, 0.5 * plus), (odd, 0.5 * minus)


def vertex_pair(first_mode, second_mode):
    base, tilt = ROOT_HALF * first_mode, THIRD * second_mode
    return base - tilt, base + tilt


def sum_to_vertices(grid, pairs, row, lane):
    top = pairs.top
    rows = {}
    for (dy, dz), value in grid.items():
        rows.setdefault(dy, []).append((dz, value))
    result = [[[], []], [[], []]]
    for dy, entries in rows.items():
        inner, outer = [], []
        for dz, value in entries:
            if dz == 0:
                inner.append(value)
                continue
            moved = pltpu.roll(value, dz % 128, 1)
            inside = lane >= dz if dz > 0 else lane < 128 + dz
            inner.append(jnp.where(inside, moved, 0.0))
            outer.append(jnp.where(inside, 0.0, moved))
        for beyond, terms in ((0, inner), (1, outer)):
            if not terms:
                continue
            value = total(terms)
            if dy == 0:
                result[0][beyond].append(value)
                continue
            moved = pltpu.roll(value, dy % 8, 0)
            inside = row >= dy if dy > 0 else row < 4 + dy
            result[0][beyond].append(jnp.where(inside, moved, 0.0))
            result[1][beyond].append(jnp.where(inside, 0.0, swap(moved)))
    return [[total(result[r][z]) for z in range(2)] for r in range(2)]


def finish_kernel(
    first, local, orders, x_a, x_b, y_a, y_b, z_a, z_b,
    y_below, y_above, z_below, z_above, field, here, sum_a, sum_b, far,
):
    pairs = Pairs()
    top = pairs.top
    row, lane = row_in_half(), lanes()
    keep = keep_masks(orders[0], top)

    def inside(axis, distance):
        place = lax.axis_index(axis) + distance
        return jnp.where((place >= 0) & (place < lax.axis_size(axis)), 1.0, 0.0).astype(
            jnp.float32
        )

    def is_even(axis):
        return jnp.full((8, 128), lax.rem(lax.axis_index(axis), 2), jnp.int32) == 0

    x_has_b = inside("gx", -1) * inside("gx", 1)
    x_even, y_even, z_even = is_even("gx"), is_even("gy"), is_even("gz")
    x_sign = jnp.where(x_even, 1.0, -1.0)
    y_has_low, y_has_high = inside("gy", -1), inside("gy", 1)
    z_has_low, z_has_high = inside("gz", -1), inside("gz", 1)
    for b in range(MODES):
        for e in range(MODES):
            one, two = x_a[b * MODES + e], x_has_b * x_b[b * MODES + e]
            plus, minus = one + two, swap(x_sign * (one - two))
            slope = 0.5 * jnp.where(top, plus, minus)
            value = (-2.0 * PENALTY) * slope - 0.5 * jnp.where(top, minus, plus)
            for i in range(PAIRS):
                last = 2 * i + 1 >= MODES
                k = odd_of(i)
                local[i, b, e] += (
                    pairs(NORMED[2 * i], 0.0 if last else NORMED[k]) * value
                    + pairs(SLOPE[2 * i], 0.0 if last else SLOPE[k]) * slope
                )
    y_low, y_high = [], []
    for k in range(FACE_ROWS):
        one, two = y_a[k], y_b[k]
        y_low.append(y_has_low * jnp.where(y_even, two, one))
        y_high.append(y_has_high * jnp.where(y_even, one, two))
    for i in range(PAIRS):
        for e in range(MODES):
            m = i * MODES + e
            q = m % 4
            seen = []
            for kind in range(2):
                halo = y_low[kind * 7 + m // 4]
                halo = pltpu.roll(halo, 8 - q, 0) if q else halo
                moved = pltpu.roll(y_below[kind, m], 1, 0)
                seen.append(jnp.where(row == 0, halo, moved))
            for kind in range(2):
                halo = y_high[kind * 7 + m // 4]
                halo = pltpu.roll(halo, 3 - q, 0) if q < 3 else halo
                moved = pltpu.roll(y_above[kind, m], 7, 0)
                seen.append(jnp.where(row == 3, halo, moved))
            parts = neighbour_line(*seen)
            for n in range(MODES):
                value, slope = parts[n % 2]
                add = float(NORMED[n]) * value
                local[i, n, e] += add + float(SLOPE[n]) * slope if n else add
    z_low_halo = z_has_low * jnp.where(z_even, z_b[...], z_a[...])
    z_high_halo = z_has_high * jnp.where(z_even, z_a[...], z_b[...])
    for i in range(PAIRS):
        for b in range(MODES):
            m = i * MODES + b
            seen = []
            for kind in range(2):
                place = 2 * m + kind
                halo = pltpu.roll(z_low_halo, 128 - place, 1) if place else z_low_halo
                moved = pltpu.roll(z_below[kind, m], 1, 1)
                seen.append(jnp.where(lane == 0, halo, moved))
            for kind in range(2):
                place = 2 * m + kind
                halo = pltpu.roll(z_high_halo, 127 - place, 1)
                moved = pltpu.roll(z_above[kind, m], 127, 1)
                seen.append(jnp.where(lane == 127, halo, moved))
            parts = neighbour_line(*seen)
            for e in range(MODES):
                value, slope = parts[e % 2]
                add = float(NORMED[e]) * value
                if e:
                    add = add + float(SLOPE[e]) * slope
                applied = local[i, b, e] + add
                one = 2.0 * RHO_SECOND / (DELTA * PENALTY)
                scale = pairs.once(one / diag(2 * i, b, e), one / diag(odd_of(i), b, e))
                mask = keep(max(2 * i, b, e), max(odd_of(i), b, e))
                kappa = 1.0 + RHO_SECOND * RHO_FIRST + 2.0 * RHO_SECOND * THETA / DELTA
                after = kappa * first[i, b, e] - (mask * scale) * applied
                field[i, b, e] = after

    grid = {}

    def add(key, value):
        grid[key] = grid[key] + value if key in grid else value

    spread = -SPREAD / PENALTY
    for e in range(MODES):
        low, high = vertex_pair(field[0, 0, e], field[0, 1, e])
        for dz in range(-1, 3):
            add((0, dz), float(spread[dz + 1, e]) * low)
            add((1, dz), float(spread[dz + 1, e]) * high)
    for b in range(MODES):
        low, high = vertex_pair(field[0, b, 0], field[0, b, 1])
        for dy in range(-1, 3):
            add((dy, 0), float(spread[dy + 1, b]) * low)
            add((dy, 1), float(spread[dy + 1, b]) * high)
    force = [
        [
            pairs.once(THETA * diag(0, b, e), THETA * diag(1, b, e)) * first[0, b, e]
            for e in range(2)
        ]
        for b in range(2)
    ]
    force = [vertex_pair(force[0][e], force[1][e]) for e in range(2)]
    for dy in range(2):
        low, high = vertex_pair(force[0][dy], force[1][dy])
        add((dy, 0), low)
        add((dy, 1), high)
    kept, turned = pairs(ROOT_HALF, THIRD), pairs(-THIRD, ROOT_HALF)
    near = {key: kept * value + turned * swap(value) for key, value in grid.items()}
    outer = {}
    corners = []
    for i in range(PAIRS):
        line = [vertex_pair(field[i, 0, e], field[i, 1, e]) for e in range(2)]
        corners.append([vertex_pair(line[0][dy], line[1][dy]) for dy in range(2)])
    for dy in range(2):
        for dz in range(2):
            sums = []
            for dx in range(-1, 3):
                part = total(
                    pairs(
                        spread[dx + 1, 2 * i],
                        spread[dx + 1, 2 * i + 1] if 2 * i + 1 < MODES else 0.0,
                    )
                    * corners[i][dy][dz]
                    for i in range(PAIRS)
                )
                sums.append(part + swap(part))
            near[dy, dz] += jnp.where(top, sums[1], sums[2])
            outer[dy, dz] = jnp.where(top, sums[0], sums[3])
    near = sum_to_vertices(near, pairs, row, lane)
    outer = sum_to_vertices(outer, pairs, row, lane)
    for z in range(2):
        here[z] = jnp.where(top, near[0][z], swap(near[1][z]))
        ahead = jnp.where(top, swap(near[0][z]), near[1][z])
        behind = jnp.where(top, outer[0][z], swap(outer[1][z]))
        sum_a[z] = jnp.where(x_even, ahead, behind)
        sum_b[z] = jnp.where(x_even, behind, ahead)
        far[z] = jnp.where(top, swap(outer[0][z]), outer[1][z])


def unpack_kernel(field, smoothed):
    for b in range(MODES):
        for e in range(MODES):
            for i in range(PAIRS):
                value = field[i, b, e]
                smoothed[2 * i, b, e, 0] = value[:4]
                if 2 * i + 1 < MODES:
                    smoothed[2 * i + 1, b, e, 0] = value[4:]


def column_kernel(own, other, next_chip, over_chip, last_chip, column, blocks):
    count = lax.axis_size("gz")
    me = lax.axis_index("gz")
    mate = me + 1 - 2 * lax.rem(me, 2)
    zero = jnp.zeros((8, 128), jnp.float32)
    blocks[0] = zero
    blocks[count + 1] = zero
    blocks[me + 1] = own[...]
    blocks[mate + 1] = other[...]
    core = lax.rem(me, 2)
    place = lax.div(me, 2)
    beside = place + 1 - 2 * lax.rem(place, 2)
    across = lax.rem(place + 2, 4)
    for source, chip in ((beside, next_chip), (across, over_chip), (3 - place, last_chip)):
        blocks[2 * source + core + 1] = chip[0]
        blocks[2 * source + 2 - core] = chip[1]
    lane = lax.broadcasted_iota(jnp.int32, (4, 128), 1)
    row = lax.broadcasted_iota(jnp.int32, (4, 128), 0)
    interior = (lax.axis_index("gx") > 0) & (lax.axis_index("gy") * 4 + row > 0)
    for k in range(count):
        value = (
            blocks[k + 1, :4]
            + jnp.where(lane < 2, blocks[k, 4:], 0.0)
            + jnp.where(lane == 127, blocks[k + 2, 4:], 0.0)
        )
        here = interior & (lane > 0) if k == 0 else interior
        column[0, :, k * 128 : (k + 1) * 128] = jnp.where(here, value, 0.0)


def shape(*dims):
    return jax.ShapeDtypeStruct(dims, jnp.float32)


def in_vmem(count):
    return [pl.BlockSpec(memory_space=pltpu.VMEM)] * count


def call(kernel, name, inputs, outputs, flops, scratch=(), in_hbm=False):
    size = sum(4 * int(np.prod(v.shape)) for v in (*inputs, *outputs))
    space = pltpu.HBM if in_hbm else pltpu.VMEM
    return pl.pallas_call(
        kernel,
        out_shape=outputs,
        in_specs=[pl.BlockSpec(memory_space=space)] * len(inputs),
        out_specs=[pl.BlockSpec(memory_space=pltpu.VMEM)] * len(outputs),
        scratch_shapes=list(scratch),
        name=name,
        cost_estimate=pl.CostEstimate(flops=flops, bytes_accessed=size, transcendentals=0),
        compiler_params=pltpu.CompilerParams(vmem_limit_bytes=24 * 1024 * 1024),
    )(*inputs)


def shift(value, axis, distance):
    count = lax.axis_size(axis)
    return lax.ppermute(value, axis, [(i, (i + distance) % count) for i in range(count)])


def flip(value, axis, bits):
    return lax.ppermute(value, axis, [(i, i ^ bits) for i in range(lax.axis_size(axis))])


def second_pairs(value, axis):
    axes = ("gx", "gy", "gz")
    sizes = [lax.axis_size(name) for name in axes]
    route = []
    for source, place in enumerate(np.ndindex(*sizes)):
        target = list(place)
        k = axes.index(axis)
        if place[k] in (0, sizes[k] - 1):
            target[2] ^= 1
        else:
            target[k] += 1 if place[k] % 2 else -1
        route.append((source, int(np.ravel_multi_index(target, sizes))))
    return lax.ppermute(value, axes, route)


def second_ring(value, axis):
    count = lax.axis_size(axis)
    return lax.ppermute(
        value, axis, [(i, (i + (1 if i % 2 else -1)) % count) for i in range(count)]
    )


def inside(axis, distance):
    place = lax.axis_index(axis) + distance
    return ((place >= 0) & (place < lax.axis_size(axis))).astype(jnp.float32)


def per_device(rhs, orders):
    cells = (PAIRS, MODES, MODES, 8, 128)
    first, x_a, x_b, y_a, y_b, z_a, z_b, y_low, y_high, z_low, z_high, held = call(
        trace_kernel,
        "face_traces",
        tuple(pltpu.with_memory_space_constraint(v, pltpu.HBM) for v in (rhs, orders)),
        (
            shape(*cells), shape(49, 8, 128), shape(49, 8, 128),
            shape(FACE_ROWS, 8, 128), shape(FACE_ROWS, 8, 128), shape(8, 128), shape(8, 128),
            shape(2, 28, 8, 128), shape(2, 28, 8, 128), shape(2, 28, 8, 128), shape(2, 28, 8, 128),
            jax.ShapeDtypeStruct(orders.shape, jnp.int32),
        ),
        4_000_000,
        scratch=(
            pltpu.VMEM(rhs.shape, jnp.float32),
            pltpu.SemaphoreType.DMA((MODES + 1,)),
        ),
        in_hbm=True,
    )
    x_a, x_b = flip(x_a, "gx", 1), second_pairs(x_b, "gx")
    y_a, y_b = flip(y_a, "gy", 1), second_pairs(y_b, "gy")
    z_a, z_b = flip(z_a, "gz", 1), second_ring(z_b, "gz")
    (local,) = call(own_kernel, "own_cells", (first,), (shape(*cells),), 4_000_000_000)
    field, here, sum_a, sum_b, far = call(
        finish_in_place,
        "smooth_and_restrict",
        (
            first, local, held, x_a, x_b, y_a, y_b, z_a, z_b, y_high, y_low, z_high, z_low,
        ),
        (shape(*cells),) + (shape(2, 8, 128),) * 4,
        5_000_000,
        scratch=(pltpu.VMEM(cells, jnp.float32),),
    )
    (smoothed,) = call(unpack_kernel, "unpack_modes", (field,), (shape(*rhs.shape),), 200_000)
    sums = (
        here
        + flip(sum_a, "gx", 1)
        + inside("gx", -1) * inside("gx", 1) * second_pairs(sum_b, "gx")
        + inside("gx", -2) * flip(far, "gx", 2)
    )
    from_low, from_high = shift(sums, "gy", 1), shift(sums, "gy", -1)
    row = lax.broadcasted_iota(jnp.int32, (1, 4, 1), 1)
    owned = (
        sums[:, :4]
        + jnp.where(row < 2, from_low[:, 4:], 0.0) * inside("gy", -1)
        + jnp.where(row == 3, from_high[:, 4:], 0.0) * inside("gy", 1)
    ).reshape(8, 128)
    count = lax.axis_size("gz")
    other = flip(owned, "gz", 1)
    chip = jnp.stack([owned, other])
    chips = [flip(chip, "gz", 2 * k) for k in range(1, count // 2)]
    (column,) = call(
        column_kernel,
        "column",
        (owned, other, *chips),
        (shape(1, 4, 128 * count),),
        20_000,
        scratch=(pltpu.VMEM((count + 2, 8, 128), jnp.float32),),
    )
    return smoothed, column


def finish_in_place(
    first, local, orders, x_a, x_b, y_a, y_b, z_a, z_b,
    y_below, y_above, z_below, z_above, field, here, sum_a, sum_b, far, work,
):
    work[...] = local[...]
    finish_kernel(
        first, work, orders, x_a, x_b, y_a, y_b, z_a, z_b,
        y_below, y_above, z_below, z_above, field, here, sum_a, sum_b, far,
    )


def solution(mesh):
    return jax.shard_map(
        per_device,
        mesh=mesh,
        in_specs=(P(None, None, None, "gx", "gy", "gz"), P("gx", "gy", "gz")),
        out_specs=(P(None, None, None, "gx", "gy", "gz"), P("gx", "gy", None)),
        check_vma=False,
    )
```

```python
import jax
import jax.numpy as jnp
import numpy as np
from jax import lax
from jax.experimental import pallas as pl
from jax.experimental.pallas import tpu as pltpu
from jax.sharding import PartitionSpec as P

PENALTY = 49.0
EIGEN_HIGH = 2.4
EIGEN_LOW = 0.24
THETA = 0.5 * (EIGEN_HIGH + EIGEN_LOW)
DELTA = 0.5 * (EIGEN_HIGH - EIGEN_LOW)
RHO_FIRST = DELTA / THETA
RHO_SECOND = 1.0 / (2.0 * THETA / DELTA - RHO_FIRST)
MODES = 7
PAIRS = 4
FACE_ROWS = 14


def basis_tables():
    degree = np.arange(MODES)
    normed = np.sqrt((2.0 * degree + 1.0) / 2.0)
    smaller = np.minimum(degree[:, None], degree[None, :])
    parity = (degree[:, None] + degree[None, :]) % 2 == 0
    stiffness = np.where(parity, normed[:, None] * normed[None, :] * smaller * (smaller + 1), 0.0)
    signs = (-1.0) ** degree
    slope = normed * degree * (degree + 1) / 2.0
    high, high_slope = normed, slope
    low, low_slope = normed * signs, -slope * signs
    own = (
        stiffness
        + PENALTY * (np.outer(high, high) + np.outer(low, low))
        - 0.5 * (np.outer(high, high_slope) + np.outer(high_slope, high))
        + 0.5 * (np.outer(low, low_slope) + np.outer(low_slope, low))
    )
    own = np.where(parity, own, 0.0)
    to_next = np.outer(low, 0.5 * high_slope - PENALTY * high) - 0.5 * np.outer(low_slope, high)
    to_last = np.outer(high, -PENALTY * low - 0.5 * low_slope) + 0.5 * np.outer(high_slope, low)
    one_axis = normed * normed * degree * (degree + 1) + 2.0 * (
        PENALTY * normed * normed - normed * slope
    )
    third = np.sqrt(1.5) / 3.0
    vertex = np.zeros((MODES, 2))
    vertex[0] = np.sqrt(0.5)
    vertex[1] = -third, third
    spread = np.stack(
        [
            vertex[:, 0] @ to_last,
            vertex[:, 1] @ to_last + vertex[:, 0] @ own,
            vertex[:, 1] @ own + vertex[:, 0] @ to_next,
            vertex[:, 1] @ to_next,
        ]
    )
    return normed, slope, own, one_axis, spread, third


NORMED, SLOPE, OWN, ONE_AXIS, SPREAD, THIRD = basis_tables()
ROOT_HALF = float(np.sqrt(0.5))


def diag(a, b, e):
    return float((ONE_AXIS[a] + ONE_AXIS[b] + ONE_AXIS[e]) / PENALTY)


def half_mask():
    return lax.broadcasted_iota(jnp.int32, (8, 128), 0) < 4


def row_in_half():
    return lax.broadcasted_iota(jnp.int32, (8, 128), 0) % 4


def lanes():
    return lax.broadcasted_iota(jnp.int32, (8, 128), 1)


def swap(value):
    return pltpu.roll(value, 4, 0)


class Pairs:
    def __init__(self):
        self.top = half_mask()
        self.known = {}

    def __call__(self, upper, lower):
        key = (float(upper), float(lower))
        if key[0] == key[1]:
            return jnp.float32(key[0])
        if key not in self.known:
            self.known[key] = jnp.where(self.top, jnp.float32(key[0]), jnp.float32(key[1]))
        return self.known[key]

    def once(self, upper, lower):
        if float(upper) == float(lower):
            return jnp.float32(upper)
        return jnp.where(self.top, jnp.float32(upper), jnp.float32(lower))


def total(terms):
    terms = list(terms)
    while len(terms) > 1:
        terms = [
            terms[k] + terms[k + 1] if k + 1 < len(terms) else terms[k]
            for k in range(0, len(terms), 2)
        ]
    return terms[0]


def keep_masks(orders, top):
    both = jnp.concatenate([orders, orders], axis=0)
    known = {}

    def get(upper, lower):
        if (upper, lower) not in known:
            if upper == lower:
                bound = jnp.int32(upper)
            else:
                bound = jnp.where(top, jnp.int32(upper), jnp.int32(lower))
            known[upper, lower] = (both >= bound).astype(jnp.float32)
        return known[upper, lower]

    return get


def odd_of(pair):
    return min(2 * pair + 1, MODES - 1)


def line_traces(line):
    even = total(float(NORMED[n]) * line[n] for n in range(0, MODES, 2))
    odd = total(float(NORMED[n]) * line[n] for n in range(1, MODES, 2))
    even_slope = total(float(SLOPE[n]) * line[n] for n in range(2, MODES, 2))
    odd_slope = total(float(SLOPE[n]) * line[n] for n in range(1, MODES, 2))
    return even + odd, even_slope + odd_slope, even - odd, odd_slope - even_slope


def trace_kernel(
    rhs_hbm, orders_hbm, first, x_a, x_b, y_a, y_b, z_a, z_b, y_low, y_high, z_low, z_high,
    orders, rhs, arrived,
):
    copies = [pltpu.make_async_copy(orders_hbm, orders, arrived.at[MODES])]
    for b in range(MODES):
        copies.append(pltpu.make_async_copy(rhs_hbm.at[:, b], rhs.at[:, b], arrived.at[b]))
    for copy in copies:
        copy.start()
    pairs = Pairs()
    top = pairs.top
    row, lane = row_in_half(), lanes()

    def put(ref, other_ref, index, axis, up, down):
        even = jnp.full((8, 128), lax.rem(lax.axis_index(axis), 2), jnp.int32) == 0
        ref[index] = jnp.where(even, up, down)
        other_ref[index] = jnp.where(even, down, up)

    copies[0].wait()
    keep = keep_masks(orders[0], top)
    for b in range(MODES):
        copies[1 + b].wait()
        for e in range(MODES):
            column = []
            for i in range(PAIRS):
                upper = rhs[2 * i, b, e, 0]
                lower = rhs[2 * i + 1, b, e, 0] if 2 * i + 1 < MODES else jnp.zeros_like(upper)
                cell = jnp.concatenate([upper, lower], axis=0)
                mask = keep(max(2 * i, b, e), max(odd_of(i), b, e))
                scale = pairs.once(
                    1.0 / (THETA * diag(2 * i, b, e)), 1.0 / (THETA * diag(odd_of(i), b, e))
                )
                cell = cell * mask * scale
                first[i, b, e] = cell
                column.append(cell)
            odd = [odd_of(i) if 2 * i + 1 < MODES else None for i in range(PAIRS)]
            value = total(
                pairs(NORMED[2 * i], NORMED[odd[i]] if odd[i] else 0.0) * column[i]
                for i in range(PAIRS)
            )
            slope = total(
                pairs(SLOPE[2 * i], SLOPE[odd[i]] if odd[i] else 0.0) * column[i]
                for i in range(PAIRS)
            )
            both_value = jnp.where(top, value + swap(value), swap(value) - value)
            both_slope = jnp.where(top, slope + swap(slope), slope - swap(slope))
            up = jnp.where(top, both_value, swap(both_slope))
            down = jnp.where(top, swap(both_value), both_slope)
            put(x_a, x_b, b * MODES + e, "gx", up, down)
    packed_up = packed_down = None
    for kind in range(2):
        for i in range(PAIRS):
            for e in range(MODES):
                m = i * MODES + e
                q = m % 4
                line = [first[i, b, e] for b in range(MODES)]
                traces = line_traces(line)
                high, low = traces[kind], traces[2 + kind]
                y_high[kind, m] = high
                y_low[kind, m] = low
                up, down = pltpu.roll(high, 5 + q, 0), pltpu.roll(low, q, 0) if q else low
                packed_up = up if q == 0 else jnp.where(row == q, up, packed_up)
                packed_down = down if q == 0 else jnp.where(row == q, down, packed_down)
                if q == 3:
                    put(y_a, y_b, kind * 7 + m // 4, "gy", packed_up, packed_down)
    packed_up = packed_down = jnp.zeros((8, 128), jnp.float32)
    for i in range(PAIRS):
        for b in range(MODES):
            m = i * MODES + b
            line = [first[i, b, e] for e in range(MODES)]
            traces = line_traces(line)
            for kind in range(2):
                high, low = traces[kind], traces[2 + kind]
                z_high[kind, m] = high
                z_low[kind, m] = low
                place = 2 * m + kind
                packed_up = jnp.where(lane == place, pltpu.roll(high, 1 + place, 1), packed_up)
                down = pltpu.roll(low, place, 1) if place else low
                packed_down = jnp.where(lane == place, down, packed_down)
    put(z_a, z_b, ..., "gz", packed_up, packed_down)


def own_kernel(first, out):
    pairs = Pairs()
    for b in range(MODES):
        for e in range(MODES):
            column = [first[i, b, e] for i in range(PAIRS)]
            for i in range(PAIRS):
                terms = []
                for j in range(PAIRS):
                    lower = OWN[2 * i + 1, 2 * j + 1] if max(i, j) < 3 else 0.0
                    terms.append(pairs(OWN[2 * i, 2 * j], lower) * column[j])
                out[i, b, e] = total(terms)
    for i in range(PAIRS):
        for b in range(MODES):
            line = [first[i, b, e] for e in range(MODES)]
            for n in range(MODES):
                out[i, b, n] += total(
                    float(OWN[n, k]) * line[k] for k in range(n % 2, MODES, 2)
                )
        for e in range(MODES):
            line = [first[i, b, e] for b in range(MODES)]
            for n in range(MODES):
                out[i, n, e] += total(
                    float(OWN[n, k]) * line[k] for k in range(n % 2, MODES, 2)
                )


def neighbour_line(low_value, low_slope, high_value, high_slope):
    plus, minus = high_value + low_value, high_value - low_value
    even = 0.5 * (low_slope - high_slope) - PENALTY * plus
    odd = -0.5 * (low_slope + high_slope) - PENALTY * minus
    return (even, 0.5 * plus), (odd, 0.5 * minus)


def vertex_pair(first_mode, second_mode):
    base, tilt = ROOT_HALF * first_mode, THIRD * second_mode
    return base - tilt, base + tilt


def sum_to_vertices(grid, pairs, row, lane):
    top = pairs.top
    rows = {}
    for (dy, dz), value in grid.items():
        rows.setdefault(dy, []).append((dz, value))
    result = [[[], []], [[], []]]
    for dy, entries in rows.items():
        inner, outer = [], []
        for dz, value in entries:
            if dz == 0:
                inner.append(value)
                continue
            moved = pltpu.roll(value, dz % 128, 1)
            inside = lane >= dz if dz > 0 else lane < 128 + dz
            inner.append(jnp.where(inside, moved, 0.0))
            outer.append(jnp.where(inside, 0.0, moved))
        for beyond, terms in ((0, inner), (1, outer)):
            if not terms:
                continue
            value = total(terms)
            if dy == 0:
                result[0][beyond].append(value)
                continue
            moved = pltpu.roll(value, dy % 8, 0)
            inside = row >= dy if dy > 0 else row < 4 + dy
            result[0][beyond].append(jnp.where(inside, moved, 0.0))
            result[1][beyond].append(jnp.where(inside, 0.0, swap(moved)))
    return [[total(result[r][z]) for z in range(2)] for r in range(2)]


def finish_kernel(
    first, local, orders, x_a, x_b, y_a, y_b, z_a, z_b,
    y_below, y_above, z_below, z_above, field, here, sum_a, sum_b, far,
):
    pairs = Pairs()
    top = pairs.top
    row, lane = row_in_half(), lanes()
    keep = keep_masks(orders[0], top)

    def inside(axis, distance):
        place = lax.axis_index(axis) + distance
        return jnp.where((place >= 0) & (place < lax.axis_size(axis)), 1.0, 0.0).astype(
            jnp.float32
        )

    def is_even(axis):
        return jnp.full((8, 128), lax.rem(lax.axis_index(axis), 2), jnp.int32) == 0

    x_has_b = inside("gx", -1) * inside("gx", 1)
    x_even, y_even, z_even = is_even("gx"), is_even("gy"), is_even("gz")
    x_sign = jnp.where(x_even, 1.0, -1.0)
    y_has_low, y_has_high = inside("gy", -1), inside("gy", 1)
    z_has_low, z_has_high = inside("gz", -1), inside("gz", 1)
    for b in range(MODES):
        for e in range(MODES):
            one, two = x_a[b * MODES + e], x_has_b * x_b[b * MODES + e]
            plus, minus = one + two, swap(x_sign * (one - two))
            slope = 0.5 * jnp.where(top, plus, minus)
            value = (-2.0 * PENALTY) * slope - 0.5 * jnp.where(top, minus, plus)
            for i in range(PAIRS):
                last = 2 * i + 1 >= MODES
                k = odd_of(i)
                local[i, b, e] += (
                    pairs(NORMED[2 * i], 0.0 if last else NORMED[k]) * value
                    + pairs(SLOPE[2 * i], 0.0 if last else SLOPE[k]) * slope
                )
    y_low, y_high = [], []
    for k in range(FACE_ROWS):
        one, two = y_a[k], y_b[k]
        y_low.append(y_has_low * jnp.where(y_even, two, one))
        y_high.append(y_has_high * jnp.where(y_even, one, two))
    for i in range(PAIRS):
        for e in range(MODES):
            m = i * MODES + e
            q = m % 4
            seen = []
            for kind in range(2):
                halo = y_low[kind * 7 + m // 4]
                halo = pltpu.roll(halo, 8 - q, 0) if q else halo
                moved = pltpu.roll(y_below[kind, m], 1, 0)
                seen.append(jnp.where(row == 0, halo, moved))
            for kind in range(2):
                halo = y_high[kind * 7 + m // 4]
                halo = pltpu.roll(halo, 3 - q, 0) if q < 3 else halo
                moved = pltpu.roll(y_above[kind, m], 7, 0)
                seen.append(jnp.where(row == 3, halo, moved))
            parts = neighbour_line(*seen)
            for n in range(MODES):
                value, slope = parts[n % 2]
                add = float(NORMED[n]) * value
                local[i, n, e] += add + float(SLOPE[n]) * slope if n else add
    z_low_halo = z_has_low * jnp.where(z_even, z_b[...], z_a[...])
    z_high_halo = z_has_high * jnp.where(z_even, z_a[...], z_b[...])
    for i in range(PAIRS):
        for b in range(MODES):
            m = i * MODES + b
            seen = []
            for kind in range(2):
                place = 2 * m + kind
                halo = pltpu.roll(z_low_halo, 128 - place, 1) if place else z_low_halo
                moved = pltpu.roll(z_below[kind, m], 1, 1)
                seen.append(jnp.where(lane == 0, halo, moved))
            for kind in range(2):
                place = 2 * m + kind
                halo = pltpu.roll(z_high_halo, 127 - place, 1)
                moved = pltpu.roll(z_above[kind, m], 127, 1)
                seen.append(jnp.where(lane == 127, halo, moved))
            parts = neighbour_line(*seen)
            for e in range(MODES):
                value, slope = parts[e % 2]
                add = float(NORMED[e]) * value
                if e:
                    add = add + float(SLOPE[e]) * slope
                applied = local[i, b, e] + add
                one = 2.0 * RHO_SECOND / (DELTA * PENALTY)
                scale = pairs.once(one / diag(2 * i, b, e), one / diag(odd_of(i), b, e))
                mask = keep(max(2 * i, b, e), max(odd_of(i), b, e))
                kappa = 1.0 + RHO_SECOND * RHO_FIRST + 2.0 * RHO_SECOND * THETA / DELTA
                after = kappa * first[i, b, e] - (mask * scale) * applied
                field[i, b, e] = after

    grid = {}

    def add(key, value):
        grid[key] = grid[key] + value if key in grid else value

    spread = -SPREAD / PENALTY
    for e in range(MODES):
        low, high = vertex_pair(field[0, 0, e], field[0, 1, e])
        for dz in range(-1, 3):
            add((0, dz), float(spread[dz + 1, e]) * low)
            add((1, dz), float(spread[dz + 1, e]) * high)
    for b in range(MODES):
        low, high = vertex_pair(field[0, b, 0], field[0, b, 1])
        for dy in range(-1, 3):
            add((dy, 0), float(spread[dy + 1, b]) * low)
            add((dy, 1), float(spread[dy + 1, b]) * high)
    force = [
        [
            pairs.once(THETA * diag(0, b, e), THETA * diag(1, b, e)) * first[0, b, e]
            for e in range(2)
        ]
        for b in range(2)
    ]
    force = [vertex_pair(force[0][e], force[1][e]) for e in range(2)]
    for dy in range(2):
        low, high = vertex_pair(force[0][dy], force[1][dy])
        add((dy, 0), low)
        add((dy, 1), high)
    kept, turned = pairs(ROOT_HALF, THIRD), pairs(-THIRD, ROOT_HALF)
    near = {key: kept * value + turned * swap(value) for key, value in grid.items()}
    outer = {}
    corners = []
    for i in range(PAIRS):
        line = [vertex_pair(field[i, 0, e], field[i, 1, e]) for e in range(2)]
        corners.append([vertex_pair(line[0][dy], line[1][dy]) for dy in range(2)])
    for dy in range(2):
        for dz in range(2):
            sums = []
            for dx in range(-1, 3):
                part = total(
                    pairs(
                        spread[dx + 1, 2 * i],
                        spread[dx + 1, 2 * i + 1] if 2 * i + 1 < MODES else 0.0,
                    )
                    * corners[i][dy][dz]
                    for i in range(PAIRS)
                )
                sums.append(part + swap(part))
            near[dy, dz] += jnp.where(top, sums[1], sums[2])
            outer[dy, dz] = jnp.where(top, sums[0], sums[3])
    near = sum_to_vertices(near, pairs, row, lane)
    outer = sum_to_vertices(outer, pairs, row, lane)
    for z in range(2):
        here[z] = jnp.where(top, near[0][z], swap(near[1][z]))
        ahead = jnp.where(top, swap(near[0][z]), near[1][z])
        behind = jnp.where(top, outer[0][z], swap(outer[1][z]))
        sum_a[z] = jnp.where(x_even, ahead, behind)
        sum_b[z] = jnp.where(x_even, behind, ahead)
        far[z] = jnp.where(top, swap(outer[0][z]), outer[1][z])


def unpack_kernel(field, smoothed):
    for b in range(MODES):
        for e in range(MODES):
            for i in range(PAIRS):
                value = field[i, b, e]
                smoothed[2 * i, b, e, 0] = value[:4]
                if 2 * i + 1 < MODES:
                    smoothed[2 * i + 1, b, e, 0] = value[4:]


def column_kernel(own, other, over_chip, next_chip, last_chip, column, blocks):
    count = lax.axis_size("gz")
    me = lax.axis_index("gz")
    mate = me + 1 - 2 * lax.rem(me, 2)
    zero = jnp.zeros((8, 128), jnp.float32)
    blocks[0] = zero
    blocks[count + 1] = zero
    blocks[me + 1] = own[...]
    blocks[mate + 1] = other[...]
    core = lax.rem(me, 2)
    place = lax.div(me, 2)
    beside = place + 1 - 2 * lax.rem(place, 2)
    across = lax.rem(place + 2, 4)
    for source, chip in ((beside, next_chip), (across, over_chip), (3 - place, last_chip)):
        blocks[2 * source + core + 1] = chip[0]
        blocks[2 * source + 2 - core] = chip[1]
    lane = lax.broadcasted_iota(jnp.int32, (4, 128), 1)
    row = lax.broadcasted_iota(jnp.int32, (4, 128), 0)
    interior = (lax.axis_index("gx") > 0) & (lax.axis_index("gy") * 4 + row > 0)
    for k in range(count):
        value = (
            blocks[k + 1, :4]
            + jnp.where(lane < 2, blocks[k, 4:], 0.0)
            + jnp.where(lane == 127, blocks[k + 2, 4:], 0.0)
        )
        here = interior & (lane > 0) if k == 0 else interior
        column[0, :, k * 128 : (k + 1) * 128] = jnp.where(here, value, 0.0)


def shape(*dims):
    return jax.ShapeDtypeStruct(dims, jnp.float32)


def in_vmem(count):
    return [pl.BlockSpec(memory_space=pltpu.VMEM)] * count


def call(kernel, name, inputs, outputs, flops, scratch=(), in_hbm=False):
    size = sum(4 * int(np.prod(v.shape)) for v in (*inputs, *outputs))
    space = pltpu.HBM if in_hbm else pltpu.VMEM
    return pl.pallas_call(
        kernel,
        out_shape=outputs,
        in_specs=[pl.BlockSpec(memory_space=space)] * len(inputs),
        out_specs=[pl.BlockSpec(memory_space=pltpu.VMEM)] * len(outputs),
        scratch_shapes=list(scratch),
        name=name,
        cost_estimate=pl.CostEstimate(flops=flops, bytes_accessed=size, transcendentals=0),
        compiler_params=pltpu.CompilerParams(vmem_limit_bytes=24 * 1024 * 1024),
    )(*inputs)


def flip(value, axis, bits):
    return lax.ppermute(value, axis, [(i, i ^ bits) for i in range(lax.axis_size(axis))])


def second_pairs(value, axis):
    axes = ("gx", "gy", "gz")
    sizes = [lax.axis_size(name) for name in axes]
    route = []
    for source, place in enumerate(np.ndindex(*sizes)):
        target = list(place)
        k = axes.index(axis)
        if place[k] in (0, sizes[k] - 1):
            target[0 if axis == "gz" else 2] ^= 1
        else:
            target[k] += 1 if place[k] % 2 else -1
        route.append((source, int(np.ravel_multi_index(target, sizes))))
    return lax.ppermute(value, axes, route)


def inside(axis, distance):
    place = lax.axis_index(axis) + distance
    return ((place >= 0) & (place < lax.axis_size(axis))).astype(jnp.float32)


def per_device(rhs, orders):
    cells = (PAIRS, MODES, MODES, 8, 128)
    first, x_a, x_b, y_a, y_b, z_a, z_b, y_low, y_high, z_low, z_high, held = call(
        trace_kernel,
        "face_traces",
        tuple(pltpu.with_memory_space_constraint(v, pltpu.HBM) for v in (rhs, orders)),
        (
            shape(*cells), shape(49, 8, 128), shape(49, 8, 128),
            shape(FACE_ROWS, 8, 128), shape(FACE_ROWS, 8, 128), shape(8, 128), shape(8, 128),
            shape(2, 28, 8, 128), shape(2, 28, 8, 128), shape(2, 28, 8, 128), shape(2, 28, 8, 128),
            jax.ShapeDtypeStruct(orders.shape, jnp.int32),
        ),
        4_000_000,
        scratch=(
            pltpu.VMEM(rhs.shape, jnp.float32),
            pltpu.SemaphoreType.DMA((MODES + 1,)),
        ),
        in_hbm=True,
    )
    x_a, x_b = flip(x_a, "gx", 1), second_pairs(x_b, "gx")
    y_a, y_b = flip(y_a, "gy", 1), second_pairs(y_b, "gy")
    z_a, z_b = flip(z_a, "gz", 1), second_pairs(z_b, "gz")
    (local,) = call(own_kernel, "own_cells", (first,), (shape(*cells),), 4_000_000_000)
    field, here, sum_a, sum_b, far = call(
        finish_in_place,
        "smooth_and_restrict",
        (
            first, local, held, x_a, x_b, y_a, y_b, z_a, z_b, y_high, y_low, z_high, z_low,
        ),
        (shape(*cells),) + (shape(2, 8, 128),) * 4,
        5_000_000,
        scratch=(pltpu.VMEM(cells, jnp.float32),),
    )
    (smoothed,) = call(unpack_kernel, "unpack_modes", (field,), (shape(*rhs.shape),), 200_000)
    from_far = flip(far, "gx", 2)
    from_a = flip(sum_a, "gx", 1)
    from_b = second_pairs(sum_b, "gx")
    sums = (
        here
        + inside("gx", -2) * from_far
        + from_a
        + inside("gx", -1) * inside("gx", 1) * from_b
    )
    even = lax.axis_index("gy") % 2 == 0
    from_a, from_b = flip(sums, "gy", 1), second_pairs(sums, "gy")
    from_low, from_high = jnp.where(even, from_b, from_a), jnp.where(even, from_a, from_b)
    row = lax.broadcasted_iota(jnp.int32, (1, 4, 1), 1)
    owned = (
        sums[:, :4]
        + jnp.where(row < 2, from_low[:, 4:], 0.0) * inside("gy", -1)
        + jnp.where(row == 3, from_high[:, 4:], 0.0) * inside("gy", 1)
    ).reshape(8, 128)
    count = lax.axis_size("gz")
    other = flip(owned, "gz", 1)
    chip = jnp.stack([owned, other])
    across, beside, opposite = (flip(chip, "gz", bits) for bits in (4, 2, 6))
    (column,) = call(
        column_kernel,
        "column",
        (owned, other, across, beside, opposite),
        (shape(1, 4, 128 * count),),
        20_000,
        scratch=(pltpu.VMEM((count + 2, 8, 128), jnp.float32),),
    )
    return smoothed, column


def finish_in_place(
    first, local, orders, x_a, x_b, y_a, y_b, z_a, z_b,
    y_below, y_above, z_below, z_above, field, here, sum_a, sum_b, far, work,
):
    work[...] = local[...]
    finish_kernel(
        first, work, orders, x_a, x_b, y_a, y_b, z_a, z_b,
        y_below, y_above, z_below, z_above, field, here, sum_a, sum_b, far,
    )


def solution(mesh):
    return jax.shard_map(
        per_device,
        mesh=mesh,
        in_specs=(P(None, None, None, "gx", "gy", "gz"), P("gx", "gy", "gz")),
        out_specs=(P(None, None, None, "gx", "gy", "gz"), P("gx", "gy", None)),
        check_vma=False,
    )
```

```python
import jax
import jax.numpy as jnp
import numpy as np
from jax import lax
from jax.experimental import pallas as pl
from jax.experimental.pallas import tpu as pltpu
from jax.sharding import PartitionSpec as P

PENALTY = 49.0
EIGEN_HIGH = 2.4
EIGEN_LOW = 0.24
THETA = 0.5 * (EIGEN_HIGH + EIGEN_LOW)
DELTA = 0.5 * (EIGEN_HIGH - EIGEN_LOW)
RHO_FIRST = DELTA / THETA
RHO_SECOND = 1.0 / (2.0 * THETA / DELTA - RHO_FIRST)
MODES = 7
PAIRS = 4
FACE_ROWS = 14


def basis_tables():
    degree = np.arange(MODES)
    normed = np.sqrt((2.0 * degree + 1.0) / 2.0)
    smaller = np.minimum(degree[:, None], degree[None, :])
    parity = (degree[:, None] + degree[None, :]) % 2 == 0
    stiffness = np.where(parity, normed[:, None] * normed[None, :] * smaller * (smaller + 1), 0.0)
    signs = (-1.0) ** degree
    slope = normed * degree * (degree + 1) / 2.0
    high, high_slope = normed, slope
    low, low_slope = normed * signs, -slope * signs
    own = (
        stiffness
        + PENALTY * (np.outer(high, high) + np.outer(low, low))
        - 0.5 * (np.outer(high, high_slope) + np.outer(high_slope, high))
        + 0.5 * (np.outer(low, low_slope) + np.outer(low_slope, low))
    )
    own = np.where(parity, own, 0.0)
    to_next = np.outer(low, 0.5 * high_slope - PENALTY * high) - 0.5 * np.outer(low_slope, high)
    to_last = np.outer(high, -PENALTY * low - 0.5 * low_slope) + 0.5 * np.outer(high_slope, low)
    one_axis = normed * normed * degree * (degree + 1) + 2.0 * (
        PENALTY * normed * normed - normed * slope
    )
    third = np.sqrt(1.5) / 3.0
    vertex = np.zeros((MODES, 2))
    vertex[0] = np.sqrt(0.5)
    vertex[1] = -third, third
    spread = np.stack(
        [
            vertex[:, 0] @ to_last,
            vertex[:, 1] @ to_last + vertex[:, 0] @ own,
            vertex[:, 1] @ own + vertex[:, 0] @ to_next,
            vertex[:, 1] @ to_next,
        ]
    )
    return normed, slope, own, one_axis, spread, third


NORMED, SLOPE, OWN, ONE_AXIS, SPREAD, THIRD = basis_tables()
ROOT_HALF = float(np.sqrt(0.5))


def diag(a, b, e):
    return float((ONE_AXIS[a] + ONE_AXIS[b] + ONE_AXIS[e]) / PENALTY)


def half_mask():
    return lax.broadcasted_iota(jnp.int32, (8, 128), 0) < 4


def row_in_half():
    return lax.broadcasted_iota(jnp.int32, (8, 128), 0) % 4


def lanes():
    return lax.broadcasted_iota(jnp.int32, (8, 128), 1)


def swap(value):
    return pltpu.roll(value, 4, 0)


class Pairs:
    def __init__(self):
        self.top = half_mask()
        self.known = {}

    def __call__(self, upper, lower):
        key = (float(upper), float(lower))
        if key[0] == key[1]:
            return jnp.float32(key[0])
        if key not in self.known:
            self.known[key] = jnp.where(self.top, jnp.float32(key[0]), jnp.float32(key[1]))
        return self.known[key]

    def once(self, upper, lower):
        if float(upper) == float(lower):
            return jnp.float32(upper)
        return jnp.where(self.top, jnp.float32(upper), jnp.float32(lower))


def total(terms):
    terms = list(terms)
    while len(terms) > 1:
        terms = [
            terms[k] + terms[k + 1] if k + 1 < len(terms) else terms[k]
            for k in range(0, len(terms), 2)
        ]
    return terms[0]


def keep_masks(orders, top):
    both = jnp.concatenate([orders, orders], axis=0)
    known = {}

    def get(upper, lower):
        if (upper, lower) not in known:
            if upper == lower:
                bound = jnp.int32(upper)
            else:
                bound = jnp.where(top, jnp.int32(upper), jnp.int32(lower))
            known[upper, lower] = (both >= bound).astype(jnp.float32)
        return known[upper, lower]

    return get


def odd_of(pair):
    return min(2 * pair + 1, MODES - 1)


def line_traces(line):
    even = total(float(NORMED[n]) * line[n] for n in range(0, MODES, 2))
    odd = total(float(NORMED[n]) * line[n] for n in range(1, MODES, 2))
    even_slope = total(float(SLOPE[n]) * line[n] for n in range(2, MODES, 2))
    odd_slope = total(float(SLOPE[n]) * line[n] for n in range(1, MODES, 2))
    return even + odd, even_slope + odd_slope, even - odd, odd_slope - even_slope


def trace_kernel(
    rhs_hbm, orders_hbm, first, x_a, x_b, y_a, y_b, z_a, z_b, y_low, y_high, z_low, z_high,
    orders, rhs, arrived,
):
    copies = [pltpu.make_async_copy(orders_hbm, orders, arrived.at[MODES])]
    for b in range(MODES):
        copies.append(pltpu.make_async_copy(rhs_hbm.at[:, b], rhs.at[:, b], arrived.at[b]))
    for copy in copies:
        copy.start()
    pairs = Pairs()
    top = pairs.top
    row, lane = row_in_half(), lanes()

    def put(ref, other_ref, index, axis, up, down):
        even = jnp.full((8, 128), lax.rem(lax.axis_index(axis), 2), jnp.int32) == 0
        ref[index] = jnp.where(even, up, down)
        other_ref[index] = jnp.where(even, down, up)

    copies[0].wait()
    keep = keep_masks(orders[0], top)
    for b in range(MODES):
        copies[1 + b].wait()
        for e in range(MODES):
            column = []
            for i in range(PAIRS):
                upper = rhs[2 * i, b, e, 0]
                lower = rhs[2 * i + 1, b, e, 0] if 2 * i + 1 < MODES else jnp.zeros_like(upper)
                cell = jnp.concatenate([upper, lower], axis=0)
                mask = keep(max(2 * i, b, e), max(odd_of(i), b, e))
                scale = pairs.once(
                    1.0 / (THETA * diag(2 * i, b, e)), 1.0 / (THETA * diag(odd_of(i), b, e))
                )
                cell = cell * mask * scale
                first[i, b, e] = cell
                column.append(cell)
            odd = [odd_of(i) if 2 * i + 1 < MODES else None for i in range(PAIRS)]
            value = total(
                pairs(NORMED[2 * i], NORMED[odd[i]] if odd[i] else 0.0) * column[i]
                for i in range(PAIRS)
            )
            slope = total(
                pairs(SLOPE[2 * i], SLOPE[odd[i]] if odd[i] else 0.0) * column[i]
                for i in range(PAIRS)
            )
            both_value = jnp.where(top, value + swap(value), swap(value) - value)
            both_slope = jnp.where(top, slope + swap(slope), slope - swap(slope))
            up = jnp.where(top, both_value, swap(both_slope))
            down = jnp.where(top, swap(both_value), both_slope)
            put(x_a, x_b, b * MODES + e, "gx", up, down)
    packed_up = packed_down = None
    for kind in range(2):
        for i in range(PAIRS):
            for e in range(MODES):
                m = i * MODES + e
                q = m % 4
                line = [first[i, b, e] for b in range(MODES)]
                traces = line_traces(line)
                high, low = traces[kind], traces[2 + kind]
                y_high[kind, m] = high
                y_low[kind, m] = low
                up, down = pltpu.roll(high, 5 + q, 0), pltpu.roll(low, q, 0) if q else low
                packed_up = up if q == 0 else jnp.where(row == q, up, packed_up)
                packed_down = down if q == 0 else jnp.where(row == q, down, packed_down)
                if q == 3:
                    put(y_a, y_b, kind * 7 + m // 4, "gy", packed_up, packed_down)
    packed_up = packed_down = jnp.zeros((8, 128), jnp.float32)
    for i in range(PAIRS):
        for b in range(MODES):
            m = i * MODES + b
            line = [first[i, b, e] for e in range(MODES)]
            traces = line_traces(line)
            for kind in range(2):
                high, low = traces[kind], traces[2 + kind]
                z_high[kind, m] = high
                z_low[kind, m] = low
                place = 2 * m + kind
                packed_up = jnp.where(lane == place, pltpu.roll(high, 1 + place, 1), packed_up)
                down = pltpu.roll(low, place, 1) if place else low
                packed_down = jnp.where(lane == place, down, packed_down)
    put(z_a, z_b, ..., "gz", packed_up, packed_down)


def own_kernel(first, out):
    pairs = Pairs()
    for b in range(MODES):
        for e in range(MODES):
            column = [first[i, b, e] for i in range(PAIRS)]
            for i in range(PAIRS):
                terms = []
                for j in range(PAIRS):
                    lower = OWN[2 * i + 1, 2 * j + 1] if max(i, j) < 3 else 0.0
                    terms.append(pairs(OWN[2 * i, 2 * j], lower) * column[j])
                out[i, b, e] = total(terms)
    for i in range(PAIRS):
        for b in range(MODES):
            line = [first[i, b, e] for e in range(MODES)]
            for n in range(MODES):
                out[i, b, n] += total(
                    float(OWN[n, k]) * line[k] for k in range(n % 2, MODES, 2)
                )
        for e in range(MODES):
            line = [first[i, b, e] for b in range(MODES)]
            for n in range(MODES):
                out[i, n, e] += total(
                    float(OWN[n, k]) * line[k] for k in range(n % 2, MODES, 2)
                )


def neighbour_line(low_value, low_slope, high_value, high_slope):
    plus, minus = high_value + low_value, high_value - low_value
    even = 0.5 * (low_slope - high_slope) - PENALTY * plus
    odd = -0.5 * (low_slope + high_slope) - PENALTY * minus
    return (even, 0.5 * plus), (odd, 0.5 * minus)


def vertex_pair(first_mode, second_mode):
    base, tilt = ROOT_HALF * first_mode, THIRD * second_mode
    return base - tilt, base + tilt


def sum_to_vertices(grid, pairs, row, lane):
    top = pairs.top
    rows = {}
    for (dy, dz), value in grid.items():
        rows.setdefault(dy, []).append((dz, value))
    result = [[[], []], [[], []]]
    for dy, entries in rows.items():
        inner, outer = [], []
        for dz, value in entries:
            if dz == 0:
                inner.append(value)
                continue
            moved = pltpu.roll(value, dz % 128, 1)
            inside = lane >= dz if dz > 0 else lane < 128 + dz
            inner.append(jnp.where(inside, moved, 0.0))
            outer.append(jnp.where(inside, 0.0, moved))
        for beyond, terms in ((0, inner), (1, outer)):
            if not terms:
                continue
            value = total(terms)
            if dy == 0:
                result[0][beyond].append(value)
                continue
            moved = pltpu.roll(value, dy % 8, 0)
            inside = row >= dy if dy > 0 else row < 4 + dy
            result[0][beyond].append(jnp.where(inside, moved, 0.0))
            result[1][beyond].append(jnp.where(inside, 0.0, swap(moved)))
    return [[total(result[r][z]) for z in range(2)] for r in range(2)]


def finish_kernel(
    first, local, orders, x_a, x_b, y_a, y_b, z_a, z_b,
    y_below, y_above, z_below, z_above, field, here, sum_a, sum_b, far,
):
    pairs = Pairs()
    top = pairs.top
    row, lane = row_in_half(), lanes()
    keep = keep_masks(orders[0], top)

    def inside(axis, distance):
        place = lax.axis_index(axis) + distance
        return jnp.where((place >= 0) & (place < lax.axis_size(axis)), 1.0, 0.0).astype(
            jnp.float32
        )

    def is_even(axis):
        return jnp.full((8, 128), lax.rem(lax.axis_index(axis), 2), jnp.int32) == 0

    x_has_b = inside("gx", -1) * inside("gx", 1)
    x_even, y_even, z_even = is_even("gx"), is_even("gy"), is_even("gz")
    x_sign = jnp.where(x_even, 1.0, -1.0)
    y_has_low, y_has_high = inside("gy", -1), inside("gy", 1)
    z_has_low, z_has_high = inside("gz", -1), inside("gz", 1)
    for b in range(MODES):
        for e in range(MODES):
            one, two = x_a[b * MODES + e], x_has_b * x_b[b * MODES + e]
            plus, minus = one + two, swap(x_sign * (one - two))
            slope = 0.5 * jnp.where(top, plus, minus)
            value = (-2.0 * PENALTY) * slope - 0.5 * jnp.where(top, minus, plus)
            for i in range(PAIRS):
                last = 2 * i + 1 >= MODES
                k = odd_of(i)
                local[i, b, e] += (
                    pairs(NORMED[2 * i], 0.0 if last else NORMED[k]) * value
                    + pairs(SLOPE[2 * i], 0.0 if last else SLOPE[k]) * slope
                )
    y_low, y_high = [], []
    for k in range(FACE_ROWS):
        one, two = y_a[k], y_b[k]
        y_low.append(y_has_low * jnp.where(y_even, two, one))
        y_high.append(y_has_high * jnp.where(y_even, one, two))
    for i in range(PAIRS):
        for e in range(MODES):
            m = i * MODES + e
            q = m % 4
            seen = []
            for kind in range(2):
                halo = y_low[kind * 7 + m // 4]
                halo = pltpu.roll(halo, 8 - q, 0) if q else halo
                moved = pltpu.roll(y_below[kind, m], 1, 0)
                seen.append(jnp.where(row == 0, halo, moved))
            for kind in range(2):
                halo = y_high[kind * 7 + m // 4]
                halo = pltpu.roll(halo, 3 - q, 0) if q < 3 else halo
                moved = pltpu.roll(y_above[kind, m], 7, 0)
                seen.append(jnp.where(row == 3, halo, moved))
            parts = neighbour_line(*seen)
            for n in range(MODES):
                value, slope = parts[n % 2]
                add = float(NORMED[n]) * value
                local[i, n, e] += add + float(SLOPE[n]) * slope if n else add
    z_low_halo = z_has_low * jnp.where(z_even, z_b[...], z_a[...])
    z_high_halo = z_has_high * jnp.where(z_even, z_a[...], z_b[...])
    for i in range(PAIRS):
        for b in range(MODES):
            m = i * MODES + b
            seen = []
            for kind in range(2):
                place = 2 * m + kind
                halo = pltpu.roll(z_low_halo, 128 - place, 1) if place else z_low_halo
                moved = pltpu.roll(z_below[kind, m], 1, 1)
                seen.append(jnp.where(lane == 0, halo, moved))
            for kind in range(2):
                place = 2 * m + kind
                halo = pltpu.roll(z_high_halo, 127 - place, 1)
                moved = pltpu.roll(z_above[kind, m], 127, 1)
                seen.append(jnp.where(lane == 127, halo, moved))
            parts = neighbour_line(*seen)
            for e in range(MODES):
                value, slope = parts[e % 2]
                add = float(NORMED[e]) * value
                if e:
                    add = add + float(SLOPE[e]) * slope
                applied = local[i, b, e] + add
                one = 2.0 * RHO_SECOND / (DELTA * PENALTY)
                scale = pairs.once(one / diag(2 * i, b, e), one / diag(odd_of(i), b, e))
                mask = keep(max(2 * i, b, e), max(odd_of(i), b, e))
                kappa = 1.0 + RHO_SECOND * RHO_FIRST + 2.0 * RHO_SECOND * THETA / DELTA
                after = kappa * first[i, b, e] - (mask * scale) * applied
                field[i, b, e] = after

    grid = {}

    def add(key, value):
        grid[key] = grid[key] + value if key in grid else value

    spread = -SPREAD / PENALTY
    for e in range(MODES):
        low, high = vertex_pair(field[0, 0, e], field[0, 1, e])
        for dz in range(-1, 3):
            add((0, dz), float(spread[dz + 1, e]) * low)
            add((1, dz), float(spread[dz + 1, e]) * high)
    for b in range(MODES):
        low, high = vertex_pair(field[0, b, 0], field[0, b, 1])
        for dy in range(-1, 3):
            add((dy, 0), float(spread[dy + 1, b]) * low)
            add((dy, 1), float(spread[dy + 1, b]) * high)
    force = [
        [
            pairs.once(THETA * diag(0, b, e), THETA * diag(1, b, e)) * first[0, b, e]
            for e in range(2)
        ]
        for b in range(2)
    ]
    force = [vertex_pair(force[0][e], force[1][e]) for e in range(2)]
    for dy in range(2):
        low, high = vertex_pair(force[0][dy], force[1][dy])
        add((dy, 0), low)
        add((dy, 1), high)
    kept, turned = pairs(ROOT_HALF, THIRD), pairs(-THIRD, ROOT_HALF)
    near = {key: kept * value + turned * swap(value) for key, value in grid.items()}
    outer = {}
    corners = []
    for i in range(PAIRS):
        line = [vertex_pair(field[i, 0, e], field[i, 1, e]) for e in range(2)]
        corners.append([vertex_pair(line[0][dy], line[1][dy]) for dy in range(2)])
    for dy in range(2):
        for dz in range(2):
            sums = []
            for dx in range(-1, 3):
                part = total(
                    pairs(
                        spread[dx + 1, 2 * i],
                        spread[dx + 1, 2 * i + 1] if 2 * i + 1 < MODES else 0.0,
                    )
                    * corners[i][dy][dz]
                    for i in range(PAIRS)
                )
                sums.append(part + swap(part))
            near[dy, dz] += jnp.where(top, sums[1], sums[2])
            outer[dy, dz] = jnp.where(top, sums[0], sums[3])
    near = sum_to_vertices(near, pairs, row, lane)
    outer = sum_to_vertices(outer, pairs, row, lane)
    for z in range(2):
        here[z] = jnp.where(top, near[0][z], swap(near[1][z]))
        ahead = jnp.where(top, swap(near[0][z]), near[1][z])
        behind = jnp.where(top, outer[0][z], swap(outer[1][z]))
        sum_a[z] = jnp.where(x_even, ahead, behind)
        sum_b[z] = jnp.where(x_even, behind, ahead)
        far[z] = jnp.where(top, swap(outer[0][z]), outer[1][z])


def unpack_kernel(field, smoothed):
    for b in range(MODES):
        for e in range(MODES):
            for i in range(PAIRS):
                value = field[i, b, e]
                smoothed[2 * i, b, e, 0] = value[:4]
                if 2 * i + 1 < MODES:
                    smoothed[2 * i + 1, b, e, 0] = value[4:]


def column_kernel(chip, fetched, mated, third, column, blocks):
    count = lax.axis_size("gz")
    me = lax.axis_index("gz")
    core, place = lax.rem(me, 2), lax.div(me, 2)
    beside = place + 1 - 2 * lax.rem(place, 2)
    across = lax.rem(place + 2, 4)
    asked = beside + core * (across - beside)
    zero = jnp.zeros((8, 128), jnp.float32)
    blocks[0] = zero
    blocks[count + 1] = zero
    for source, sender, pair in (
        (place, core, chip),
        (asked, core, fetched),
        (beside + across - asked, 1 - core, mated),
        (3 - place, core, third),
    ):
        blocks[2 * source + sender + 1] = pair[0]
        blocks[2 * source + 2 - sender] = pair[1]
    lane = lax.broadcasted_iota(jnp.int32, (4, 128), 1)
    row = lax.broadcasted_iota(jnp.int32, (4, 128), 0)
    interior = (lax.axis_index("gx") > 0) & (lax.axis_index("gy") * 4 + row > 0)
    for k in range(count):
        value = (
            blocks[k + 1, :4]
            + jnp.where(lane < 2, blocks[k, 4:], 0.0)
            + jnp.where(lane == 127, blocks[k + 2, 4:], 0.0)
        )
        here = interior & (lane > 0) if k == 0 else interior
        column[0, :, k * 128 : (k + 1) * 128] = jnp.where(here, value, 0.0)


def shape(*dims):
    return jax.ShapeDtypeStruct(dims, jnp.float32)


def in_vmem(count):
    return [pl.BlockSpec(memory_space=pltpu.VMEM)] * count


def call(kernel, name, inputs, outputs, flops, scratch=(), in_hbm=False):
    size = sum(4 * int(np.prod(v.shape)) for v in (*inputs, *outputs))
    space = pltpu.HBM if in_hbm else pltpu.VMEM
    return pl.pallas_call(
        kernel,
        out_shape=outputs,
        in_specs=[pl.BlockSpec(memory_space=space)] * len(inputs),
        out_specs=[pl.BlockSpec(memory_space=pltpu.VMEM)] * len(outputs),
        scratch_shapes=list(scratch),
        name=name,
        cost_estimate=pl.CostEstimate(flops=flops, bytes_accessed=size, transcendentals=0),
        compiler_params=pltpu.CompilerParams(vmem_limit_bytes=24 * 1024 * 1024),
    )(*inputs)


def flip(value, axis, bits):
    return lax.ppermute(value, axis, [(i, i ^ bits) for i in range(lax.axis_size(axis))])


def exchange(value, partner):
    axes = ("gx", "gy", "gz")
    sizes = [lax.axis_size(name) for name in axes]
    route = [
        (source, int(np.ravel_multi_index(partner(list(place)), sizes)))
        for source, place in enumerate(np.ndindex(*sizes))
    ]
    return lax.ppermute(value, axes, route)


def second_of_pair(place, k, count, spare, bit):
    if place[k] in (0, count - 1):
        place[spare] ^= bit
    else:
        place[k] += 1 if place[k] % 2 else -1
    return place


def second_pairs(value, axis):
    k, count = ("gx", "gy", "gz").index(axis), lax.axis_size(axis)
    return exchange(value, lambda place: second_of_pair(place, k, count, 0 if k == 2 else 2, 1))


def both_y_sides(value):
    count = lax.axis_size("gy")

    def partner(place):
        if place[2] % 2:
            place[1] ^= 1
            return place
        return second_of_pair(place, 1, count, 0, 1)

    return exchange(value, partner)


def two_chips(value):
    def partner(place):
        place[2] ^= 4 if place[2] % 2 else 2
        return place

    return exchange(value, partner)


def inside(axis, distance):
    place = lax.axis_index(axis) + distance
    return ((place >= 0) & (place < lax.axis_size(axis))).astype(jnp.float32)


def per_device(rhs, orders):
    cells = (PAIRS, MODES, MODES, 8, 128)
    first, x_a, x_b, y_a, y_b, z_a, z_b, y_low, y_high, z_low, z_high, held = call(
        trace_kernel,
        "face_traces",
        tuple(pltpu.with_memory_space_constraint(v, pltpu.HBM) for v in (rhs, orders)),
        (
            shape(*cells), shape(49, 8, 128), shape(49, 8, 128),
            shape(FACE_ROWS, 8, 128), shape(FACE_ROWS, 8, 128), shape(8, 128), shape(8, 128),
            shape(2, 28, 8, 128), shape(2, 28, 8, 128), shape(2, 28, 8, 128), shape(2, 28, 8, 128),
            jax.ShapeDtypeStruct(orders.shape, jnp.int32),
        ),
        4_000_000,
        scratch=(
            pltpu.VMEM(rhs.shape, jnp.float32),
            pltpu.SemaphoreType.DMA((MODES + 1,)),
        ),
        in_hbm=True,
    )
    x_a, x_b = flip(x_a, "gx", 1), second_pairs(x_b, "gx")
    y_a, y_b = flip(y_a, "gy", 1), second_pairs(y_b, "gy")
    z_a, z_b = flip(z_a, "gz", 1), second_pairs(z_b, "gz")
    (local,) = call(own_kernel, "own_cells", (first,), (shape(*cells),), 4_000_000_000)
    field, here, sum_a, sum_b, far = call(
        finish_in_place,
        "smooth_and_restrict",
        (
            first, local, held, x_a, x_b, y_a, y_b, z_a, z_b, y_high, y_low, z_high, z_low,
        ),
        (shape(*cells),) + (shape(2, 8, 128),) * 4,
        5_000_000,
        scratch=(pltpu.VMEM(cells, jnp.float32),),
    )
    (smoothed,) = call(unpack_kernel, "unpack_modes", (field,), (shape(*rhs.shape),), 200_000)
    from_far = flip(far, "gx", 2)
    from_a = flip(sum_a, "gx", 1)
    from_b = second_pairs(sum_b, "gx")
    sums = (
        here
        + inside("gx", -2) * from_far
        + from_a
        + inside("gx", -1) * inside("gx", 1) * from_b
    )
    count = lax.axis_size("gz")
    chip = jnp.stack([sums, flip(sums, "gz", 1)])
    from_beside = both_y_sides(chip)
    from_low = (lax.axis_index("gy") + lax.axis_index("gz")) % 2 == 0
    row = lax.broadcasted_iota(jnp.int32, (1, 1, 4, 1), 2)
    wanted = jnp.where(from_low, row < 2, row == 3)
    valid = jnp.where(from_low, inside("gy", -1), inside("gy", 1))
    edges = jnp.where(wanted, from_beside[:, :, 4:], 0.0) * valid
    edges = edges.reshape(2, 8, 128)
    mated = flip(edges, "gz", 1)
    owned = chip[:, :, :4].reshape(2, 8, 128) + edges + mated[::-1]
    fetched = two_chips(owned)
    third = flip(owned, "gz", 6)
    (column,) = call(
        column_kernel,
        "column",
        (owned, fetched, flip(fetched, "gz", 1), third),
        (shape(1, 4, 128 * count),),
        20_000,
        scratch=(pltpu.VMEM((count + 2, 8, 128), jnp.float32),),
    )
    return smoothed, column


def finish_in_place(
    first, local, orders, x_a, x_b, y_a, y_b, z_a, z_b,
    y_below, y_above, z_below, z_above, field, here, sum_a, sum_b, far, work,
):
    work[...] = local[...]
    finish_kernel(
        first, work, orders, x_a, x_b, y_a, y_b, z_a, z_b,
        y_below, y_above, z_below, z_above, field, here, sum_a, sum_b, far,
    )


def solution(mesh):
    return jax.shard_map(
        per_device,
        mesh=mesh,
        in_specs=(P(None, None, None, "gx", "gy", "gz"), P("gx", "gy", "gz")),
        out_specs=(P(None, None, None, "gx", "gy", "gz"), P("gx", "gy", None)),
        check_vma=False,
    )
```

```python
import jax
import jax.numpy as jnp
import numpy as np
from jax import lax
from jax.experimental import pallas as pl
from jax.experimental.pallas import tpu as pltpu
from jax.sharding import PartitionSpec as P

PENALTY = 49.0
EIGEN_HIGH = 2.4
EIGEN_LOW = 0.24
THETA = 0.5 * (EIGEN_HIGH + EIGEN_LOW)
DELTA = 0.5 * (EIGEN_HIGH - EIGEN_LOW)
RHO_FIRST = DELTA / THETA
RHO_SECOND = 1.0 / (2.0 * THETA / DELTA - RHO_FIRST)
MODES = 7
PAIRS = 4
FACE_ROWS = 14
SIDE_COST = 4_000_000
OWN_COST = 1_400_000_000
HALO_COST = 4_000_000


def basis_tables():
    degree = np.arange(MODES)
    normed = np.sqrt((2.0 * degree + 1.0) / 2.0)
    smaller = np.minimum(degree[:, None], degree[None, :])
    parity = (degree[:, None] + degree[None, :]) % 2 == 0
    stiffness = np.where(parity, normed[:, None] * normed[None, :] * smaller * (smaller + 1), 0.0)
    signs = (-1.0) ** degree
    slope = normed * degree * (degree + 1) / 2.0
    high, high_slope = normed, slope
    low, low_slope = normed * signs, -slope * signs
    own = (
        stiffness
        + PENALTY * (np.outer(high, high) + np.outer(low, low))
        - 0.5 * (np.outer(high, high_slope) + np.outer(high_slope, high))
        + 0.5 * (np.outer(low, low_slope) + np.outer(low_slope, low))
    )
    own = np.where(parity, own, 0.0)
    to_next = np.outer(low, 0.5 * high_slope - PENALTY * high) - 0.5 * np.outer(low_slope, high)
    to_last = np.outer(high, -PENALTY * low - 0.5 * low_slope) + 0.5 * np.outer(high_slope, low)
    one_axis = normed * normed * degree * (degree + 1) + 2.0 * (
        PENALTY * normed * normed - normed * slope
    )
    third = np.sqrt(1.5) / 3.0
    vertex = np.zeros((MODES, 2))
    vertex[0] = np.sqrt(0.5)
    vertex[1] = -third, third
    spread = np.stack(
        [
            vertex[:, 0] @ to_last,
            vertex[:, 1] @ to_last + vertex[:, 0] @ own,
            vertex[:, 1] @ own + vertex[:, 0] @ to_next,
            vertex[:, 1] @ to_next,
        ]
    )
    return normed, slope, own, one_axis, spread, third


NORMED, SLOPE, OWN, ONE_AXIS, SPREAD, THIRD = basis_tables()
ROOT_HALF = float(np.sqrt(0.5))


def diag(a, b, e):
    return float((ONE_AXIS[a] + ONE_AXIS[b] + ONE_AXIS[e]) / PENALTY)


def half_mask():
    return lax.broadcasted_iota(jnp.int32, (8, 128), 0) < 4


def row_in_half():
    return lax.broadcasted_iota(jnp.int32, (8, 128), 0) % 4


def lanes():
    return lax.broadcasted_iota(jnp.int32, (8, 128), 1)


def swap(value):
    return pltpu.roll(value, 4, 0)


class Pairs:
    def __init__(self):
        self.top = half_mask()
        self.known = {}

    def __call__(self, upper, lower):
        key = (float(upper), float(lower))
        if key[0] == key[1]:
            return jnp.float32(key[0])
        if key not in self.known:
            self.known[key] = jnp.where(self.top, jnp.float32(key[0]), jnp.float32(key[1]))
        return self.known[key]

    def once(self, upper, lower):
        if float(upper) == float(lower):
            return jnp.float32(upper)
        return jnp.where(self.top, jnp.float32(upper), jnp.float32(lower))


def total(terms):
    terms = list(terms)
    while len(terms) > 1:
        terms = [
            terms[k] + terms[k + 1] if k + 1 < len(terms) else terms[k]
            for k in range(0, len(terms), 2)
        ]
    return terms[0]


def keep_masks(orders, top):
    both = jnp.concatenate([orders, orders], axis=0)
    known = {}

    def get(upper, lower):
        if (upper, lower) not in known:
            if upper == lower:
                bound = jnp.int32(upper)
            else:
                bound = jnp.where(top, jnp.int32(upper), jnp.int32(lower))
            known[upper, lower] = (both >= bound).astype(jnp.float32)
        return known[upper, lower]

    return get


def odd_of(pair):
    return min(2 * pair + 1, MODES - 1)


def line_traces(line):
    even = total(float(NORMED[n]) * line[n] for n in range(0, MODES, 2))
    odd = total(float(NORMED[n]) * line[n] for n in range(1, MODES, 2))
    even_slope = total(float(SLOPE[n]) * line[n] for n in range(2, MODES, 2))
    odd_slope = total(float(SLOPE[n]) * line[n] for n in range(1, MODES, 2))
    return even + odd, even_slope + odd_slope, even - odd, odd_slope - even_slope


def x_turn():
    return lax.axis_index("gx") + lax.axis_index("gz")


def goes_up(turn):
    return jnp.full((8, 128), lax.rem(turn, 2), jnp.int32) == 0


def has_place(axis, distance):
    place = lax.axis_index(axis) + distance
    return jnp.where((place >= 0) & (place < lax.axis_size(axis)), 1.0, 0.0).astype(jnp.float32)


def trace_kernel(
    rhs_hbm, orders_hbm, first, x_a, x_b, orders, rhs, arrived,
):
    copies = [pltpu.make_async_copy(orders_hbm, orders, arrived.at[MODES])]
    for b in range(MODES):
        copies.append(pltpu.make_async_copy(rhs_hbm.at[:, b], rhs.at[:, b], arrived.at[b]))
    for copy in copies:
        copy.start()
    pairs = Pairs()
    top = pairs.top
    upward = goes_up(x_turn())
    copies[0].wait()
    keep = keep_masks(orders[0], top)
    for b in range(MODES):
        copies[1 + b].wait()
        for e in range(MODES):
            column = []
            for i in range(PAIRS):
                upper = rhs[2 * i, b, e, 0]
                lower = rhs[2 * i + 1, b, e, 0] if 2 * i + 1 < MODES else jnp.zeros_like(upper)
                cell = jnp.concatenate([upper, lower], axis=0)
                mask = keep(max(2 * i, b, e), max(odd_of(i), b, e))
                scale = pairs.once(
                    1.0 / (THETA * diag(2 * i, b, e)), 1.0 / (THETA * diag(odd_of(i), b, e))
                )
                cell = cell * mask * scale
                first[i, b, e] = cell
                column.append(cell)
            odd = [odd_of(i) if 2 * i + 1 < MODES else None for i in range(PAIRS)]
            value = total(
                pairs(NORMED[2 * i], NORMED[odd[i]] if odd[i] else 0.0) * column[i]
                for i in range(PAIRS)
            )
            slope = total(
                pairs(SLOPE[2 * i], SLOPE[odd[i]] if odd[i] else 0.0) * column[i]
                for i in range(PAIRS)
            )
            both_value = jnp.where(top, value + swap(value), swap(value) - value)
            both_slope = jnp.where(top, slope + swap(slope), slope - swap(slope))
            up = jnp.where(top, both_value, swap(both_slope))
            down = jnp.where(top, swap(both_value), both_slope)
            x_a[b * MODES + e] = jnp.where(upward, up, down)
            x_b[b * MODES + e] = jnp.where(upward, down, up)


def side_trace_kernel(first, y_a, y_b, z_a, z_b, y_low, y_high, z_low, z_high):
    row, lane = row_in_half(), lanes()
    y_up, z_up = goes_up(lax.axis_index("gy")), goes_up(lax.axis_index("gz"))
    packed_up = packed_down = None
    for kind in range(2):
        for i in range(PAIRS):
            for e in range(MODES):
                m = i * MODES + e
                q = m % 4
                line = [first[i, b, e] for b in range(MODES)]
                traces = line_traces(line)
                high, low = traces[kind], traces[2 + kind]
                y_high[kind, m] = high
                y_low[kind, m] = low
                up, down = pltpu.roll(high, 5 + q, 0), pltpu.roll(low, q, 0) if q else low
                packed_up = up if q == 0 else jnp.where(row == q, up, packed_up)
                packed_down = down if q == 0 else jnp.where(row == q, down, packed_down)
                if q == 3:
                    k = kind * 7 + m // 4
                    y_a[k] = jnp.where(y_up, packed_up, packed_down)
                    y_b[k] = jnp.where(y_up, packed_down, packed_up)
    packed_up = packed_down = jnp.zeros((8, 128), jnp.float32)
    for i in range(PAIRS):
        for b in range(MODES):
            m = i * MODES + b
            line = [first[i, b, e] for e in range(MODES)]
            traces = line_traces(line)
            for kind in range(2):
                high, low = traces[kind], traces[2 + kind]
                z_high[kind, m] = high
                z_low[kind, m] = low
                place = 2 * m + kind
                packed_up = jnp.where(lane == place, pltpu.roll(high, 1 + place, 1), packed_up)
                down = pltpu.roll(low, place, 1) if place else low
                packed_down = jnp.where(lane == place, down, packed_down)
    z_a[...] = jnp.where(z_up, packed_up, packed_down)
    z_b[...] = jnp.where(z_up, packed_down, packed_up)


def own_kernel(first, out):
    pairs = Pairs()
    for b in range(MODES):
        for e in range(MODES):
            column = [first[i, b, e] for i in range(PAIRS)]
            for i in range(PAIRS):
                terms = []
                for j in range(PAIRS):
                    lower = OWN[2 * i + 1, 2 * j + 1] if max(i, j) < 3 else 0.0
                    terms.append(pairs(OWN[2 * i, 2 * j], lower) * column[j])
                out[i, b, e] = total(terms)
    for i in range(PAIRS):
        for b in range(MODES):
            line = [first[i, b, e] for e in range(MODES)]
            for n in range(MODES):
                out[i, b, n] += total(
                    float(OWN[n, k]) * line[k] for k in range(n % 2, MODES, 2)
                )
        for e in range(MODES):
            line = [first[i, b, e] for b in range(MODES)]
            for n in range(MODES):
                out[i, n, e] += total(
                    float(OWN[n, k]) * line[k] for k in range(n % 2, MODES, 2)
                )


def neighbour_line(low_value, low_slope, high_value, high_slope):
    plus, minus = high_value + low_value, high_value - low_value
    even = 0.5 * (low_slope - high_slope) - PENALTY * plus
    odd = -0.5 * (low_slope + high_slope) - PENALTY * minus
    return (even, 0.5 * plus), (odd, 0.5 * minus)


def vertex_pair(first_mode, second_mode):
    base, tilt = ROOT_HALF * first_mode, THIRD * second_mode
    return base - tilt, base + tilt


def sum_to_vertices(grid, pairs, row, lane):
    top = pairs.top
    rows = {}
    for (dy, dz), value in grid.items():
        rows.setdefault(dy, []).append((dz, value))
    result = [[[], []], [[], []]]
    for dy, entries in rows.items():
        inner, outer = [], []
        for dz, value in entries:
            if dz == 0:
                inner.append(value)
                continue
            moved = pltpu.roll(value, dz % 128, 1)
            inside = lane >= dz if dz > 0 else lane < 128 + dz
            inner.append(jnp.where(inside, moved, 0.0))
            outer.append(jnp.where(inside, 0.0, moved))
        for beyond, terms in ((0, inner), (1, outer)):
            if not terms:
                continue
            value = total(terms)
            if dy == 0:
                result[0][beyond].append(value)
                continue
            moved = pltpu.roll(value, dy % 8, 0)
            inside = row >= dy if dy > 0 else row < 4 + dy
            result[0][beyond].append(jnp.where(inside, moved, 0.0))
            result[1][beyond].append(jnp.where(inside, 0.0, swap(moved)))
    return [[total(result[r][z]) for z in range(2)] for r in range(2)]


def side_kernel(
    local, y_a, y_b, z_a, z_b, y_below, y_above, z_below, z_above, out
):
    row, lane = row_in_half(), lanes()
    y_even, z_even = goes_up(lax.axis_index("gy")), goes_up(lax.axis_index("gz"))
    y_has_low, y_has_high = has_place("gy", -1), has_place("gy", 1)
    z_has_low, z_has_high = has_place("gz", -1), has_place("gz", 1)
    y_low, y_high = [], []
    for k in range(FACE_ROWS):
        one, two = y_a[k], y_b[k]
        y_low.append(y_has_low * jnp.where(y_even, two, one))
        y_high.append(y_has_high * jnp.where(y_even, one, two))
    for i in range(PAIRS):
        for e in range(MODES):
            m = i * MODES + e
            q = m % 4
            seen = []
            for kind in range(2):
                halo = y_low[kind * 7 + m // 4]
                halo = pltpu.roll(halo, 8 - q, 0) if q else halo
                moved = pltpu.roll(y_below[kind, m], 1, 0)
                seen.append(jnp.where(row == 0, halo, moved))
            for kind in range(2):
                halo = y_high[kind * 7 + m // 4]
                halo = pltpu.roll(halo, 3 - q, 0) if q < 3 else halo
                moved = pltpu.roll(y_above[kind, m], 7, 0)
                seen.append(jnp.where(row == 3, halo, moved))
            parts = neighbour_line(*seen)
            for n in range(MODES):
                value, slope = parts[n % 2]
                add = float(NORMED[n]) * value
                add = add + float(SLOPE[n]) * slope if n else add
                out[i, n, e] = local[i, n, e] + add
    z_low_halo = z_has_low * jnp.where(z_even, z_b[...], z_a[...])
    z_high_halo = z_has_high * jnp.where(z_even, z_a[...], z_b[...])
    for i in range(PAIRS):
        for b in range(MODES):
            m = i * MODES + b
            seen = []
            for kind in range(2):
                place = 2 * m + kind
                halo = pltpu.roll(z_low_halo, 128 - place, 1) if place else z_low_halo
                moved = pltpu.roll(z_below[kind, m], 1, 1)
                seen.append(jnp.where(lane == 0, halo, moved))
            for kind in range(2):
                place = 2 * m + kind
                halo = pltpu.roll(z_high_halo, 127 - place, 1)
                moved = pltpu.roll(z_above[kind, m], 127, 1)
                seen.append(jnp.where(lane == 127, halo, moved))
            parts = neighbour_line(*seen)
            for e in range(MODES):
                value, slope = parts[e % 2]
                add = float(NORMED[e]) * value
                if e:
                    add = add + float(SLOPE[e]) * slope
                out[i, b, e] += add


def finish_kernel(first, local, orders, x_a, x_b, field, here, sum_a, sum_b, far):
    pairs = Pairs()
    top = pairs.top
    row, lane = row_in_half(), lanes()
    keep = keep_masks(orders[0], top)
    has_low, has_high = has_place("gx", -1), has_place("gx", 1)
    upward = goes_up(x_turn())
    one_valid = jnp.where(upward, has_high, has_low)
    two_valid = jnp.where(upward, has_low, has_high)
    x_sign = jnp.where(upward, 1.0, -1.0)
    x_even = goes_up(lax.axis_index("gx"))
    for b in range(MODES):
        for e in range(MODES):
            one, two = one_valid * x_a[b * MODES + e], two_valid * x_b[b * MODES + e]
            plus, minus = one + two, swap(x_sign * (one - two))
            slope = 0.5 * jnp.where(top, plus, minus)
            value = (-2.0 * PENALTY) * slope - 0.5 * jnp.where(top, minus, plus)
            for i in range(PAIRS):
                last = 2 * i + 1 >= MODES
                k = odd_of(i)
                applied = local[i, b, e] + (
                    pairs(NORMED[2 * i], 0.0 if last else NORMED[k]) * value
                    + pairs(SLOPE[2 * i], 0.0 if last else SLOPE[k]) * slope
                )
                one = 2.0 * RHO_SECOND / (DELTA * PENALTY)
                scale = pairs.once(one / diag(2 * i, b, e), one / diag(odd_of(i), b, e))
                mask = keep(max(2 * i, b, e), max(odd_of(i), b, e))
                kappa = 1.0 + RHO_SECOND * RHO_FIRST + 2.0 * RHO_SECOND * THETA / DELTA
                after = kappa * first[i, b, e] - (mask * scale) * applied
                field[i, b, e] = after

    grid = {}

    def add(key, value):
        grid[key] = grid[key] + value if key in grid else value

    spread = -SPREAD / PENALTY
    for e in range(MODES):
        low, high = vertex_pair(field[0, 0, e], field[0, 1, e])
        for dz in range(-1, 3):
            add((0, dz), float(spread[dz + 1, e]) * low)
            add((1, dz), float(spread[dz + 1, e]) * high)
    for b in range(MODES):
        low, high = vertex_pair(field[0, b, 0], field[0, b, 1])
        for dy in range(-1, 3):
            add((dy, 0), float(spread[dy + 1, b]) * low)
            add((dy, 1), float(spread[dy + 1, b]) * high)
    force = [
        [
            pairs.once(THETA * diag(0, b, e), THETA * diag(1, b, e)) * first[0, b, e]
            for e in range(2)
        ]
        for b in range(2)
    ]
    force = [vertex_pair(force[0][e], force[1][e]) for e in range(2)]
    for dy in range(2):
        low, high = vertex_pair(force[0][dy], force[1][dy])
        add((dy, 0), low)
        add((dy, 1), high)
    kept, turned = pairs(ROOT_HALF, THIRD), pairs(-THIRD, ROOT_HALF)
    near = {key: kept * value + turned * swap(value) for key, value in grid.items()}
    outer = {}
    corners = []
    for i in range(PAIRS):
        line = [vertex_pair(field[i, 0, e], field[i, 1, e]) for e in range(2)]
        corners.append([vertex_pair(line[0][dy], line[1][dy]) for dy in range(2)])
    for dy in range(2):
        for dz in range(2):
            sums = []
            for dx in range(-1, 3):
                part = total(
                    pairs(
                        spread[dx + 1, 2 * i],
                        spread[dx + 1, 2 * i + 1] if 2 * i + 1 < MODES else 0.0,
                    )
                    * corners[i][dy][dz]
                    for i in range(PAIRS)
                )
                sums.append(part + swap(part))
            near[dy, dz] += jnp.where(top, sums[1], sums[2])
            outer[dy, dz] = jnp.where(top, sums[0], sums[3])
    near = sum_to_vertices(near, pairs, row, lane)
    outer = sum_to_vertices(outer, pairs, row, lane)
    for z in range(2):
        here[z] = jnp.where(top, near[0][z], swap(near[1][z]))
        ahead = jnp.where(top, swap(near[0][z]), near[1][z])
        behind = jnp.where(top, outer[0][z], swap(outer[1][z]))
        sum_a[z] = jnp.where(x_even, ahead, behind)
        sum_b[z] = jnp.where(x_even, behind, ahead)
        far[z] = jnp.where(top, swap(outer[0][z]), outer[1][z])


def unpack_kernel(field, smoothed):
    for b in range(MODES):
        for e in range(MODES):
            for i in range(PAIRS):
                value = field[i, b, e]
                smoothed[2 * i, b, e, 0] = value[:4]
                if 2 * i + 1 < MODES:
                    smoothed[2 * i + 1, b, e, 0] = value[4:]


def column_kernel(chip, fetched, mated, third, column, blocks):
    count = lax.axis_size("gz")
    me = lax.axis_index("gz")
    core, place = lax.rem(me, 2), lax.div(me, 2)
    beside = place + 1 - 2 * lax.rem(place, 2)
    across = lax.rem(place + 2, 4)
    asked = beside + core * (across - beside)
    zero = jnp.zeros((8, 128), jnp.float32)
    blocks[0] = zero
    blocks[count + 1] = zero
    for source, sender, pair in (
        (place, core, chip),
        (asked, core, fetched),
        (beside + across - asked, 1 - core, mated),
        (3 - place, core, third),
    ):
        blocks[2 * source + sender + 1] = pair[0]
        blocks[2 * source + 2 - sender] = pair[1]
    lane = lax.broadcasted_iota(jnp.int32, (4, 128), 1)
    row = lax.broadcasted_iota(jnp.int32, (4, 128), 0)
    interior = (lax.axis_index("gx") > 0) & (lax.axis_index("gy") * 4 + row > 0)
    for k in range(count):
        value = (
            blocks[k + 1, :4]
            + jnp.where(lane < 2, blocks[k, 4:], 0.0)
            + jnp.where(lane == 127, blocks[k + 2, 4:], 0.0)
        )
        here = interior & (lane > 0) if k == 0 else interior
        column[0, :, k * 128 : (k + 1) * 128] = jnp.where(here, value, 0.0)


def shape(*dims):
    return jax.ShapeDtypeStruct(dims, jnp.float32)


def in_vmem(count):
    return [pl.BlockSpec(memory_space=pltpu.VMEM)] * count


def call(kernel, name, inputs, outputs, flops, scratch=(), in_hbm=False):
    size = sum(4 * int(np.prod(v.shape)) for v in (*inputs, *outputs))
    space = pltpu.HBM if in_hbm else pltpu.VMEM
    return pl.pallas_call(
        kernel,
        out_shape=outputs,
        in_specs=[pl.BlockSpec(memory_space=space)] * len(inputs),
        out_specs=[pl.BlockSpec(memory_space=pltpu.VMEM)] * len(outputs),
        scratch_shapes=list(scratch),
        name=name,
        cost_estimate=pl.CostEstimate(flops=flops, bytes_accessed=size, transcendentals=0),
        compiler_params=pltpu.CompilerParams(vmem_limit_bytes=24 * 1024 * 1024),
    )(*inputs)


def flip(value, axis, bits):
    return lax.ppermute(value, axis, [(i, i ^ bits) for i in range(lax.axis_size(axis))])


def exchange(value, partner):
    axes = ("gx", "gy", "gz")
    sizes = [lax.axis_size(name) for name in axes]
    route = [
        (source, int(np.ravel_multi_index(partner(list(place)), sizes)))
        for source, place in enumerate(np.ndindex(*sizes))
    ]
    return lax.ppermute(value, axes, route)


def second_of_pair(place, k, count, spare, bit):
    if place[k] in (0, count - 1):
        place[spare] ^= bit
    else:
        place[k] += 1 if place[k] % 2 else -1
    return place


def second_pairs(value, axis):
    k, count = ("gx", "gy", "gz").index(axis), lax.axis_size(axis)
    return exchange(value, lambda place: second_of_pair(place, k, count, 0 if k == 2 else 2, 1))


def x_pairs(value, turn):
    count = lax.axis_size("gx")

    def partner(place):
        if place[2] % 2 == turn:
            place[0] ^= 1
            return place
        return second_of_pair(place, 0, count, 1, 1)

    return exchange(value, partner)


def both_y_sides(value):
    count = lax.axis_size("gy")

    def partner(place):
        if place[2] % 2:
            place[1] ^= 1
            return place
        return second_of_pair(place, 1, count, 0, 1)

    return exchange(value, partner)


def two_chips(value):
    def partner(place):
        place[2] ^= 4 if place[2] % 2 else 2
        return place

    return exchange(value, partner)


def inside(axis, distance):
    place = lax.axis_index(axis) + distance
    return ((place >= 0) & (place < lax.axis_size(axis))).astype(jnp.float32)


def per_device(rhs, orders):
    cells = (PAIRS, MODES, MODES, 8, 128)
    sides = (shape(2, 28, 8, 128),) * 4
    first, x_a, x_b, held = call(
        trace_kernel,
        "x_traces",
        tuple(pltpu.with_memory_space_constraint(v, pltpu.HBM) for v in (rhs, orders)),
        (
            shape(*cells), shape(49, 8, 128), shape(49, 8, 128),
            jax.ShapeDtypeStruct(orders.shape, jnp.int32),
        ),
        4_000_000,
        scratch=(pltpu.VMEM(rhs.shape, jnp.float32), pltpu.SemaphoreType.DMA((MODES + 1,))),
        in_hbm=True,
    )
    x_a, x_b = x_pairs(x_a, 0), x_pairs(x_b, 1)
    y_a, y_b, z_a, z_b, y_low, y_high, z_low, z_high = call(
        side_trace_kernel,
        "side_traces",
        (first,),
        (shape(FACE_ROWS, 8, 128),) * 2 + (shape(8, 128),) * 2 + sides,
        SIDE_COST,
    )
    y_a, y_b = flip(y_a, "gy", 1), second_pairs(y_b, "gy")
    z_a, z_b = flip(z_a, "gz", 1), second_pairs(z_b, "gz")
    (local,) = call(own_kernel, "own_cells", (first,), (shape(*cells),), OWN_COST)
    (local,) = call(
        side_kernel,
        "side_halo",
        (local, y_a, y_b, z_a, z_b, y_high, y_low, z_high, z_low),
        (shape(*cells),),
        HALO_COST,
    )
    field, here, sum_a, sum_b, far = call(
        finish_kernel,
        "smooth_and_restrict",
        (first, local, held, x_a, x_b),
        (shape(*cells),) + (shape(2, 8, 128),) * 4,
        5_000_000,
    )
    (smoothed,) = call(unpack_kernel, "unpack_modes", (field,), (shape(*rhs.shape),), 200_000)
    from_far = flip(far, "gx", 2)
    from_a = flip(sum_a, "gx", 1)
    from_b = second_pairs(sum_b, "gx")
    sums = (
        here
        + inside("gx", -2) * from_far
        + from_a
        + inside("gx", -1) * inside("gx", 1) * from_b
    )
    count = lax.axis_size("gz")
    chip = jnp.stack([sums, flip(sums, "gz", 1)])
    from_beside = both_y_sides(chip)
    from_low = (lax.axis_index("gy") + lax.axis_index("gz")) % 2 == 0
    row = lax.broadcasted_iota(jnp.int32, (1, 1, 4, 1), 2)
    wanted = jnp.where(from_low, row < 2, row == 3)
    valid = jnp.where(from_low, inside("gy", -1), inside("gy", 1))
    edges = jnp.where(wanted, from_beside[:, :, 4:], 0.0) * valid
    edges = edges.reshape(2, 8, 128)
    mated = flip(edges, "gz", 1)
    owned = chip[:, :, :4].reshape(2, 8, 128) + edges + mated[::-1]
    fetched = two_chips(owned)
    third = flip(owned, "gz", 6)
    (column,) = call(
        column_kernel,
        "column",
        (owned, fetched, flip(fetched, "gz", 1), third),
        (shape(1, 4, 128 * count),),
        20_000,
        scratch=(pltpu.VMEM((count + 2, 8, 128), jnp.float32),),
    )
    return smoothed, column


def solution(mesh):
    return jax.shard_map(
        per_device,
        mesh=mesh,
        in_specs=(P(None, None, None, "gx", "gy", "gz"), P("gx", "gy", "gz")),
        out_specs=(P(None, None, None, "gx", "gy", "gz"), P("gx", "gy", None)),
        check_vma=False,
    )
```

```python
import jax
import jax.numpy as jnp
import numpy as np
from jax import lax
from jax.experimental import pallas as pl
from jax.experimental.pallas import tpu as pltpu
from jax.sharding import PartitionSpec as P

PENALTY = 49.0
EIGEN_HIGH = 2.4
EIGEN_LOW = 0.24
THETA = 0.5 * (EIGEN_HIGH + EIGEN_LOW)
DELTA = 0.5 * (EIGEN_HIGH - EIGEN_LOW)
RHO_FIRST = DELTA / THETA
RHO_SECOND = 1.0 / (2.0 * THETA / DELTA - RHO_FIRST)
MODES = 7
PAIRS = 4
FACE_ROWS = 14
SIDE_COST = 4_000_000
OWN_COST = 1_400_000_000
HALO_COST = 4_000_000


def basis_tables():
    degree = np.arange(MODES)
    normed = np.sqrt((2.0 * degree + 1.0) / 2.0)
    smaller = np.minimum(degree[:, None], degree[None, :])
    parity = (degree[:, None] + degree[None, :]) % 2 == 0
    stiffness = np.where(parity, normed[:, None] * normed[None, :] * smaller * (smaller + 1), 0.0)
    signs = (-1.0) ** degree
    slope = normed * degree * (degree + 1) / 2.0
    high, high_slope = normed, slope
    low, low_slope = normed * signs, -slope * signs
    own = (
        stiffness
        + PENALTY * (np.outer(high, high) + np.outer(low, low))
        - 0.5 * (np.outer(high, high_slope) + np.outer(high_slope, high))
        + 0.5 * (np.outer(low, low_slope) + np.outer(low_slope, low))
    )
    own = np.where(parity, own, 0.0)
    to_next = np.outer(low, 0.5 * high_slope - PENALTY * high) - 0.5 * np.outer(low_slope, high)
    to_last = np.outer(high, -PENALTY * low - 0.5 * low_slope) + 0.5 * np.outer(high_slope, low)
    one_axis = normed * normed * degree * (degree + 1) + 2.0 * (
        PENALTY * normed * normed - normed * slope
    )
    third = np.sqrt(1.5) / 3.0
    vertex = np.zeros((MODES, 2))
    vertex[0] = np.sqrt(0.5)
    vertex[1] = -third, third
    spread = np.stack(
        [
            vertex[:, 0] @ to_last,
            vertex[:, 1] @ to_last + vertex[:, 0] @ own,
            vertex[:, 1] @ own + vertex[:, 0] @ to_next,
            vertex[:, 1] @ to_next,
        ]
    )
    return normed, slope, own, one_axis, spread, third


NORMED, SLOPE, OWN, ONE_AXIS, SPREAD, THIRD = basis_tables()
ROOT_HALF = float(np.sqrt(0.5))


def diag(a, b, e):
    return float((ONE_AXIS[a] + ONE_AXIS[b] + ONE_AXIS[e]) / PENALTY)


def half_mask():
    return lax.broadcasted_iota(jnp.int32, (8, 128), 0) < 4


def row_in_half():
    return lax.broadcasted_iota(jnp.int32, (8, 128), 0) % 4


def lanes():
    return lax.broadcasted_iota(jnp.int32, (8, 128), 1)


def swap(value):
    return pltpu.roll(value, 4, 0)


class Pairs:
    def __init__(self):
        self.top = half_mask()
        self.known = {}

    def __call__(self, upper, lower):
        key = (float(upper), float(lower))
        if key[0] == key[1]:
            return jnp.float32(key[0])
        if key not in self.known:
            self.known[key] = jnp.where(self.top, jnp.float32(key[0]), jnp.float32(key[1]))
        return self.known[key]

    def once(self, upper, lower):
        if float(upper) == float(lower):
            return jnp.float32(upper)
        return jnp.where(self.top, jnp.float32(upper), jnp.float32(lower))


def total(terms):
    terms = list(terms)
    while len(terms) > 1:
        terms = [
            terms[k] + terms[k + 1] if k + 1 < len(terms) else terms[k]
            for k in range(0, len(terms), 2)
        ]
    return terms[0]


def keep_masks(orders, top):
    both = jnp.concatenate([orders, orders], axis=0)
    known = {}

    def get(upper, lower):
        if (upper, lower) not in known:
            if upper == lower:
                bound = jnp.int32(upper)
            else:
                bound = jnp.where(top, jnp.int32(upper), jnp.int32(lower))
            known[upper, lower] = (both >= bound).astype(jnp.float32)
        return known[upper, lower]

    return get


def odd_of(pair):
    return min(2 * pair + 1, MODES - 1)


def line_traces(line):
    even = total(float(NORMED[n]) * line[n] for n in range(0, MODES, 2))
    odd = total(float(NORMED[n]) * line[n] for n in range(1, MODES, 2))
    even_slope = total(float(SLOPE[n]) * line[n] for n in range(2, MODES, 2))
    odd_slope = total(float(SLOPE[n]) * line[n] for n in range(1, MODES, 2))
    return even + odd, even_slope + odd_slope, even - odd, odd_slope - even_slope


def x_turn():
    return lax.axis_index("gx") + lax.axis_index("gz")


def goes_up(turn):
    return jnp.full((8, 128), lax.rem(turn, 2), jnp.int32) == 0


def has_place(axis, distance):
    place = lax.axis_index(axis) + distance
    return jnp.where((place >= 0) & (place < lax.axis_size(axis)), 1.0, 0.0).astype(jnp.float32)


def trace_kernel(
    rhs_hbm, orders_hbm, first, x_a, x_b, orders, rhs, arrived,
):
    copies = [pltpu.make_async_copy(orders_hbm, orders, arrived.at[MODES])]
    for b in range(MODES):
        copies.append(pltpu.make_async_copy(rhs_hbm.at[:, b], rhs.at[:, b], arrived.at[b]))
    for copy in copies:
        copy.start()
    pairs = Pairs()
    top = pairs.top
    upward = goes_up(x_turn())
    copies[0].wait()
    keep = keep_masks(orders[0], top)
    for b in range(MODES):
        copies[1 + b].wait()
        for e in range(MODES):
            column = []
            for i in range(PAIRS):
                upper = rhs[2 * i, b, e, 0]
                lower = rhs[2 * i + 1, b, e, 0] if 2 * i + 1 < MODES else jnp.zeros_like(upper)
                cell = jnp.concatenate([upper, lower], axis=0)
                mask = keep(max(2 * i, b, e), max(odd_of(i), b, e))
                scale = pairs.once(
                    1.0 / (THETA * diag(2 * i, b, e)), 1.0 / (THETA * diag(odd_of(i), b, e))
                )
                cell = cell * mask * scale
                first[i, b, e] = cell
                column.append(cell)
            odd = [odd_of(i) if 2 * i + 1 < MODES else None for i in range(PAIRS)]
            value = total(
                pairs(NORMED[2 * i], NORMED[odd[i]] if odd[i] else 0.0) * column[i]
                for i in range(PAIRS)
            )
            slope = total(
                pairs(SLOPE[2 * i], SLOPE[odd[i]] if odd[i] else 0.0) * column[i]
                for i in range(PAIRS)
            )
            both_value = jnp.where(top, value + swap(value), swap(value) - value)
            both_slope = jnp.where(top, slope + swap(slope), slope - swap(slope))
            up = jnp.where(top, both_value, swap(both_slope))
            down = jnp.where(top, swap(both_value), both_slope)
            x_a[b * MODES + e] = jnp.where(upward, up, down)
            x_b[b * MODES + e] = jnp.where(upward, down, up)


def side_trace_kernel(first, y_a, y_b, z_a, z_b, y_low, y_high, z_low, z_high):
    row, lane = row_in_half(), lanes()
    y_up, z_up = goes_up(lax.axis_index("gy")), goes_up(lax.axis_index("gz"))
    packed_up = packed_down = None
    for kind in range(2):
        for i in range(PAIRS):
            for e in range(MODES):
                m = i * MODES + e
                q = m % 4
                line = [first[i, b, e] for b in range(MODES)]
                traces = line_traces(line)
                high, low = traces[kind], traces[2 + kind]
                y_high[kind, m] = high
                y_low[kind, m] = low
                up, down = pltpu.roll(high, 5 + q, 0), pltpu.roll(low, q, 0) if q else low
                packed_up = up if q == 0 else jnp.where(row == q, up, packed_up)
                packed_down = down if q == 0 else jnp.where(row == q, down, packed_down)
                if q == 3:
                    k = kind * 7 + m // 4
                    y_a[k] = jnp.where(y_up, packed_up, packed_down)
                    y_b[k] = jnp.where(y_up, packed_down, packed_up)
    packed_up = packed_down = jnp.zeros((8, 128), jnp.float32)
    for i in range(PAIRS):
        for b in range(MODES):
            m = i * MODES + b
            line = [first[i, b, e] for e in range(MODES)]
            traces = line_traces(line)
            for kind in range(2):
                high, low = traces[kind], traces[2 + kind]
                z_high[kind, m] = high
                z_low[kind, m] = low
                place = 2 * m + kind
                packed_up = jnp.where(lane == place, pltpu.roll(high, 1 + place, 1), packed_up)
                down = pltpu.roll(low, place, 1) if place else low
                packed_down = jnp.where(lane == place, down, packed_down)
    z_a[...] = jnp.where(z_up, packed_up, packed_down)
    z_b[...] = jnp.where(z_up, packed_down, packed_up)


def own_kernel(first, out):
    pairs = Pairs()
    for b in range(MODES):
        for e in range(MODES):
            column = [first[i, b, e] for i in range(PAIRS)]
            for i in range(PAIRS):
                terms = []
                for j in range(PAIRS):
                    lower = OWN[2 * i + 1, 2 * j + 1] if max(i, j) < 3 else 0.0
                    terms.append(pairs(OWN[2 * i, 2 * j], lower) * column[j])
                out[i, b, e] = total(terms)
    for i in range(PAIRS):
        for b in range(MODES):
            line = [first[i, b, e] for e in range(MODES)]
            for n in range(MODES):
                out[i, b, n] += total(
                    float(OWN[n, k]) * line[k] for k in range(n % 2, MODES, 2)
                )
        for e in range(MODES):
            line = [first[i, b, e] for b in range(MODES)]
            for n in range(MODES):
                out[i, n, e] += total(
                    float(OWN[n, k]) * line[k] for k in range(n % 2, MODES, 2)
                )


def neighbour_line(low_value, low_slope, high_value, high_slope):
    plus, minus = high_value + low_value, high_value - low_value
    even = 0.5 * (low_slope - high_slope) - PENALTY * plus
    odd = -0.5 * (low_slope + high_slope) - PENALTY * minus
    return (even, 0.5 * plus), (odd, 0.5 * minus)


def vertex_pair(first_mode, second_mode):
    base, tilt = ROOT_HALF * first_mode, THIRD * second_mode
    return base - tilt, base + tilt


def sum_to_vertices(grid, pairs, row, lane):
    top = pairs.top
    rows = {}
    for (dy, dz), value in grid.items():
        rows.setdefault(dy, []).append((dz, value))
    result = [[[], []], [[], []]]
    for dy, entries in rows.items():
        inner, outer = [], []
        for dz, value in entries:
            if dz == 0:
                inner.append(value)
                continue
            moved = pltpu.roll(value, dz % 128, 1)
            inside = lane >= dz if dz > 0 else lane < 128 + dz
            inner.append(jnp.where(inside, moved, 0.0))
            outer.append(jnp.where(inside, 0.0, moved))
        for beyond, terms in ((0, inner), (1, outer)):
            if not terms:
                continue
            value = total(terms)
            if dy == 0:
                result[0][beyond].append(value)
                continue
            moved = pltpu.roll(value, dy % 8, 0)
            inside = row >= dy if dy > 0 else row < 4 + dy
            result[0][beyond].append(jnp.where(inside, moved, 0.0))
            result[1][beyond].append(jnp.where(inside, 0.0, swap(moved)))
    return [[total(result[r][z]) for z in range(2)] for r in range(2)]


def side_kernel(
    local, z_b, y_a, y_b, z_a, y_below, y_above, z_below, z_above, out
):
    row, lane = row_in_half(), lanes()
    y_even, z_even = goes_up(lax.axis_index("gy")), goes_up(lax.axis_index("gz"))
    y_has_low, y_has_high = has_place("gy", -1), has_place("gy", 1)
    z_has_low, z_has_high = has_place("gz", -1), has_place("gz", 1)
    y_low, y_high = [], []
    for k in range(FACE_ROWS):
        one, two = y_a[k], y_b[k]
        y_low.append(y_has_low * jnp.where(y_even, two, one))
        y_high.append(y_has_high * jnp.where(y_even, one, two))
    for i in range(PAIRS):
        for e in range(MODES):
            m = i * MODES + e
            q = m % 4
            seen = []
            for kind in range(2):
                halo = y_low[kind * 7 + m // 4]
                halo = pltpu.roll(halo, 8 - q, 0) if q else halo
                moved = pltpu.roll(y_below[kind, m], 1, 0)
                seen.append(jnp.where(row == 0, halo, moved))
            for kind in range(2):
                halo = y_high[kind * 7 + m // 4]
                halo = pltpu.roll(halo, 3 - q, 0) if q < 3 else halo
                moved = pltpu.roll(y_above[kind, m], 7, 0)
                seen.append(jnp.where(row == 3, halo, moved))
            parts = neighbour_line(*seen)
            for n in range(MODES):
                value, slope = parts[n % 2]
                add = float(NORMED[n]) * value
                add = add + float(SLOPE[n]) * slope if n else add
                out[i, n, e] = local[i, n, e] + add
    z_low_halo = z_has_low * jnp.where(z_even, z_b[...], z_a[...])
    z_high_halo = z_has_high * jnp.where(z_even, z_a[...], z_b[...])
    for i in range(PAIRS):
        for b in range(MODES):
            m = i * MODES + b
            seen = []
            for kind in range(2):
                place = 2 * m + kind
                halo = pltpu.roll(z_low_halo, 128 - place, 1) if place else z_low_halo
                moved = pltpu.roll(z_below[kind, m], 1, 1)
                seen.append(jnp.where(lane == 0, halo, moved))
            for kind in range(2):
                place = 2 * m + kind
                halo = pltpu.roll(z_high_halo, 127 - place, 1)
                moved = pltpu.roll(z_above[kind, m], 127, 1)
                seen.append(jnp.where(lane == 127, halo, moved))
            parts = neighbour_line(*seen)
            for e in range(MODES):
                value, slope = parts[e % 2]
                add = float(NORMED[e]) * value
                if e:
                    add = add + float(SLOPE[e]) * slope
                out[i, b, e] += add


def finish_kernel(first, local, orders, x_a, x_b, field, here, sum_a, sum_b, far):
    pairs = Pairs()
    top = pairs.top
    row, lane = row_in_half(), lanes()
    keep = keep_masks(orders[0], top)
    has_low, has_high = has_place("gx", -1), has_place("gx", 1)
    upward = goes_up(x_turn())
    one_valid = jnp.where(upward, has_high, has_low)
    two_valid = jnp.where(upward, has_low, has_high)
    x_sign = jnp.where(upward, 1.0, -1.0)
    x_even = goes_up(lax.axis_index("gx"))
    for b in range(MODES):
        for e in range(MODES):
            one, two = one_valid * x_a[b * MODES + e], two_valid * x_b[b * MODES + e]
            plus, minus = one + two, swap(x_sign * (one - two))
            slope = 0.5 * jnp.where(top, plus, minus)
            value = (-2.0 * PENALTY) * slope - 0.5 * jnp.where(top, minus, plus)
            for i in range(PAIRS):
                last = 2 * i + 1 >= MODES
                k = odd_of(i)
                applied = local[i, b, e] + (
                    pairs(NORMED[2 * i], 0.0 if last else NORMED[k]) * value
                    + pairs(SLOPE[2 * i], 0.0 if last else SLOPE[k]) * slope
                )
                one = 2.0 * RHO_SECOND / (DELTA * PENALTY)
                scale = pairs.once(one / diag(2 * i, b, e), one / diag(odd_of(i), b, e))
                mask = keep(max(2 * i, b, e), max(odd_of(i), b, e))
                kappa = 1.0 + RHO_SECOND * RHO_FIRST + 2.0 * RHO_SECOND * THETA / DELTA
                after = kappa * first[i, b, e] - (mask * scale) * applied
                field[i, b, e] = after

    grid = {}

    def add(key, value):
        grid[key] = grid[key] + value if key in grid else value

    spread = -SPREAD / PENALTY
    for e in range(MODES):
        low, high = vertex_pair(field[0, 0, e], field[0, 1, e])
        for dz in range(-1, 3):
            add((0, dz), float(spread[dz + 1, e]) * low)
            add((1, dz), float(spread[dz + 1, e]) * high)
    for b in range(MODES):
        low, high = vertex_pair(field[0, b, 0], field[0, b, 1])
        for dy in range(-1, 3):
            add((dy, 0), float(spread[dy + 1, b]) * low)
            add((dy, 1), float(spread[dy + 1, b]) * high)
    force = [
        [
            pairs.once(THETA * diag(0, b, e), THETA * diag(1, b, e)) * first[0, b, e]
            for e in range(2)
        ]
        for b in range(2)
    ]
    force = [vertex_pair(force[0][e], force[1][e]) for e in range(2)]
    for dy in range(2):
        low, high = vertex_pair(force[0][dy], force[1][dy])
        add((dy, 0), low)
        add((dy, 1), high)
    kept, turned = pairs(ROOT_HALF, THIRD), pairs(-THIRD, ROOT_HALF)
    near = {key: kept * value + turned * swap(value) for key, value in grid.items()}
    outer = {}
    corners = []
    for i in range(PAIRS):
        line = [vertex_pair(field[i, 0, e], field[i, 1, e]) for e in range(2)]
        corners.append([vertex_pair(line[0][dy], line[1][dy]) for dy in range(2)])
    for dy in range(2):
        for dz in range(2):
            sums = []
            for dx in range(-1, 3):
                part = total(
                    pairs(
                        spread[dx + 1, 2 * i],
                        spread[dx + 1, 2 * i + 1] if 2 * i + 1 < MODES else 0.0,
                    )
                    * corners[i][dy][dz]
                    for i in range(PAIRS)
                )
                sums.append(part + swap(part))
            near[dy, dz] += jnp.where(top, sums[1], sums[2])
            outer[dy, dz] = jnp.where(top, sums[0], sums[3])
    near = sum_to_vertices(near, pairs, row, lane)
    outer = sum_to_vertices(outer, pairs, row, lane)
    for z in range(2):
        here[z] = jnp.where(top, near[0][z], swap(near[1][z]))
        ahead = jnp.where(top, swap(near[0][z]), near[1][z])
        behind = jnp.where(top, outer[0][z], swap(outer[1][z]))
        sum_a[z] = jnp.where(x_even, ahead, behind)
        sum_b[z] = jnp.where(x_even, behind, ahead)
        far[z] = jnp.where(top, swap(outer[0][z]), outer[1][z])


def unpack_kernel(field, smoothed):
    for b in range(MODES):
        for e in range(MODES):
            for i in range(PAIRS):
                value = field[i, b, e]
                smoothed[2 * i, b, e, 0] = value[:4]
                if 2 * i + 1 < MODES:
                    smoothed[2 * i + 1, b, e, 0] = value[4:]


def column_kernel(chip, fetched, mated, third, column, blocks):
    count = lax.axis_size("gz")
    me = lax.axis_index("gz")
    core, place = lax.rem(me, 2), lax.div(me, 2)
    beside = place + 1 - 2 * lax.rem(place, 2)
    across = lax.rem(place + 2, 4)
    asked = beside + core * (across - beside)
    zero = jnp.zeros((8, 128), jnp.float32)
    blocks[0] = zero
    blocks[count + 1] = zero
    for source, sender, pair in (
        (place, core, chip),
        (asked, core, fetched),
        (beside + across - asked, 1 - core, mated),
        (3 - place, core, third),
    ):
        blocks[2 * source + sender + 1] = pair[0]
        blocks[2 * source + 2 - sender] = pair[1]
    lane = lax.broadcasted_iota(jnp.int32, (4, 128), 1)
    row = lax.broadcasted_iota(jnp.int32, (4, 128), 0)
    interior = (lax.axis_index("gx") > 0) & (lax.axis_index("gy") * 4 + row > 0)
    for k in range(count):
        value = (
            blocks[k + 1, :4]
            + jnp.where(lane < 2, blocks[k, 4:], 0.0)
            + jnp.where(lane == 127, blocks[k + 2, 4:], 0.0)
        )
        here = interior & (lane > 0) if k == 0 else interior
        column[0, :, k * 128 : (k + 1) * 128] = jnp.where(here, value, 0.0)


def shape(*dims):
    return jax.ShapeDtypeStruct(dims, jnp.float32)


def in_vmem(count):
    return [pl.BlockSpec(memory_space=pltpu.VMEM)] * count


def call(kernel, name, inputs, outputs, flops, scratch=(), in_hbm=False):
    size = sum(4 * int(np.prod(v.shape)) for v in (*inputs, *outputs))
    space = pltpu.HBM if in_hbm else pltpu.VMEM
    return pl.pallas_call(
        kernel,
        out_shape=outputs,
        in_specs=[pl.BlockSpec(memory_space=space)] * len(inputs),
        out_specs=[pl.BlockSpec(memory_space=pltpu.VMEM)] * len(outputs),
        scratch_shapes=list(scratch),
        name=name,
        cost_estimate=pl.CostEstimate(flops=flops, bytes_accessed=size, transcendentals=0),
        compiler_params=pltpu.CompilerParams(vmem_limit_bytes=24 * 1024 * 1024),
    )(*inputs)


def flip(value, axis, bits):
    return lax.ppermute(value, axis, [(i, i ^ bits) for i in range(lax.axis_size(axis))])


def exchange(value, partner):
    axes = ("gx", "gy", "gz")
    sizes = [lax.axis_size(name) for name in axes]
    route = [
        (source, int(np.ravel_multi_index(partner(list(place)), sizes)))
        for source, place in enumerate(np.ndindex(*sizes))
    ]
    return lax.ppermute(value, axes, route)


def second_of_pair(place, k, count, spare, bit):
    if place[k] in (0, count - 1):
        place[spare] ^= bit
    else:
        place[k] += 1 if place[k] % 2 else -1
    return place


def second_pairs(value, axis):
    k, count = ("gx", "gy", "gz").index(axis), lax.axis_size(axis)
    return exchange(value, lambda place: second_of_pair(place, k, count, 0 if k == 2 else 2, 1))


def x_pairs(value, turn):
    count = lax.axis_size("gx")

    def partner(place):
        if place[2] % 2 == turn:
            place[0] ^= 1
            return place
        return second_of_pair(place, 0, count, 1, 1)

    return exchange(value, partner)


def both_y_sides(value):
    count = lax.axis_size("gy")

    def partner(place):
        if place[2] % 2:
            place[1] ^= 1
            return place
        return second_of_pair(place, 1, count, 0, 1)

    return exchange(value, partner)


def two_chips(value):
    def partner(place):
        place[2] ^= 4 if place[2] % 2 else 2
        return place

    return exchange(value, partner)


def inside(axis, distance):
    place = lax.axis_index(axis) + distance
    return ((place >= 0) & (place < lax.axis_size(axis))).astype(jnp.float32)


def per_device(rhs, orders):
    cells = (PAIRS, MODES, MODES, 8, 128)
    sides = (shape(2, 28, 8, 128),) * 4
    first, x_a, x_b, held = call(
        trace_kernel,
        "x_traces",
        tuple(pltpu.with_memory_space_constraint(v, pltpu.HBM) for v in (rhs, orders)),
        (
            shape(*cells), shape(49, 8, 128), shape(49, 8, 128),
            jax.ShapeDtypeStruct(orders.shape, jnp.int32),
        ),
        4_000_000,
        scratch=(pltpu.VMEM(rhs.shape, jnp.float32), pltpu.SemaphoreType.DMA((MODES + 1,))),
        in_hbm=True,
    )
    x_a, x_b = x_pairs(x_a, 0), x_pairs(x_b, 1)
    y_a, y_b, z_a, z_b, y_low, y_high, z_low, z_high = call(
        side_trace_kernel,
        "side_traces",
        (first,),
        (shape(FACE_ROWS, 8, 128),) * 2 + (shape(8, 128),) * 2 + sides,
        SIDE_COST,
    )
    z_b = second_pairs(z_b, "gz")
    y_a, y_b = flip(y_a, "gy", 1), second_pairs(y_b, "gy")
    z_a = flip(z_a, "gz", 1)
    (local,) = call(own_kernel, "own_cells", (first,), (shape(*cells),), OWN_COST)
    (local,) = call(
        side_kernel,
        "side_halo",
        (local, z_b, y_a, y_b, z_a, y_high, y_low, z_high, z_low),
        (shape(*cells),),
        HALO_COST,
    )
    field, here, sum_a, sum_b, far = call(
        finish_kernel,
        "smooth_and_restrict",
        (first, local, held, x_a, x_b),
        (shape(*cells),) + (shape(2, 8, 128),) * 4,
        5_000_000,
    )
    (smoothed,) = call(unpack_kernel, "unpack_modes", (field,), (shape(*rhs.shape),), 200_000)
    from_far = flip(far, "gx", 2)
    from_a = flip(sum_a, "gx", 1)
    from_b = second_pairs(sum_b, "gx")
    sums = (
        here
        + inside("gx", -2) * from_far
        + from_a
        + inside("gx", -1) * inside("gx", 1) * from_b
    )
    count = lax.axis_size("gz")
    chip = jnp.stack([sums, flip(sums, "gz", 1)])
    from_beside = both_y_sides(chip)
    from_low = (lax.axis_index("gy") + lax.axis_index("gz")) % 2 == 0
    row = lax.broadcasted_iota(jnp.int32, (1, 1, 4, 1), 2)
    wanted = jnp.where(from_low, row < 2, row == 3)
    valid = jnp.where(from_low, inside("gy", -1), inside("gy", 1))
    edges = jnp.where(wanted, from_beside[:, :, 4:], 0.0) * valid
    edges = edges.reshape(2, 8, 128)
    mated = flip(edges, "gz", 1)
    owned = chip[:, :, :4].reshape(2, 8, 128) + edges + mated[::-1]
    fetched = two_chips(owned)
    third = flip(owned, "gz", 6)
    (column,) = call(
        column_kernel,
        "column",
        (owned, fetched, flip(fetched, "gz", 1), third),
        (shape(1, 4, 128 * count),),
        20_000,
        scratch=(pltpu.VMEM((count + 2, 8, 128), jnp.float32),),
    )
    return smoothed, column


def solution(mesh):
    return jax.shard_map(
        per_device,
        mesh=mesh,
        in_specs=(P(None, None, None, "gx", "gy", "gz"), P("gx", "gy", "gz")),
        out_specs=(P(None, None, None, "gx", "gy", "gz"), P("gx", "gy", None)),
        check_vma=False,
    )
```

```python
import jax
import jax.numpy as jnp
import numpy as np
from jax import lax
from jax.experimental import pallas as pl
from jax.experimental.pallas import tpu as pltpu
from jax.sharding import PartitionSpec as P

PENALTY = 49.0
EIGEN_HIGH = 2.4
EIGEN_LOW = 0.24
THETA = 0.5 * (EIGEN_HIGH + EIGEN_LOW)
DELTA = 0.5 * (EIGEN_HIGH - EIGEN_LOW)
RHO_FIRST = DELTA / THETA
RHO_SECOND = 1.0 / (2.0 * THETA / DELTA - RHO_FIRST)
MODES = 7
PAIRS = 4
FACE_ROWS = 14
SIDE_COST = 4_000_000
OWN_COST = 1_400_000_000
HALO_COST = 4_000_000


def basis_tables():
    degree = np.arange(MODES)
    normed = np.sqrt((2.0 * degree + 1.0) / 2.0)
    smaller = np.minimum(degree[:, None], degree[None, :])
    parity = (degree[:, None] + degree[None, :]) % 2 == 0
    stiffness = np.where(parity, normed[:, None] * normed[None, :] * smaller * (smaller + 1), 0.0)
    signs = (-1.0) ** degree
    slope = normed * degree * (degree + 1) / 2.0
    high, high_slope = normed, slope
    low, low_slope = normed * signs, -slope * signs
    own = (
        stiffness
        + PENALTY * (np.outer(high, high) + np.outer(low, low))
        - 0.5 * (np.outer(high, high_slope) + np.outer(high_slope, high))
        + 0.5 * (np.outer(low, low_slope) + np.outer(low_slope, low))
    )
    own = np.where(parity, own, 0.0)
    to_next = np.outer(low, 0.5 * high_slope - PENALTY * high) - 0.5 * np.outer(low_slope, high)
    to_last = np.outer(high, -PENALTY * low - 0.5 * low_slope) + 0.5 * np.outer(high_slope, low)
    one_axis = normed * normed * degree * (degree + 1) + 2.0 * (
        PENALTY * normed * normed - normed * slope
    )
    third = np.sqrt(1.5) / 3.0
    vertex = np.zeros((MODES, 2))
    vertex[0] = np.sqrt(0.5)
    vertex[1] = -third, third
    spread = np.stack(
        [
            vertex[:, 0] @ to_last,
            vertex[:, 1] @ to_last + vertex[:, 0] @ own,
            vertex[:, 1] @ own + vertex[:, 0] @ to_next,
            vertex[:, 1] @ to_next,
        ]
    )
    return normed, slope, own, one_axis, spread, third


NORMED, SLOPE, OWN, ONE_AXIS, SPREAD, THIRD = basis_tables()
ROOT_HALF = float(np.sqrt(0.5))


def diag(a, b, e):
    return float((ONE_AXIS[a] + ONE_AXIS[b] + ONE_AXIS[e]) / PENALTY)


def half_mask():
    return lax.broadcasted_iota(jnp.int32, (8, 128), 0) < 4


def row_in_half():
    return lax.broadcasted_iota(jnp.int32, (8, 128), 0) % 4


def lanes():
    return lax.broadcasted_iota(jnp.int32, (8, 128), 1)


def swap(value):
    return pltpu.roll(value, 4, 0)


class Pairs:
    def __init__(self):
        self.top = half_mask()
        self.known = {}

    def __call__(self, upper, lower):
        key = (float(upper), float(lower))
        if key[0] == key[1]:
            return jnp.float32(key[0])
        if key not in self.known:
            self.known[key] = jnp.where(self.top, jnp.float32(key[0]), jnp.float32(key[1]))
        return self.known[key]

    def once(self, upper, lower):
        if float(upper) == float(lower):
            return jnp.float32(upper)
        return jnp.where(self.top, jnp.float32(upper), jnp.float32(lower))


def total(terms):
    terms = list(terms)
    while len(terms) > 1:
        terms = [
            terms[k] + terms[k + 1] if k + 1 < len(terms) else terms[k]
            for k in range(0, len(terms), 2)
        ]
    return terms[0]


def keep_masks(orders, top):
    both = jnp.concatenate([orders, orders], axis=0)
    known = {}

    def get(upper, lower):
        if (upper, lower) not in known:
            if upper == lower:
                bound = jnp.int32(upper)
            else:
                bound = jnp.where(top, jnp.int32(upper), jnp.int32(lower))
            known[upper, lower] = (both >= bound).astype(jnp.float32)
        return known[upper, lower]

    return get


def odd_of(pair):
    return min(2 * pair + 1, MODES - 1)


def line_traces(line):
    even = total(float(NORMED[n]) * line[n] for n in range(0, MODES, 2))
    odd = total(float(NORMED[n]) * line[n] for n in range(1, MODES, 2))
    even_slope = total(float(SLOPE[n]) * line[n] for n in range(2, MODES, 2))
    odd_slope = total(float(SLOPE[n]) * line[n] for n in range(1, MODES, 2))
    return even + odd, even_slope + odd_slope, even - odd, odd_slope - even_slope


def x_turn():
    return lax.axis_index("gx") + lax.axis_index("gz")


def goes_up(turn):
    return jnp.full((8, 128), lax.rem(turn, 2), jnp.int32) == 0


def has_place(axis, distance):
    place = lax.axis_index(axis) + distance
    return jnp.where((place >= 0) & (place < lax.axis_size(axis)), 1.0, 0.0).astype(jnp.float32)


def trace_kernel(
    rhs_hbm, orders_hbm, first, x_a, x_b, orders, rhs, arrived,
):
    copies = [pltpu.make_async_copy(orders_hbm, orders, arrived.at[MODES])]
    for b in range(MODES):
        copies.append(pltpu.make_async_copy(rhs_hbm.at[:, b], rhs.at[:, b], arrived.at[b]))
    for copy in copies:
        copy.start()
    pairs = Pairs()
    top = pairs.top
    upward = goes_up(x_turn())
    copies[0].wait()
    keep = keep_masks(orders[0], top)
    for b in range(MODES):
        copies[1 + b].wait()
        for e in range(MODES):
            column = []
            for i in range(PAIRS):
                upper = rhs[2 * i, b, e, 0]
                lower = rhs[2 * i + 1, b, e, 0] if 2 * i + 1 < MODES else jnp.zeros_like(upper)
                cell = jnp.concatenate([upper, lower], axis=0)
                mask = keep(max(2 * i, b, e), max(odd_of(i), b, e))
                scale = pairs.once(
                    1.0 / (THETA * diag(2 * i, b, e)), 1.0 / (THETA * diag(odd_of(i), b, e))
                )
                cell = cell * mask * scale
                first[i, b, e] = cell
                column.append(cell)
            odd = [odd_of(i) if 2 * i + 1 < MODES else None for i in range(PAIRS)]
            value = total(
                pairs(NORMED[2 * i], NORMED[odd[i]] if odd[i] else 0.0) * column[i]
                for i in range(PAIRS)
            )
            slope = total(
                pairs(SLOPE[2 * i], SLOPE[odd[i]] if odd[i] else 0.0) * column[i]
                for i in range(PAIRS)
            )
            both_value = jnp.where(top, value + swap(value), swap(value) - value)
            both_slope = jnp.where(top, slope + swap(slope), slope - swap(slope))
            up = jnp.where(top, both_value, swap(both_slope))
            down = jnp.where(top, swap(both_value), both_slope)
            x_a[b * MODES + e] = jnp.where(upward, up, down)
            x_b[b * MODES + e] = jnp.where(upward, down, up)


def side_trace_kernel(first, y_a, y_b, z_a, z_b, y_low, y_high, z_low, z_high):
    row, lane = row_in_half(), lanes()
    y_up, z_up = goes_up(lax.axis_index("gy")), goes_up(lax.axis_index("gz"))
    packed_up = packed_down = None
    for kind in range(2):
        for i in range(PAIRS):
            for e in range(MODES):
                m = i * MODES + e
                q = m % 4
                line = [first[i, b, e] for b in range(MODES)]
                traces = line_traces(line)
                high, low = traces[kind], traces[2 + kind]
                y_high[kind, m] = high
                y_low[kind, m] = low
                up, down = pltpu.roll(high, 5 + q, 0), pltpu.roll(low, q, 0) if q else low
                packed_up = up if q == 0 else jnp.where(row == q, up, packed_up)
                packed_down = down if q == 0 else jnp.where(row == q, down, packed_down)
                if q == 3:
                    k = kind * 7 + m // 4
                    y_a[k] = jnp.where(y_up, packed_up, packed_down)
                    y_b[k] = jnp.where(y_up, packed_down, packed_up)
    packed_up = packed_down = jnp.zeros((8, 128), jnp.float32)
    for i in range(PAIRS):
        for b in range(MODES):
            m = i * MODES + b
            line = [first[i, b, e] for e in range(MODES)]
            traces = line_traces(line)
            for kind in range(2):
                high, low = traces[kind], traces[2 + kind]
                z_high[kind, m] = high
                z_low[kind, m] = low
                place = 2 * m + kind
                packed_up = jnp.where(lane == place, pltpu.roll(high, 1 + place, 1), packed_up)
                down = pltpu.roll(low, place, 1) if place else low
                packed_down = jnp.where(lane == place, down, packed_down)
    z_a[...] = jnp.where(z_up, packed_up, packed_down)
    z_b[...] = jnp.where(z_up, packed_down, packed_up)


def own_kernel(first, out):
    pairs = Pairs()
    for b in range(MODES):
        for e in range(MODES):
            column = [first[i, b, e] for i in range(PAIRS)]
            for i in range(PAIRS):
                terms = []
                for j in range(PAIRS):
                    lower = OWN[2 * i + 1, 2 * j + 1] if max(i, j) < 3 else 0.0
                    terms.append(pairs(OWN[2 * i, 2 * j], lower) * column[j])
                out[i, b, e] = total(terms)
    for i in range(PAIRS):
        for b in range(MODES):
            line = [first[i, b, e] for e in range(MODES)]
            for n in range(MODES):
                out[i, b, n] += total(
                    float(OWN[n, k]) * line[k] for k in range(n % 2, MODES, 2)
                )
        for e in range(MODES):
            line = [first[i, b, e] for b in range(MODES)]
            for n in range(MODES):
                out[i, n, e] += total(
                    float(OWN[n, k]) * line[k] for k in range(n % 2, MODES, 2)
                )


def neighbour_line(low_value, low_slope, high_value, high_slope):
    plus, minus = high_value + low_value, high_value - low_value
    even = 0.5 * (low_slope - high_slope) - PENALTY * plus
    odd = -0.5 * (low_slope + high_slope) - PENALTY * minus
    return (even, 0.5 * plus), (odd, 0.5 * minus)


def vertex_pair(first_mode, second_mode):
    base, tilt = ROOT_HALF * first_mode, THIRD * second_mode
    return base - tilt, base + tilt


def sum_to_vertices(grid, pairs, row, lane):
    top = pairs.top
    rows = {}
    for (dy, dz), value in grid.items():
        rows.setdefault(dy, []).append((dz, value))
    result = [[[], []], [[], []]]
    for dy, entries in rows.items():
        inner, outer = [], []
        for dz, value in entries:
            if dz == 0:
                inner.append(value)
                continue
            moved = pltpu.roll(value, dz % 128, 1)
            inside = lane >= dz if dz > 0 else lane < 128 + dz
            inner.append(jnp.where(inside, moved, 0.0))
            outer.append(jnp.where(inside, 0.0, moved))
        for beyond, terms in ((0, inner), (1, outer)):
            if not terms:
                continue
            value = total(terms)
            if dy == 0:
                result[0][beyond].append(value)
                continue
            moved = pltpu.roll(value, dy % 8, 0)
            inside = row >= dy if dy > 0 else row < 4 + dy
            result[0][beyond].append(jnp.where(inside, moved, 0.0))
            result[1][beyond].append(jnp.where(inside, 0.0, swap(moved)))
    return [[total(result[r][z]) for z in range(2)] for r in range(2)]


def side_kernel(
    local, y_b, y_a, z_a, z_b, y_below, y_above, z_below, z_above, out
):
    row, lane = row_in_half(), lanes()
    y_even, z_even = goes_up(lax.axis_index("gy")), goes_up(lax.axis_index("gz"))
    y_has_low, y_has_high = has_place("gy", -1), has_place("gy", 1)
    z_has_low, z_has_high = has_place("gz", -1), has_place("gz", 1)
    y_low, y_high = [], []
    for k in range(FACE_ROWS):
        one, two = y_a[k], y_b[k]
        y_low.append(y_has_low * jnp.where(y_even, two, one))
        y_high.append(y_has_high * jnp.where(y_even, one, two))
    for i in range(PAIRS):
        for e in range(MODES):
            m = i * MODES + e
            q = m % 4
            seen = []
            for kind in range(2):
                halo = y_low[kind * 7 + m // 4]
                halo = pltpu.roll(halo, 8 - q, 0) if q else halo
                moved = pltpu.roll(y_below[kind, m], 1, 0)
                seen.append(jnp.where(row == 0, halo, moved))
            for kind in range(2):
                halo = y_high[kind * 7 + m // 4]
                halo = pltpu.roll(halo, 3 - q, 0) if q < 3 else halo
                moved = pltpu.roll(y_above[kind, m], 7, 0)
                seen.append(jnp.where(row == 3, halo, moved))
            parts = neighbour_line(*seen)
            for n in range(MODES):
                value, slope = parts[n % 2]
                add = float(NORMED[n]) * value
                add = add + float(SLOPE[n]) * slope if n else add
                out[i, n, e] = local[i, n, e] + add
    z_low_halo = z_has_low * jnp.where(z_even, z_b[...], z_a[...])
    z_high_halo = z_has_high * jnp.where(z_even, z_a[...], z_b[...])
    for i in range(PAIRS):
        for b in range(MODES):
            m = i * MODES + b
            seen = []
            for kind in range(2):
                place = 2 * m + kind
                halo = pltpu.roll(z_low_halo, 128 - place, 1) if place else z_low_halo
                moved = pltpu.roll(z_below[kind, m], 1, 1)
                seen.append(jnp.where(lane == 0, halo, moved))
            for kind in range(2):
                place = 2 * m + kind
                halo = pltpu.roll(z_high_halo, 127 - place, 1)
                moved = pltpu.roll(z_above[kind, m], 127, 1)
                seen.append(jnp.where(lane == 127, halo, moved))
            parts = neighbour_line(*seen)
            for e in range(MODES):
                value, slope = parts[e % 2]
                add = float(NORMED[e]) * value
                if e:
                    add = add + float(SLOPE[e]) * slope
                out[i, b, e] += add


def finish_kernel(first, local, orders, x_a, x_b, field, here, sum_a, sum_b, far):
    pairs = Pairs()
    top = pairs.top
    row, lane = row_in_half(), lanes()
    keep = keep_masks(orders[0], top)
    has_low, has_high = has_place("gx", -1), has_place("gx", 1)
    upward = goes_up(x_turn())
    one_valid = jnp.where(upward, has_high, has_low)
    two_valid = jnp.where(upward, has_low, has_high)
    x_sign = jnp.where(upward, 1.0, -1.0)
    x_even = goes_up(lax.axis_index("gx"))
    for b in range(MODES):
        for e in range(MODES):
            one, two = one_valid * x_a[b * MODES + e], two_valid * x_b[b * MODES + e]
            plus, minus = one + two, swap(x_sign * (one - two))
            slope = 0.5 * jnp.where(top, plus, minus)
            value = (-2.0 * PENALTY) * slope - 0.5 * jnp.where(top, minus, plus)
            for i in range(PAIRS):
                last = 2 * i + 1 >= MODES
                k = odd_of(i)
                applied = local[i, b, e] + (
                    pairs(NORMED[2 * i], 0.0 if last else NORMED[k]) * value
                    + pairs(SLOPE[2 * i], 0.0 if last else SLOPE[k]) * slope
                )
                one = 2.0 * RHO_SECOND / (DELTA * PENALTY)
                scale = pairs.once(one / diag(2 * i, b, e), one / diag(odd_of(i), b, e))
                mask = keep(max(2 * i, b, e), max(odd_of(i), b, e))
                kappa = 1.0 + RHO_SECOND * RHO_FIRST + 2.0 * RHO_SECOND * THETA / DELTA
                after = kappa * first[i, b, e] - (mask * scale) * applied
                field[i, b, e] = after

    grid = {}

    def add(key, value):
        grid[key] = grid[key] + value if key in grid else value

    spread = -SPREAD / PENALTY
    for e in range(MODES):
        low, high = vertex_pair(field[0, 0, e], field[0, 1, e])
        for dz in range(-1, 3):
            add((0, dz), float(spread[dz + 1, e]) * low)
            add((1, dz), float(spread[dz + 1, e]) * high)
    for b in range(MODES):
        low, high = vertex_pair(field[0, b, 0], field[0, b, 1])
        for dy in range(-1, 3):
            add((dy, 0), float(spread[dy + 1, b]) * low)
            add((dy, 1), float(spread[dy + 1, b]) * high)
    force = [
        [
            pairs.once(THETA * diag(0, b, e), THETA * diag(1, b, e)) * first[0, b, e]
            for e in range(2)
        ]
        for b in range(2)
    ]
    force = [vertex_pair(force[0][e], force[1][e]) for e in range(2)]
    for dy in range(2):
        low, high = vertex_pair(force[0][dy], force[1][dy])
        add((dy, 0), low)
        add((dy, 1), high)
    kept, turned = pairs(ROOT_HALF, THIRD), pairs(-THIRD, ROOT_HALF)
    near = {key: kept * value + turned * swap(value) for key, value in grid.items()}
    outer = {}
    corners = []
    for i in range(PAIRS):
        line = [vertex_pair(field[i, 0, e], field[i, 1, e]) for e in range(2)]
        corners.append([vertex_pair(line[0][dy], line[1][dy]) for dy in range(2)])
    for dy in range(2):
        for dz in range(2):
            sums = []
            for dx in range(-1, 3):
                part = total(
                    pairs(
                        spread[dx + 1, 2 * i],
                        spread[dx + 1, 2 * i + 1] if 2 * i + 1 < MODES else 0.0,
                    )
                    * corners[i][dy][dz]
                    for i in range(PAIRS)
                )
                sums.append(part + swap(part))
            near[dy, dz] += jnp.where(top, sums[1], sums[2])
            outer[dy, dz] = jnp.where(top, sums[0], sums[3])
    near = sum_to_vertices(near, pairs, row, lane)
    outer = sum_to_vertices(outer, pairs, row, lane)
    for z in range(2):
        here[z] = jnp.where(top, near[0][z], swap(near[1][z]))
        ahead = jnp.where(top, swap(near[0][z]), near[1][z])
        behind = jnp.where(top, outer[0][z], swap(outer[1][z]))
        sum_a[z] = jnp.where(x_even, ahead, behind)
        sum_b[z] = jnp.where(x_even, behind, ahead)
        far[z] = jnp.where(top, swap(outer[0][z]), outer[1][z])


def unpack_kernel(field, smoothed):
    for b in range(MODES):
        for e in range(MODES):
            for i in range(PAIRS):
                value = field[i, b, e]
                smoothed[2 * i, b, e, 0] = value[:4]
                if 2 * i + 1 < MODES:
                    smoothed[2 * i + 1, b, e, 0] = value[4:]


def column_kernel(chip, fetched, mated, third, column, blocks):
    count = lax.axis_size("gz")
    me = lax.axis_index("gz")
    core, place = lax.rem(me, 2), lax.div(me, 2)
    beside = place + 1 - 2 * lax.rem(place, 2)
    across = lax.rem(place + 2, 4)
    asked = beside + core * (across - beside)
    zero = jnp.zeros((8, 128), jnp.float32)
    blocks[0] = zero
    blocks[count + 1] = zero
    for source, sender, pair in (
        (place, core, chip),
        (asked, core, fetched),
        (beside + across - asked, 1 - core, mated),
        (3 - place, core, third),
    ):
        blocks[2 * source + sender + 1] = pair[0]
        blocks[2 * source + 2 - sender] = pair[1]
    lane = lax.broadcasted_iota(jnp.int32, (4, 128), 1)
    row = lax.broadcasted_iota(jnp.int32, (4, 128), 0)
    interior = (lax.axis_index("gx") > 0) & (lax.axis_index("gy") * 4 + row > 0)
    for k in range(count):
        value = (
            blocks[k + 1, :4]
            + jnp.where(lane < 2, blocks[k, 4:], 0.0)
            + jnp.where(lane == 127, blocks[k + 2, 4:], 0.0)
        )
        here = interior & (lane > 0) if k == 0 else interior
        column[0, :, k * 128 : (k + 1) * 128] = jnp.where(here, value, 0.0)


def shape(*dims):
    return jax.ShapeDtypeStruct(dims, jnp.float32)


def in_vmem(count):
    return [pl.BlockSpec(memory_space=pltpu.VMEM)] * count


def call(kernel, name, inputs, outputs, flops, scratch=(), in_hbm=False):
    size = sum(4 * int(np.prod(v.shape)) for v in (*inputs, *outputs))
    space = pltpu.HBM if in_hbm else pltpu.VMEM
    return pl.pallas_call(
        kernel,
        out_shape=outputs,
        in_specs=[pl.BlockSpec(memory_space=space)] * len(inputs),
        out_specs=[pl.BlockSpec(memory_space=pltpu.VMEM)] * len(outputs),
        scratch_shapes=list(scratch),
        name=name,
        cost_estimate=pl.CostEstimate(flops=flops, bytes_accessed=size, transcendentals=0),
        compiler_params=pltpu.CompilerParams(vmem_limit_bytes=24 * 1024 * 1024),
    )(*inputs)


def flip(value, axis, bits):
    return lax.ppermute(value, axis, [(i, i ^ bits) for i in range(lax.axis_size(axis))])


def exchange(value, partner):
    axes = ("gx", "gy", "gz")
    sizes = [lax.axis_size(name) for name in axes]
    route = [
        (source, int(np.ravel_multi_index(partner(list(place)), sizes)))
        for source, place in enumerate(np.ndindex(*sizes))
    ]
    return lax.ppermute(value, axes, route)


def second_of_pair(place, k, count, spare, bit):
    if place[k] in (0, count - 1):
        place[spare] ^= bit
    else:
        place[k] += 1 if place[k] % 2 else -1
    return place


def second_pairs(value, axis):
    k, count = ("gx", "gy", "gz").index(axis), lax.axis_size(axis)
    return exchange(value, lambda place: second_of_pair(place, k, count, 0 if k == 2 else 2, 1))


def x_pairs(value, turn):
    count = lax.axis_size("gx")

    def partner(place):
        if place[2] % 2 == turn:
            place[0] ^= 1
            return place
        return second_of_pair(place, 0, count, 1, 1)

    return exchange(value, partner)


def both_y_sides(value):
    count = lax.axis_size("gy")

    def partner(place):
        if place[2] % 2:
            return second_of_pair(place, 1, count, 0, 1)
        place[1] ^= 1
        return place

    return exchange(value, partner)


def two_chips(value):
    def partner(place):
        place[2] ^= 4 if place[2] % 2 else 2
        return place

    return exchange(value, partner)


def inside(axis, distance):
    place = lax.axis_index(axis) + distance
    return ((place >= 0) & (place < lax.axis_size(axis))).astype(jnp.float32)


def per_device(rhs, orders):
    cells = (PAIRS, MODES, MODES, 8, 128)
    sides = (shape(2, 28, 8, 128),) * 4
    first, x_a, x_b, held = call(
        trace_kernel,
        "x_traces",
        tuple(pltpu.with_memory_space_constraint(v, pltpu.HBM) for v in (rhs, orders)),
        (
            shape(*cells), shape(49, 8, 128), shape(49, 8, 128),
            jax.ShapeDtypeStruct(orders.shape, jnp.int32),
        ),
        4_000_000,
        scratch=(pltpu.VMEM(rhs.shape, jnp.float32), pltpu.SemaphoreType.DMA((MODES + 1,))),
        in_hbm=True,
    )
    x_a, x_b = x_pairs(x_a, 0), x_pairs(x_b, 1)
    y_a, y_b, z_a, z_b, y_low, y_high, z_low, z_high = call(
        side_trace_kernel,
        "side_traces",
        (first,),
        (shape(FACE_ROWS, 8, 128),) * 2 + (shape(8, 128),) * 2 + sides,
        SIDE_COST,
    )
    y_b = second_pairs(y_b, "gy")
    y_a = flip(y_a, "gy", 1)
    z_a, z_b = flip(z_a, "gz", 1), second_pairs(z_b, "gz")
    (local,) = call(own_kernel, "own_cells", (first,), (shape(*cells),), OWN_COST)
    (local,) = call(
        side_kernel,
        "side_halo",
        (local, y_b, y_a, z_a, z_b, y_high, y_low, z_high, z_low),
        (shape(*cells),),
        HALO_COST,
    )
    field, here, sum_a, sum_b, far = call(
        finish_kernel,
        "smooth_and_restrict",
        (first, local, held, x_a, x_b),
        (shape(*cells),) + (shape(2, 8, 128),) * 4,
        5_000_000,
    )
    (smoothed,) = call(unpack_kernel, "unpack_modes", (field,), (shape(*rhs.shape),), 200_000)
    from_far = flip(far, "gx", 2)
    from_a = flip(sum_a, "gx", 1)
    from_b = second_pairs(sum_b, "gx")
    sums = (
        here
        + inside("gx", -2) * from_far
        + from_a
        + inside("gx", -1) * inside("gx", 1) * from_b
    )
    count = lax.axis_size("gz")
    chip = jnp.stack([sums, flip(sums, "gz", 1)])
    from_beside = both_y_sides(chip)
    from_low = (lax.axis_index("gy") + lax.axis_index("gz")) % 2 == 1
    row = lax.broadcasted_iota(jnp.int32, (1, 1, 4, 1), 2)
    wanted = jnp.where(from_low, row < 2, row == 3)
    valid = jnp.where(from_low, inside("gy", -1), inside("gy", 1))
    edges = jnp.where(wanted, from_beside[:, :, 4:], 0.0) * valid
    edges = edges.reshape(2, 8, 128)
    mated = flip(edges, "gz", 1)
    owned = chip[:, :, :4].reshape(2, 8, 128) + edges + mated[::-1]
    fetched = two_chips(owned)
    third = flip(owned, "gz", 6)
    (column,) = call(
        column_kernel,
        "column",
        (owned, fetched, flip(fetched, "gz", 1), third),
        (shape(1, 4, 128 * count),),
        20_000,
        scratch=(pltpu.VMEM((count + 2, 8, 128), jnp.float32),),
    )
    return smoothed, column


def solution(mesh):
    return jax.shard_map(
        per_device,
        mesh=mesh,
        in_specs=(P(None, None, None, "gx", "gy", "gz"), P("gx", "gy", "gz")),
        out_specs=(P(None, None, None, "gx", "gy", "gz"), P("gx", "gy", None)),
        check_vma=False,
    )
```

```python
import jax
import jax.numpy as jnp
import numpy as np
from jax import lax
from jax.experimental import pallas as pl
from jax.experimental.pallas import tpu as pltpu
from jax.sharding import PartitionSpec as P

PENALTY = 49.0
EIGEN_HIGH = 2.4
EIGEN_LOW = 0.24
THETA = 0.5 * (EIGEN_HIGH + EIGEN_LOW)
DELTA = 0.5 * (EIGEN_HIGH - EIGEN_LOW)
RHO_FIRST = DELTA / THETA
RHO_SECOND = 1.0 / (2.0 * THETA / DELTA - RHO_FIRST)
MODES = 7
PAIRS = 4
FACE_ROWS = 14
SIDE_COST = 4_000_000
OWN_COST = 1_400_000_000
HALO_COST = 4_000_000


def basis_tables():
    degree = np.arange(MODES)
    normed = np.sqrt((2.0 * degree + 1.0) / 2.0)
    smaller = np.minimum(degree[:, None], degree[None, :])
    parity = (degree[:, None] + degree[None, :]) % 2 == 0
    stiffness = np.where(parity, normed[:, None] * normed[None, :] * smaller * (smaller + 1), 0.0)
    signs = (-1.0) ** degree
    slope = normed * degree * (degree + 1) / 2.0
    high, high_slope = normed, slope
    low, low_slope = normed * signs, -slope * signs
    own = (
        stiffness
        + PENALTY * (np.outer(high, high) + np.outer(low, low))
        - 0.5 * (np.outer(high, high_slope) + np.outer(high_slope, high))
        + 0.5 * (np.outer(low, low_slope) + np.outer(low_slope, low))
    )
    own = np.where(parity, own, 0.0)
    to_next = np.outer(low, 0.5 * high_slope - PENALTY * high) - 0.5 * np.outer(low_slope, high)
    to_last = np.outer(high, -PENALTY * low - 0.5 * low_slope) + 0.5 * np.outer(high_slope, low)
    one_axis = normed * normed * degree * (degree + 1) + 2.0 * (
        PENALTY * normed * normed - normed * slope
    )
    third = np.sqrt(1.5) / 3.0
    vertex = np.zeros((MODES, 2))
    vertex[0] = np.sqrt(0.5)
    vertex[1] = -third, third
    spread = np.stack(
        [
            vertex[:, 0] @ to_last,
            vertex[:, 1] @ to_last + vertex[:, 0] @ own,
            vertex[:, 1] @ own + vertex[:, 0] @ to_next,
            vertex[:, 1] @ to_next,
        ]
    )
    return normed, slope, own, one_axis, spread, third


NORMED, SLOPE, OWN, ONE_AXIS, SPREAD, THIRD = basis_tables()
ROOT_HALF = float(np.sqrt(0.5))


def diag(a, b, e):
    return float((ONE_AXIS[a] + ONE_AXIS[b] + ONE_AXIS[e]) / PENALTY)


def half_mask():
    return lax.broadcasted_iota(jnp.int32, (8, 128), 0) < 4


def row_in_half():
    return lax.broadcasted_iota(jnp.int32, (8, 128), 0) % 4


def lanes():
    return lax.broadcasted_iota(jnp.int32, (8, 128), 1)


def swap(value):
    return pltpu.roll(value, 4, 0)


class Pairs:
    def __init__(self):
        self.top = half_mask()
        self.known = {}

    def __call__(self, upper, lower):
        key = (float(upper), float(lower))
        if key[0] == key[1]:
            return jnp.float32(key[0])
        if key not in self.known:
            self.known[key] = jnp.where(self.top, jnp.float32(key[0]), jnp.float32(key[1]))
        return self.known[key]

    def once(self, upper, lower):
        if float(upper) == float(lower):
            return jnp.float32(upper)
        return jnp.where(self.top, jnp.float32(upper), jnp.float32(lower))


def total(terms):
    terms = list(terms)
    while len(terms) > 1:
        terms = [
            terms[k] + terms[k + 1] if k + 1 < len(terms) else terms[k]
            for k in range(0, len(terms), 2)
        ]
    return terms[0]


def keep_masks(orders, top):
    both = jnp.concatenate([orders, orders], axis=0)
    known = {}

    def get(upper, lower):
        if (upper, lower) not in known:
            if upper == lower:
                bound = jnp.int32(upper)
            else:
                bound = jnp.where(top, jnp.int32(upper), jnp.int32(lower))
            known[upper, lower] = (both >= bound).astype(jnp.float32)
        return known[upper, lower]

    return get


def odd_of(pair):
    return min(2 * pair + 1, MODES - 1)


def line_traces(line):
    even = total(float(NORMED[n]) * line[n] for n in range(0, MODES, 2))
    odd = total(float(NORMED[n]) * line[n] for n in range(1, MODES, 2))
    even_slope = total(float(SLOPE[n]) * line[n] for n in range(2, MODES, 2))
    odd_slope = total(float(SLOPE[n]) * line[n] for n in range(1, MODES, 2))
    return even + odd, even_slope + odd_slope, even - odd, odd_slope - even_slope


def x_turn():
    return lax.axis_index("gx") + lax.axis_index("gz")


def goes_up(turn):
    return jnp.full((8, 128), lax.rem(turn, 2), jnp.int32) == 0


def has_place(axis, distance):
    place = lax.axis_index(axis) + distance
    return jnp.where((place >= 0) & (place < lax.axis_size(axis)), 1.0, 0.0).astype(jnp.float32)


def trace_kernel(
    rhs_hbm, orders_hbm, first, x_a, x_b, orders, rhs, arrived,
):
    copies = [pltpu.make_async_copy(orders_hbm, orders, arrived.at[MODES])]
    for b in range(MODES):
        copies.append(pltpu.make_async_copy(rhs_hbm.at[:, b], rhs.at[:, b], arrived.at[b]))
    for copy in copies:
        copy.start()
    pairs = Pairs()
    top = pairs.top
    upward = goes_up(x_turn())
    copies[0].wait()
    keep = keep_masks(orders[0], top)
    for b in range(MODES):
        copies[1 + b].wait()
        for e in range(MODES):
            column = []
            for i in range(PAIRS):
                upper = rhs[2 * i, b, e, 0]
                lower = rhs[2 * i + 1, b, e, 0] if 2 * i + 1 < MODES else jnp.zeros_like(upper)
                cell = jnp.concatenate([upper, lower], axis=0)
                mask = keep(max(2 * i, b, e), max(odd_of(i), b, e))
                scale = pairs.once(
                    1.0 / (THETA * diag(2 * i, b, e)), 1.0 / (THETA * diag(odd_of(i), b, e))
                )
                cell = cell * mask * scale
                first[i, b, e] = cell
                column.append(cell)
            odd = [odd_of(i) if 2 * i + 1 < MODES else None for i in range(PAIRS)]
            value = total(
                pairs(NORMED[2 * i], NORMED[odd[i]] if odd[i] else 0.0) * column[i]
                for i in range(PAIRS)
            )
            slope = total(
                pairs(SLOPE[2 * i], SLOPE[odd[i]] if odd[i] else 0.0) * column[i]
                for i in range(PAIRS)
            )
            both_value = jnp.where(top, value + swap(value), swap(value) - value)
            both_slope = jnp.where(top, slope + swap(slope), slope - swap(slope))
            up = jnp.where(top, both_value, swap(both_slope))
            down = jnp.where(top, swap(both_value), both_slope)
            x_a[b * MODES + e] = jnp.where(upward, up, down)
            x_b[b * MODES + e] = jnp.where(upward, down, up)


def side_trace_kernel(first, y_a, y_b, z_a, z_b, y_low, y_high, z_low, z_high):
    row, lane = row_in_half(), lanes()
    y_up, z_up = goes_up(lax.axis_index("gy")), goes_up(lax.axis_index("gz"))
    packed_up = packed_down = None
    for kind in range(2):
        for i in range(PAIRS):
            for e in range(MODES):
                m = i * MODES + e
                q = m % 4
                line = [first[i, b, e] for b in range(MODES)]
                traces = line_traces(line)
                high, low = traces[kind], traces[2 + kind]
                y_high[kind, m] = high
                y_low[kind, m] = low
                up, down = pltpu.roll(high, 5 + q, 0), pltpu.roll(low, q, 0) if q else low
                packed_up = up if q == 0 else jnp.where(row == q, up, packed_up)
                packed_down = down if q == 0 else jnp.where(row == q, down, packed_down)
                if q == 3:
                    k = kind * 7 + m // 4
                    y_a[k] = jnp.where(y_up, packed_up, packed_down)
                    y_b[k] = jnp.where(y_up, packed_down, packed_up)
    packed_up = packed_down = jnp.zeros((8, 128), jnp.float32)
    for i in range(PAIRS):
        for b in range(MODES):
            m = i * MODES + b
            line = [first[i, b, e] for e in range(MODES)]
            traces = line_traces(line)
            for kind in range(2):
                high, low = traces[kind], traces[2 + kind]
                z_high[kind, m] = high
                z_low[kind, m] = low
                place = 2 * m + kind
                packed_up = jnp.where(lane == place, pltpu.roll(high, 1 + place, 1), packed_up)
                down = pltpu.roll(low, place, 1) if place else low
                packed_down = jnp.where(lane == place, down, packed_down)
    z_a[...] = jnp.where(z_up, packed_up, packed_down)
    z_b[...] = jnp.where(z_up, packed_down, packed_up)


def own_kernel(first, out):
    pairs = Pairs()
    for b in range(MODES):
        for e in range(MODES):
            column = [first[i, b, e] for i in range(PAIRS)]
            for i in range(PAIRS):
                terms = []
                for j in range(PAIRS):
                    lower = OWN[2 * i + 1, 2 * j + 1] if max(i, j) < 3 else 0.0
                    terms.append(pairs(OWN[2 * i, 2 * j], lower) * column[j])
                out[i, b, e] = total(terms)
    for i in range(PAIRS):
        for b in range(MODES):
            line = [first[i, b, e] for e in range(MODES)]
            for n in range(MODES):
                out[i, b, n] += total(
                    float(OWN[n, k]) * line[k] for k in range(n % 2, MODES, 2)
                )
        for e in range(MODES):
            line = [first[i, b, e] for b in range(MODES)]
            for n in range(MODES):
                out[i, n, e] += total(
                    float(OWN[n, k]) * line[k] for k in range(n % 2, MODES, 2)
                )


def neighbour_line(low_value, low_slope, high_value, high_slope):
    plus, minus = high_value + low_value, high_value - low_value
    even = 0.5 * (low_slope - high_slope) - PENALTY * plus
    odd = -0.5 * (low_slope + high_slope) - PENALTY * minus
    return (even, 0.5 * plus), (odd, 0.5 * minus)


def vertex_pair(first_mode, second_mode):
    base, tilt = ROOT_HALF * first_mode, THIRD * second_mode
    return base - tilt, base + tilt


def sum_to_vertices(grid, pairs, row, lane):
    top = pairs.top
    rows = {}
    for (dy, dz), value in grid.items():
        rows.setdefault(dy, []).append((dz, value))
    result = [[[], []], [[], []]]
    for dy, entries in rows.items():
        inner, outer = [], []
        for dz, value in entries:
            if dz == 0:
                inner.append(value)
                continue
            moved = pltpu.roll(value, dz % 128, 1)
            inside = lane >= dz if dz > 0 else lane < 128 + dz
            inner.append(jnp.where(inside, moved, 0.0))
            outer.append(jnp.where(inside, 0.0, moved))
        for beyond, terms in ((0, inner), (1, outer)):
            if not terms:
                continue
            value = total(terms)
            if dy == 0:
                result[0][beyond].append(value)
                continue
            moved = pltpu.roll(value, dy % 8, 0)
            inside = row >= dy if dy > 0 else row < 4 + dy
            result[0][beyond].append(jnp.where(inside, moved, 0.0))
            result[1][beyond].append(jnp.where(inside, 0.0, swap(moved)))
    return [[total(result[r][z]) for z in range(2)] for r in range(2)]


def side_kernel(
    local, y_a, y_b, z_a, z_b, y_below, y_above, z_below, z_above, out
):
    row, lane = row_in_half(), lanes()
    y_even, z_even = goes_up(lax.axis_index("gy")), goes_up(lax.axis_index("gz"))
    y_has_low, y_has_high = has_place("gy", -1), has_place("gy", 1)
    z_has_low, z_has_high = has_place("gz", -1), has_place("gz", 1)
    y_low, y_high = [], []
    for k in range(FACE_ROWS):
        one, two = y_a[k], y_b[k]
        y_low.append(y_has_low * jnp.where(y_even, two, one))
        y_high.append(y_has_high * jnp.where(y_even, one, two))
    for i in range(PAIRS):
        for e in range(MODES):
            m = i * MODES + e
            q = m % 4
            seen = []
            for kind in range(2):
                halo = y_low[kind * 7 + m // 4]
                halo = pltpu.roll(halo, 8 - q, 0) if q else halo
                moved = pltpu.roll(y_below[kind, m], 1, 0)
                seen.append(jnp.where(row == 0, halo, moved))
            for kind in range(2):
                halo = y_high[kind * 7 + m // 4]
                halo = pltpu.roll(halo, 3 - q, 0) if q < 3 else halo
                moved = pltpu.roll(y_above[kind, m], 7, 0)
                seen.append(jnp.where(row == 3, halo, moved))
            parts = neighbour_line(*seen)
            for n in range(MODES):
                value, slope = parts[n % 2]
                add = float(NORMED[n]) * value
                add = add + float(SLOPE[n]) * slope if n else add
                out[i, n, e] = local[i, n, e] + add
    z_low_halo = z_has_low * jnp.where(z_even, z_b[...], z_a[...])
    z_high_halo = z_has_high * jnp.where(z_even, z_a[...], z_b[...])
    for i in range(PAIRS):
        for b in range(MODES):
            m = i * MODES + b
            seen = []
            for kind in range(2):
                place = 2 * m + kind
                halo = pltpu.roll(z_low_halo, 128 - place, 1) if place else z_low_halo
                moved = pltpu.roll(z_below[kind, m], 1, 1)
                seen.append(jnp.where(lane == 0, halo, moved))
            for kind in range(2):
                place = 2 * m + kind
                halo = pltpu.roll(z_high_halo, 127 - place, 1)
                moved = pltpu.roll(z_above[kind, m], 127, 1)
                seen.append(jnp.where(lane == 127, halo, moved))
            parts = neighbour_line(*seen)
            for e in range(MODES):
                value, slope = parts[e % 2]
                add = float(NORMED[e]) * value
                if e:
                    add = add + float(SLOPE[e]) * slope
                out[i, b, e] += add


def finish_kernel(first, local, orders, x_a, x_b, field, here, sum_a, sum_b, far):
    pairs = Pairs()
    top = pairs.top
    row, lane = row_in_half(), lanes()
    keep = keep_masks(orders[0], top)
    has_low, has_high = has_place("gx", -1), has_place("gx", 1)
    upward = goes_up(x_turn())
    one_valid = jnp.where(upward, has_high, has_low)
    two_valid = jnp.where(upward, has_low, has_high)
    x_sign = jnp.where(upward, 1.0, -1.0)
    x_even = goes_up(lax.axis_index("gx"))
    for b in range(MODES):
        for e in range(MODES):
            one, two = one_valid * x_a[b * MODES + e], two_valid * x_b[b * MODES + e]
            plus, minus = one + two, swap(x_sign * (one - two))
            slope = 0.5 * jnp.where(top, plus, minus)
            value = (-2.0 * PENALTY) * slope - 0.5 * jnp.where(top, minus, plus)
            for i in range(PAIRS):
                last = 2 * i + 1 >= MODES
                k = odd_of(i)
                applied = local[i, b, e] + (
                    pairs(NORMED[2 * i], 0.0 if last else NORMED[k]) * value
                    + pairs(SLOPE[2 * i], 0.0 if last else SLOPE[k]) * slope
                )
                one = 2.0 * RHO_SECOND / (DELTA * PENALTY)
                scale = pairs.once(one / diag(2 * i, b, e), one / diag(odd_of(i), b, e))
                mask = keep(max(2 * i, b, e), max(odd_of(i), b, e))
                kappa = 1.0 + RHO_SECOND * RHO_FIRST + 2.0 * RHO_SECOND * THETA / DELTA
                after = kappa * first[i, b, e] - (mask * scale) * applied
                field[i, b, e] = after

    grid = {}

    def add(key, value):
        grid[key] = grid[key] + value if key in grid else value

    spread = -SPREAD / PENALTY
    for e in range(MODES):
        low, high = vertex_pair(field[0, 0, e], field[0, 1, e])
        for dz in range(-1, 3):
            add((0, dz), float(spread[dz + 1, e]) * low)
            add((1, dz), float(spread[dz + 1, e]) * high)
    for b in range(MODES):
        low, high = vertex_pair(field[0, b, 0], field[0, b, 1])
        for dy in range(-1, 3):
            add((dy, 0), float(spread[dy + 1, b]) * low)
            add((dy, 1), float(spread[dy + 1, b]) * high)
    force = [
        [
            pairs.once(THETA * diag(0, b, e), THETA * diag(1, b, e)) * first[0, b, e]
            for e in range(2)
        ]
        for b in range(2)
    ]
    force = [vertex_pair(force[0][e], force[1][e]) for e in range(2)]
    for dy in range(2):
        low, high = vertex_pair(force[0][dy], force[1][dy])
        add((dy, 0), low)
        add((dy, 1), high)
    kept, turned = pairs(ROOT_HALF, THIRD), pairs(-THIRD, ROOT_HALF)
    near = {key: kept * value + turned * swap(value) for key, value in grid.items()}
    outer = {}
    corners = []
    for i in range(PAIRS):
        line = [vertex_pair(field[i, 0, e], field[i, 1, e]) for e in range(2)]
        corners.append([vertex_pair(line[0][dy], line[1][dy]) for dy in range(2)])
    for dy in range(2):
        for dz in range(2):
            sums = []
            for dx in range(-1, 3):
                part = total(
                    pairs(
                        spread[dx + 1, 2 * i],
                        spread[dx + 1, 2 * i + 1] if 2 * i + 1 < MODES else 0.0,
                    )
                    * corners[i][dy][dz]
                    for i in range(PAIRS)
                )
                sums.append(part + swap(part))
            near[dy, dz] += jnp.where(top, sums[1], sums[2])
            outer[dy, dz] = jnp.where(top, sums[0], sums[3])
    near = sum_to_vertices(near, pairs, row, lane)
    outer = sum_to_vertices(outer, pairs, row, lane)
    for z in range(2):
        here[z] = jnp.where(top, near[0][z], swap(near[1][z]))
        ahead = jnp.where(top, swap(near[0][z]), near[1][z])
        behind = jnp.where(top, outer[0][z], swap(outer[1][z]))
        sum_a[z] = jnp.where(x_even, ahead, behind)
        sum_b[z] = jnp.where(x_even, behind, ahead)
        far[z] = jnp.where(top, swap(outer[0][z]), outer[1][z])


def unpack_kernel(field, here, smoothed, here_again):
    here_again[...] = here[...]
    for b in range(MODES):
        for e in range(MODES):
            for i in range(PAIRS):
                value = field[i, b, e]
                smoothed[2 * i, b, e, 0] = value[:4]
                if 2 * i + 1 < MODES:
                    smoothed[2 * i + 1, b, e, 0] = value[4:]


def column_kernel(chip, fetched, mated, third, column, blocks):
    count = lax.axis_size("gz")
    me = lax.axis_index("gz")
    core, place = lax.rem(me, 2), lax.div(me, 2)
    beside = place + 1 - 2 * lax.rem(place, 2)
    across = lax.rem(place + 2, 4)
    asked = beside + core * (across - beside)
    zero = jnp.zeros((8, 128), jnp.float32)
    blocks[0] = zero
    blocks[count + 1] = zero
    for source, sender, pair in (
        (place, core, chip),
        (asked, core, fetched),
        (beside + across - asked, 1 - core, mated),
        (3 - place, core, third),
    ):
        blocks[2 * source + sender + 1] = pair[0]
        blocks[2 * source + 2 - sender] = pair[1]
    lane = lax.broadcasted_iota(jnp.int32, (4, 128), 1)
    row = lax.broadcasted_iota(jnp.int32, (4, 128), 0)
    interior = (lax.axis_index("gx") > 0) & (lax.axis_index("gy") * 4 + row > 0)
    for k in range(count):
        value = (
            blocks[k + 1, :4]
            + jnp.where(lane < 2, blocks[k, 4:], 0.0)
            + jnp.where(lane == 127, blocks[k + 2, 4:], 0.0)
        )
        here = interior & (lane > 0) if k == 0 else interior
        column[0, :, k * 128 : (k + 1) * 128] = jnp.where(here, value, 0.0)


def shape(*dims):
    return jax.ShapeDtypeStruct(dims, jnp.float32)


def in_vmem(count):
    return [pl.BlockSpec(memory_space=pltpu.VMEM)] * count


def call(kernel, name, inputs, outputs, flops, scratch=(), in_hbm=False):
    size = sum(4 * int(np.prod(v.shape)) for v in (*inputs, *outputs))
    space = pltpu.HBM if in_hbm else pltpu.VMEM
    return pl.pallas_call(
        kernel,
        out_shape=outputs,
        in_specs=[pl.BlockSpec(memory_space=space)] * len(inputs),
        out_specs=[pl.BlockSpec(memory_space=pltpu.VMEM)] * len(outputs),
        scratch_shapes=list(scratch),
        name=name,
        cost_estimate=pl.CostEstimate(flops=flops, bytes_accessed=size, transcendentals=0),
        compiler_params=pltpu.CompilerParams(vmem_limit_bytes=24 * 1024 * 1024),
    )(*inputs)


def flip(value, axis, bits):
    return lax.ppermute(value, axis, [(i, i ^ bits) for i in range(lax.axis_size(axis))])


def exchange(value, partner):
    axes = ("gx", "gy", "gz")
    sizes = [lax.axis_size(name) for name in axes]
    route = [
        (source, int(np.ravel_multi_index(partner(list(place)), sizes)))
        for source, place in enumerate(np.ndindex(*sizes))
    ]
    return lax.ppermute(value, axes, route)


def second_of_pair(place, k, count, spare, bit):
    if place[k] in (0, count - 1):
        place[spare] ^= bit
    else:
        place[k] += 1 if place[k] % 2 else -1
    return place


def second_pairs(value, axis):
    k, count = ("gx", "gy", "gz").index(axis), lax.axis_size(axis)
    return exchange(value, lambda place: second_of_pair(place, k, count, 0 if k == 2 else 2, 1))


def x_pairs(value, turn):
    count = lax.axis_size("gx")

    def partner(place):
        if place[2] % 2 == turn:
            place[0] ^= 1
            return place
        return second_of_pair(place, 0, count, 1, 1)

    return exchange(value, partner)


def both_y_sides(value):
    count = lax.axis_size("gy")

    def partner(place):
        if place[2] % 2:
            return second_of_pair(place, 1, count, 0, 1)
        place[1] ^= 1
        return place

    return exchange(value, partner)


def two_chips(value):
    def partner(place):
        place[2] ^= 4 if place[2] % 2 else 2
        return place

    return exchange(value, partner)


def inside(axis, distance):
    place = lax.axis_index(axis) + distance
    return ((place >= 0) & (place < lax.axis_size(axis))).astype(jnp.float32)


def per_device(rhs, orders):
    cells = (PAIRS, MODES, MODES, 8, 128)
    sides = (shape(2, 28, 8, 128),) * 4
    first, x_a, x_b, held = call(
        trace_kernel,
        "x_traces",
        tuple(pltpu.with_memory_space_constraint(v, pltpu.HBM) for v in (rhs, orders)),
        (
            shape(*cells), shape(49, 8, 128), shape(49, 8, 128),
            jax.ShapeDtypeStruct(orders.shape, jnp.int32),
        ),
        4_000_000,
        scratch=(pltpu.VMEM(rhs.shape, jnp.float32), pltpu.SemaphoreType.DMA((MODES + 1,))),
        in_hbm=True,
    )
    x_a, x_b = x_pairs(x_a, 0), x_pairs(x_b, 1)
    y_a, y_b, z_a, z_b, y_low, y_high, z_low, z_high = call(
        side_trace_kernel,
        "side_traces",
        (first,),
        (shape(FACE_ROWS, 8, 128),) * 2 + (shape(8, 128),) * 2 + sides,
        SIDE_COST,
    )
    y_a, y_b = flip(y_a, "gy", 1), second_pairs(y_b, "gy")
    z_a, z_b = flip(z_a, "gz", 1), second_pairs(z_b, "gz")
    (local,) = call(own_kernel, "own_cells", (first,), (shape(*cells),), OWN_COST)
    (local,) = call(
        side_kernel,
        "side_halo",
        (local, y_a, y_b, z_a, z_b, y_high, y_low, z_high, z_low),
        (shape(*cells),),
        HALO_COST,
    )
    field, here, sum_a, sum_b, far = call(
        finish_kernel,
        "smooth_and_restrict",
        (first, local, held, x_a, x_b),
        (shape(*cells),) + (shape(2, 8, 128),) * 4,
        5_000_000,
    )
    smoothed, here = call(
        unpack_kernel,
        "unpack_modes",
        (field, here),
        (shape(*rhs.shape), shape(2, 8, 128)),
        200_000,
    )
    from_far = flip(far, "gx", 2)
    from_a = flip(sum_a, "gx", 1)
    from_b = second_pairs(sum_b, "gx")
    sums = (
        here
        + inside("gx", -2) * from_far
        + from_a
        + inside("gx", -1) * inside("gx", 1) * from_b
    )
    count = lax.axis_size("gz")
    chip = jnp.stack([sums, flip(sums, "gz", 1)])
    from_beside = both_y_sides(chip)
    from_low = (lax.axis_index("gy") + lax.axis_index("gz")) % 2 == 1
    row = lax.broadcasted_iota(jnp.int32, (1, 1, 4, 1), 2)
    wanted = jnp.where(from_low, row < 2, row == 3)
    valid = jnp.where(from_low, inside("gy", -1), inside("gy", 1))
    edges = jnp.where(wanted, from_beside[:, :, 4:], 0.0) * valid
    edges = edges.reshape(2, 8, 128)
    mated = flip(edges, "gz", 1)
    owned = chip[:, :, :4].reshape(2, 8, 128) + edges + mated[::-1]
    fetched = two_chips(owned)
    third = flip(owned, "gz", 6)
    (column,) = call(
        column_kernel,
        "column",
        (owned, fetched, flip(fetched, "gz", 1), third),
        (shape(1, 4, 128 * count),),
        20_000,
        scratch=(pltpu.VMEM((count + 2, 8, 128), jnp.float32),),
    )
    return smoothed, column


def solution(mesh):
    return jax.shard_map(
        per_device,
        mesh=mesh,
        in_specs=(P(None, None, None, "gx", "gy", "gz"), P("gx", "gy", "gz")),
        out_specs=(P(None, None, None, "gx", "gy", "gz"), P("gx", "gy", None)),
        check_vma=False,
    )
```

```python
import jax
import jax.numpy as jnp
import numpy as np
from jax import lax
from jax.experimental import pallas as pl
from jax.experimental.pallas import tpu as pltpu
from jax.sharding import PartitionSpec as P

PENALTY = 49.0
EIGEN_HIGH = 2.4
EIGEN_LOW = 0.24
THETA = 0.5 * (EIGEN_HIGH + EIGEN_LOW)
DELTA = 0.5 * (EIGEN_HIGH - EIGEN_LOW)
RHO_FIRST = DELTA / THETA
RHO_SECOND = 1.0 / (2.0 * THETA / DELTA - RHO_FIRST)
MODES = 7
PAIRS = 4
FACE_ROWS = 14
SIDE_COST = 4_000_000
OWN_COST = 1_400_000_000
HALO_COST = 4_000_000


def basis_tables():
    degree = np.arange(MODES)
    normed = np.sqrt((2.0 * degree + 1.0) / 2.0)
    smaller = np.minimum(degree[:, None], degree[None, :])
    parity = (degree[:, None] + degree[None, :]) % 2 == 0
    stiffness = np.where(parity, normed[:, None] * normed[None, :] * smaller * (smaller + 1), 0.0)
    signs = (-1.0) ** degree
    slope = normed * degree * (degree + 1) / 2.0
    high, high_slope = normed, slope
    low, low_slope = normed * signs, -slope * signs
    own = (
        stiffness
        + PENALTY * (np.outer(high, high) + np.outer(low, low))
        - 0.5 * (np.outer(high, high_slope) + np.outer(high_slope, high))
        + 0.5 * (np.outer(low, low_slope) + np.outer(low_slope, low))
    )
    own = np.where(parity, own, 0.0)
    to_next = np.outer(low, 0.5 * high_slope - PENALTY * high) - 0.5 * np.outer(low_slope, high)
    to_last = np.outer(high, -PENALTY * low - 0.5 * low_slope) + 0.5 * np.outer(high_slope, low)
    one_axis = normed * normed * degree * (degree + 1) + 2.0 * (
        PENALTY * normed * normed - normed * slope
    )
    third = np.sqrt(1.5) / 3.0
    vertex = np.zeros((MODES, 2))
    vertex[0] = np.sqrt(0.5)
    vertex[1] = -third, third
    spread = np.stack(
        [
            vertex[:, 0] @ to_last,
            vertex[:, 1] @ to_last + vertex[:, 0] @ own,
            vertex[:, 1] @ own + vertex[:, 0] @ to_next,
            vertex[:, 1] @ to_next,
        ]
    )
    return normed, slope, own, one_axis, spread, third


NORMED, SLOPE, OWN, ONE_AXIS, SPREAD, THIRD = basis_tables()
ROOT_HALF = float(np.sqrt(0.5))


def diag(a, b, e):
    return float((ONE_AXIS[a] + ONE_AXIS[b] + ONE_AXIS[e]) / PENALTY)


def half_mask():
    return lax.broadcasted_iota(jnp.int32, (8, 128), 0) < 4


def row_in_half():
    return lax.broadcasted_iota(jnp.int32, (8, 128), 0) % 4


def lanes():
    return lax.broadcasted_iota(jnp.int32, (8, 128), 1)


def swap(value):
    return pltpu.roll(value, 4, 0)


class Pairs:
    def __init__(self):
        self.top = half_mask()
        self.known = {}

    def __call__(self, upper, lower):
        key = (float(upper), float(lower))
        if key[0] == key[1]:
            return jnp.float32(key[0])
        if key not in self.known:
            self.known[key] = jnp.where(self.top, jnp.float32(key[0]), jnp.float32(key[1]))
        return self.known[key]

    def once(self, upper, lower):
        if float(upper) == float(lower):
            return jnp.float32(upper)
        return jnp.where(self.top, jnp.float32(upper), jnp.float32(lower))


def total(terms):
    terms = list(terms)
    while len(terms) > 1:
        terms = [
            terms[k] + terms[k + 1] if k + 1 < len(terms) else terms[k]
            for k in range(0, len(terms), 2)
        ]
    return terms[0]


def keep_masks(orders, top):
    both = jnp.concatenate([orders, orders], axis=0)
    known = {}

    def get(upper, lower):
        if (upper, lower) not in known:
            if upper == lower:
                bound = jnp.int32(upper)
            else:
                bound = jnp.where(top, jnp.int32(upper), jnp.int32(lower))
            known[upper, lower] = (both >= bound).astype(jnp.float32)
        return known[upper, lower]

    return get


def odd_of(pair):
    return min(2 * pair + 1, MODES - 1)


def line_traces(line):
    even = total(float(NORMED[n]) * line[n] for n in range(0, MODES, 2))
    odd = total(float(NORMED[n]) * line[n] for n in range(1, MODES, 2))
    even_slope = total(float(SLOPE[n]) * line[n] for n in range(2, MODES, 2))
    odd_slope = total(float(SLOPE[n]) * line[n] for n in range(1, MODES, 2))
    return even + odd, even_slope + odd_slope, even - odd, odd_slope - even_slope


def x_turn():
    return lax.axis_index("gx") + lax.axis_index("gz")


def goes_up(turn):
    return jnp.full((8, 128), lax.rem(turn, 2), jnp.int32) == 0


def has_place(axis, distance):
    place = lax.axis_index(axis) + distance
    return jnp.where((place >= 0) & (place < lax.axis_size(axis)), 1.0, 0.0).astype(jnp.float32)


def trace_kernel(
    rhs_hbm, orders_hbm, first, x_a, x_b, orders, rhs, arrived,
):
    copies = [pltpu.make_async_copy(orders_hbm, orders, arrived.at[MODES])]
    for b in range(MODES):
        copies.append(pltpu.make_async_copy(rhs_hbm.at[:, b], rhs.at[:, b], arrived.at[b]))
    for copy in copies:
        copy.start()
    pairs = Pairs()
    top = pairs.top
    upward = goes_up(x_turn())
    copies[0].wait()
    keep = keep_masks(orders[0], top)
    for b in range(MODES):
        copies[1 + b].wait()
        for e in range(MODES):
            column = []
            for i in range(PAIRS):
                upper = rhs[2 * i, b, e, 0]
                lower = rhs[2 * i + 1, b, e, 0] if 2 * i + 1 < MODES else jnp.zeros_like(upper)
                cell = jnp.concatenate([upper, lower], axis=0)
                mask = keep(max(2 * i, b, e), max(odd_of(i), b, e))
                scale = pairs.once(
                    1.0 / (THETA * diag(2 * i, b, e)), 1.0 / (THETA * diag(odd_of(i), b, e))
                )
                cell = cell * mask * scale
                first[i, b, e] = cell
                column.append(cell)
            odd = [odd_of(i) if 2 * i + 1 < MODES else None for i in range(PAIRS)]
            value = total(
                pairs(NORMED[2 * i], NORMED[odd[i]] if odd[i] else 0.0) * column[i]
                for i in range(PAIRS)
            )
            slope = total(
                pairs(SLOPE[2 * i], SLOPE[odd[i]] if odd[i] else 0.0) * column[i]
                for i in range(PAIRS)
            )
            both_value = jnp.where(top, value + swap(value), swap(value) - value)
            both_slope = jnp.where(top, slope + swap(slope), slope - swap(slope))
            up = jnp.where(top, both_value, swap(both_slope))
            down = jnp.where(top, swap(both_value), both_slope)
            x_a[b * MODES + e] = jnp.where(upward, up, down)
            x_b[b * MODES + e] = jnp.where(upward, down, up)


def side_trace_kernel(first, y_a, y_b, z_a, z_b, y_low, y_high, z_low, z_high):
    row, lane = row_in_half(), lanes()
    y_up, z_up = goes_up(lax.axis_index("gy")), goes_up(lax.axis_index("gz"))
    packed_up = packed_down = None
    for kind in range(2):
        for i in range(PAIRS):
            for e in range(MODES):
                m = i * MODES + e
                q = m % 4
                line = [first[i, b, e] for b in range(MODES)]
                traces = line_traces(line)
                high, low = traces[kind], traces[2 + kind]
                y_high[kind, m] = high
                y_low[kind, m] = low
                up, down = pltpu.roll(high, 5 + q, 0), pltpu.roll(low, q, 0) if q else low
                packed_up = up if q == 0 else jnp.where(row == q, up, packed_up)
                packed_down = down if q == 0 else jnp.where(row == q, down, packed_down)
                if q == 3:
                    k = kind * 7 + m // 4
                    y_a[k] = jnp.where(y_up, packed_up, packed_down)
                    y_b[k] = jnp.where(y_up, packed_down, packed_up)
    packed_up = packed_down = jnp.zeros((8, 128), jnp.float32)
    for i in range(PAIRS):
        for b in range(MODES):
            m = i * MODES + b
            line = [first[i, b, e] for e in range(MODES)]
            traces = line_traces(line)
            for kind in range(2):
                high, low = traces[kind], traces[2 + kind]
                z_high[kind, m] = high
                z_low[kind, m] = low
                place = 2 * m + kind
                packed_up = jnp.where(lane == place, pltpu.roll(high, 1 + place, 1), packed_up)
                down = pltpu.roll(low, place, 1) if place else low
                packed_down = jnp.where(lane == place, down, packed_down)
    z_a[...] = jnp.where(z_up, packed_up, packed_down)
    z_b[...] = jnp.where(z_up, packed_down, packed_up)


def own_kernel(first, early, out, early_again):
    early_again[...] = early[...]
    pairs = Pairs()
    for b in range(MODES):
        for e in range(MODES):
            column = [first[i, b, e] for i in range(PAIRS)]
            for i in range(PAIRS):
                terms = []
                for j in range(PAIRS):
                    lower = OWN[2 * i + 1, 2 * j + 1] if max(i, j) < 3 else 0.0
                    terms.append(pairs(OWN[2 * i, 2 * j], lower) * column[j])
                out[i, b, e] = total(terms)
    for i in range(PAIRS):
        for b in range(MODES):
            line = [first[i, b, e] for e in range(MODES)]
            for n in range(MODES):
                out[i, b, n] += total(
                    float(OWN[n, k]) * line[k] for k in range(n % 2, MODES, 2)
                )
        for e in range(MODES):
            line = [first[i, b, e] for b in range(MODES)]
            for n in range(MODES):
                out[i, n, e] += total(
                    float(OWN[n, k]) * line[k] for k in range(n % 2, MODES, 2)
                )


def neighbour_line(low_value, low_slope, high_value, high_slope):
    plus, minus = high_value + low_value, high_value - low_value
    even = 0.5 * (low_slope - high_slope) - PENALTY * plus
    odd = -0.5 * (low_slope + high_slope) - PENALTY * minus
    return (even, 0.5 * plus), (odd, 0.5 * minus)


def vertex_pair(first_mode, second_mode):
    base, tilt = ROOT_HALF * first_mode, THIRD * second_mode
    return base - tilt, base + tilt


def sum_to_vertices(grid, pairs, row, lane):
    top = pairs.top
    rows = {}
    for (dy, dz), value in grid.items():
        rows.setdefault(dy, []).append((dz, value))
    result = [[[], []], [[], []]]
    for dy, entries in rows.items():
        inner, outer = [], []
        for dz, value in entries:
            if dz == 0:
                inner.append(value)
                continue
            moved = pltpu.roll(value, dz % 128, 1)
            inside = lane >= dz if dz > 0 else lane < 128 + dz
            inner.append(jnp.where(inside, moved, 0.0))
            outer.append(jnp.where(inside, 0.0, moved))
        for beyond, terms in ((0, inner), (1, outer)):
            if not terms:
                continue
            value = total(terms)
            if dy == 0:
                result[0][beyond].append(value)
                continue
            moved = pltpu.roll(value, dy % 8, 0)
            inside = row >= dy if dy > 0 else row < 4 + dy
            result[0][beyond].append(jnp.where(inside, moved, 0.0))
            result[1][beyond].append(jnp.where(inside, 0.0, swap(moved)))
    return [[total(result[r][z]) for z in range(2)] for r in range(2)]


def side_kernel(
    local, y_a, y_b, z_b, z_a, y_below, y_above, z_below, z_above, out
):
    row, lane = row_in_half(), lanes()
    y_even, z_even = goes_up(lax.axis_index("gy")), goes_up(lax.axis_index("gz"))
    y_has_low, y_has_high = has_place("gy", -1), has_place("gy", 1)
    z_has_low, z_has_high = has_place("gz", -1), has_place("gz", 1)
    y_low, y_high = [], []
    for k in range(FACE_ROWS):
        one, two = y_a[k], y_b[k]
        y_low.append(y_has_low * jnp.where(y_even, two, one))
        y_high.append(y_has_high * jnp.where(y_even, one, two))
    for i in range(PAIRS):
        for e in range(MODES):
            m = i * MODES + e
            q = m % 4
            seen = []
            for kind in range(2):
                halo = y_low[kind * 7 + m // 4]
                halo = pltpu.roll(halo, 8 - q, 0) if q else halo
                moved = pltpu.roll(y_below[kind, m], 1, 0)
                seen.append(jnp.where(row == 0, halo, moved))
            for kind in range(2):
                halo = y_high[kind * 7 + m // 4]
                halo = pltpu.roll(halo, 3 - q, 0) if q < 3 else halo
                moved = pltpu.roll(y_above[kind, m], 7, 0)
                seen.append(jnp.where(row == 3, halo, moved))
            parts = neighbour_line(*seen)
            for n in range(MODES):
                value, slope = parts[n % 2]
                add = float(NORMED[n]) * value
                add = add + float(SLOPE[n]) * slope if n else add
                out[i, n, e] = local[i, n, e] + add
    z_low_halo = z_has_low * jnp.where(z_even, z_b[...], z_a[...])
    z_high_halo = z_has_high * jnp.where(z_even, z_a[...], z_b[...])
    for i in range(PAIRS):
        for b in range(MODES):
            m = i * MODES + b
            seen = []
            for kind in range(2):
                place = 2 * m + kind
                halo = pltpu.roll(z_low_halo, 128 - place, 1) if place else z_low_halo
                moved = pltpu.roll(z_below[kind, m], 1, 1)
                seen.append(jnp.where(lane == 0, halo, moved))
            for kind in range(2):
                place = 2 * m + kind
                halo = pltpu.roll(z_high_halo, 127 - place, 1)
                moved = pltpu.roll(z_above[kind, m], 127, 1)
                seen.append(jnp.where(lane == 127, halo, moved))
            parts = neighbour_line(*seen)
            for e in range(MODES):
                value, slope = parts[e % 2]
                add = float(NORMED[e]) * value
                if e:
                    add = add + float(SLOPE[e]) * slope
                out[i, b, e] += add


def finish_kernel(first, local, orders, x_a, x_b, field, here, sum_a, sum_b, far):
    pairs = Pairs()
    top = pairs.top
    row, lane = row_in_half(), lanes()
    keep = keep_masks(orders[0], top)
    has_low, has_high = has_place("gx", -1), has_place("gx", 1)
    upward = goes_up(x_turn())
    one_valid = jnp.where(upward, has_high, has_low)
    two_valid = jnp.where(upward, has_low, has_high)
    x_sign = jnp.where(upward, 1.0, -1.0)
    x_even = goes_up(lax.axis_index("gx"))
    for b in range(MODES):
        for e in range(MODES):
            one, two = one_valid * x_a[b * MODES + e], two_valid * x_b[b * MODES + e]
            plus, minus = one + two, swap(x_sign * (one - two))
            slope = 0.5 * jnp.where(top, plus, minus)
            value = (-2.0 * PENALTY) * slope - 0.5 * jnp.where(top, minus, plus)
            for i in range(PAIRS):
                last = 2 * i + 1 >= MODES
                k = odd_of(i)
                applied = local[i, b, e] + (
                    pairs(NORMED[2 * i], 0.0 if last else NORMED[k]) * value
                    + pairs(SLOPE[2 * i], 0.0 if last else SLOPE[k]) * slope
                )
                one = 2.0 * RHO_SECOND / (DELTA * PENALTY)
                scale = pairs.once(one / diag(2 * i, b, e), one / diag(odd_of(i), b, e))
                mask = keep(max(2 * i, b, e), max(odd_of(i), b, e))
                kappa = 1.0 + RHO_SECOND * RHO_FIRST + 2.0 * RHO_SECOND * THETA / DELTA
                after = kappa * first[i, b, e] - (mask * scale) * applied
                field[i, b, e] = after

    grid = {}

    def add(key, value):
        grid[key] = grid[key] + value if key in grid else value

    spread = -SPREAD / PENALTY
    for e in range(MODES):
        low, high = vertex_pair(field[0, 0, e], field[0, 1, e])
        for dz in range(-1, 3):
            add((0, dz), float(spread[dz + 1, e]) * low)
            add((1, dz), float(spread[dz + 1, e]) * high)
    for b in range(MODES):
        low, high = vertex_pair(field[0, b, 0], field[0, b, 1])
        for dy in range(-1, 3):
            add((dy, 0), float(spread[dy + 1, b]) * low)
            add((dy, 1), float(spread[dy + 1, b]) * high)
    force = [
        [
            pairs.once(THETA * diag(0, b, e), THETA * diag(1, b, e)) * first[0, b, e]
            for e in range(2)
        ]
        for b in range(2)
    ]
    force = [vertex_pair(force[0][e], force[1][e]) for e in range(2)]
    for dy in range(2):
        low, high = vertex_pair(force[0][dy], force[1][dy])
        add((dy, 0), low)
        add((dy, 1), high)
    kept, turned = pairs(ROOT_HALF, THIRD), pairs(-THIRD, ROOT_HALF)
    near = {key: kept * value + turned * swap(value) for key, value in grid.items()}
    outer = {}
    corners = []
    for i in range(PAIRS):
        line = [vertex_pair(field[i, 0, e], field[i, 1, e]) for e in range(2)]
        corners.append([vertex_pair(line[0][dy], line[1][dy]) for dy in range(2)])
    for dy in range(2):
        for dz in range(2):
            sums = []
            for dx in range(-1, 3):
                part = total(
                    pairs(
                        spread[dx + 1, 2 * i],
                        spread[dx + 1, 2 * i + 1] if 2 * i + 1 < MODES else 0.0,
                    )
                    * corners[i][dy][dz]
                    for i in range(PAIRS)
                )
                sums.append(part + swap(part))
            near[dy, dz] += jnp.where(top, sums[1], sums[2])
            outer[dy, dz] = jnp.where(top, sums[0], sums[3])
    near = sum_to_vertices(near, pairs, row, lane)
    outer = sum_to_vertices(outer, pairs, row, lane)
    for z in range(2):
        here[z] = jnp.where(top, near[0][z], swap(near[1][z]))
        ahead = jnp.where(top, swap(near[0][z]), near[1][z])
        behind = jnp.where(top, outer[0][z], swap(outer[1][z]))
        sum_a[z] = jnp.where(x_even, ahead, behind)
        sum_b[z] = jnp.where(x_even, behind, ahead)
        far[z] = jnp.where(top, swap(outer[0][z]), outer[1][z])


def unpack_kernel(field, here, smoothed, here_again):
    here_again[...] = here[...]
    for b in range(MODES):
        for e in range(MODES):
            for i in range(PAIRS):
                value = field[i, b, e]
                smoothed[2 * i, b, e, 0] = value[:4]
                if 2 * i + 1 < MODES:
                    smoothed[2 * i + 1, b, e, 0] = value[4:]


def column_kernel(chip, fetched, mated, third, column, blocks):
    count = lax.axis_size("gz")
    me = lax.axis_index("gz")
    core, place = lax.rem(me, 2), lax.div(me, 2)
    beside = place + 1 - 2 * lax.rem(place, 2)
    across = lax.rem(place + 2, 4)
    asked = beside + core * (across - beside)
    zero = jnp.zeros((8, 128), jnp.float32)
    blocks[0] = zero
    blocks[count + 1] = zero
    for source, sender, pair in (
        (place, core, chip),
        (asked, core, fetched),
        (beside + across - asked, 1 - core, mated),
        (3 - place, core, third),
    ):
        blocks[2 * source + sender + 1] = pair[0]
        blocks[2 * source + 2 - sender] = pair[1]
    lane = lax.broadcasted_iota(jnp.int32, (4, 128), 1)
    row = lax.broadcasted_iota(jnp.int32, (4, 128), 0)
    interior = (lax.axis_index("gx") > 0) & (lax.axis_index("gy") * 4 + row > 0)
    for k in range(count):
        value = (
            blocks[k + 1, :4]
            + jnp.where(lane < 2, blocks[k, 4:], 0.0)
            + jnp.where(lane == 127, blocks[k + 2, 4:], 0.0)
        )
        here = interior & (lane > 0) if k == 0 else interior
        column[0, :, k * 128 : (k + 1) * 128] = jnp.where(here, value, 0.0)


def shape(*dims):
    return jax.ShapeDtypeStruct(dims, jnp.float32)


def in_vmem(count):
    return [pl.BlockSpec(memory_space=pltpu.VMEM)] * count


def call(kernel, name, inputs, outputs, flops, scratch=(), in_hbm=False):
    size = sum(4 * int(np.prod(v.shape)) for v in (*inputs, *outputs))
    space = pltpu.HBM if in_hbm else pltpu.VMEM
    return pl.pallas_call(
        kernel,
        out_shape=outputs,
        in_specs=[pl.BlockSpec(memory_space=space)] * len(inputs),
        out_specs=[pl.BlockSpec(memory_space=pltpu.VMEM)] * len(outputs),
        scratch_shapes=list(scratch),
        name=name,
        cost_estimate=pl.CostEstimate(flops=flops, bytes_accessed=size, transcendentals=0),
        compiler_params=pltpu.CompilerParams(vmem_limit_bytes=24 * 1024 * 1024),
    )(*inputs)


def flip(value, axis, bits):
    return lax.ppermute(value, axis, [(i, i ^ bits) for i in range(lax.axis_size(axis))])


def exchange(value, partner):
    axes = ("gx", "gy", "gz")
    sizes = [lax.axis_size(name) for name in axes]
    route = [
        (source, int(np.ravel_multi_index(partner(list(place)), sizes)))
        for source, place in enumerate(np.ndindex(*sizes))
    ]
    return lax.ppermute(value, axes, route)


def second_of_pair(place, k, count, spare, bit):
    if place[k] in (0, count - 1):
        place[spare] ^= bit
    else:
        place[k] += 1 if place[k] % 2 else -1
    return place


def second_pairs(value, axis):
    k, count = ("gx", "gy", "gz").index(axis), lax.axis_size(axis)
    return exchange(value, lambda place: second_of_pair(place, k, count, 0 if k == 2 else 2, 1))


def x_pairs(value, turn):
    count = lax.axis_size("gx")

    def partner(place):
        if place[2] % 2 == turn:
            place[0] ^= 1
            return place
        return second_of_pair(place, 0, count, 1, 1)

    return exchange(value, partner)


def both_y_sides(value):
    count = lax.axis_size("gy")

    def partner(place):
        if place[2] % 2:
            return second_of_pair(place, 1, count, 0, 1)
        place[1] ^= 1
        return place

    return exchange(value, partner)


def two_chips(value):
    def partner(place):
        place[2] ^= 4 if place[2] % 2 else 2
        return place

    return exchange(value, partner)


def inside(axis, distance):
    place = lax.axis_index(axis) + distance
    return ((place >= 0) & (place < lax.axis_size(axis))).astype(jnp.float32)


def per_device(rhs, orders):
    cells = (PAIRS, MODES, MODES, 8, 128)
    sides = (shape(2, 28, 8, 128),) * 4
    first, x_a, x_b, held = call(
        trace_kernel,
        "x_traces",
        tuple(pltpu.with_memory_space_constraint(v, pltpu.HBM) for v in (rhs, orders)),
        (
            shape(*cells), shape(49, 8, 128), shape(49, 8, 128),
            jax.ShapeDtypeStruct(orders.shape, jnp.int32),
        ),
        4_000_000,
        scratch=(pltpu.VMEM(rhs.shape, jnp.float32), pltpu.SemaphoreType.DMA((MODES + 1,))),
        in_hbm=True,
    )
    x_a, x_b = x_pairs(x_a, 0), x_pairs(x_b, 1)
    y_a, y_b, z_a, z_b, y_low, y_high, z_low, z_high = call(
        side_trace_kernel,
        "side_traces",
        (first,),
        (shape(FACE_ROWS, 8, 128),) * 2 + (shape(8, 128),) * 2 + sides,
        SIDE_COST,
    )
    y_a, y_b = flip(y_a, "gy", 1), second_pairs(y_b, "gy")
    z_b = second_pairs(z_b, "gz")
    z_a = flip(z_a, "gz", 1)
    local, y_a = call(
        own_kernel, "own_cells", (first, y_a), (shape(*cells), shape(FACE_ROWS, 8, 128)), OWN_COST
    )
    (local,) = call(
        side_kernel,
        "side_halo",
        (local, y_a, y_b, z_b, z_a, y_high, y_low, z_high, z_low),
        (shape(*cells),),
        HALO_COST,
    )
    field, here, sum_a, sum_b, far = call(
        finish_kernel,
        "smooth_and_restrict",
        (first, local, held, x_a, x_b),
        (shape(*cells),) + (shape(2, 8, 128),) * 4,
        5_000_000,
    )
    smoothed, here = call(
        unpack_kernel,
        "unpack_modes",
        (field, here),
        (shape(*rhs.shape), shape(2, 8, 128)),
        200_000,
    )
    from_far = flip(far, "gx", 2)
    from_a = flip(sum_a, "gx", 1)
    from_b = second_pairs(sum_b, "gx")
    sums = (
        here
        + inside("gx", -2) * from_far
        + from_a
        + inside("gx", -1) * inside("gx", 1) * from_b
    )
    count = lax.axis_size("gz")
    chip = jnp.stack([sums, flip(sums, "gz", 1)])
    from_beside = both_y_sides(chip)
    from_low = (lax.axis_index("gy") + lax.axis_index("gz")) % 2 == 1
    row = lax.broadcasted_iota(jnp.int32, (1, 1, 4, 1), 2)
    wanted = jnp.where(from_low, row < 2, row == 3)
    valid = jnp.where(from_low, inside("gy", -1), inside("gy", 1))
    edges = jnp.where(wanted, from_beside[:, :, 4:], 0.0) * valid
    edges = edges.reshape(2, 8, 128)
    mated = flip(edges, "gz", 1)
    owned = chip[:, :, :4].reshape(2, 8, 128) + edges + mated[::-1]
    fetched = two_chips(owned)
    third = flip(owned, "gz", 6)
    (column,) = call(
        column_kernel,
        "column",
        (owned, fetched, flip(fetched, "gz", 1), third),
        (shape(1, 4, 128 * count),),
        20_000,
        scratch=(pltpu.VMEM((count + 2, 8, 128), jnp.float32),),
    )
    return smoothed, column


def solution(mesh):
    return jax.shard_map(
        per_device,
        mesh=mesh,
        in_specs=(P(None, None, None, "gx", "gy", "gz"), P("gx", "gy", "gz")),
        out_specs=(P(None, None, None, "gx", "gy", "gz"), P("gx", "gy", None)),
        check_vma=False,
    )
```

```python
import jax
import jax.numpy as jnp
import numpy as np
from jax import lax
from jax.experimental import pallas as pl
from jax.experimental.pallas import tpu as pltpu
from jax.sharding import PartitionSpec as P

PENALTY = 49.0
EIGEN_HIGH = 2.4
EIGEN_LOW = 0.24
THETA = 0.5 * (EIGEN_HIGH + EIGEN_LOW)
DELTA = 0.5 * (EIGEN_HIGH - EIGEN_LOW)
RHO_FIRST = DELTA / THETA
RHO_SECOND = 1.0 / (2.0 * THETA / DELTA - RHO_FIRST)
MODES = 7
PAIRS = 4
FACE_ROWS = 14
SIDE_COST = 4_000_000
OWN_COST = 1_400_000_000
HALO_COST = 4_000_000


def basis_tables():
    degree = np.arange(MODES)
    normed = np.sqrt((2.0 * degree + 1.0) / 2.0)
    smaller = np.minimum(degree[:, None], degree[None, :])
    parity = (degree[:, None] + degree[None, :]) % 2 == 0
    stiffness = np.where(parity, normed[:, None] * normed[None, :] * smaller * (smaller + 1), 0.0)
    signs = (-1.0) ** degree
    slope = normed * degree * (degree + 1) / 2.0
    high, high_slope = normed, slope
    low, low_slope = normed * signs, -slope * signs
    own = (
        stiffness
        + PENALTY * (np.outer(high, high) + np.outer(low, low))
        - 0.5 * (np.outer(high, high_slope) + np.outer(high_slope, high))
        + 0.5 * (np.outer(low, low_slope) + np.outer(low_slope, low))
    )
    own = np.where(parity, own, 0.0)
    to_next = np.outer(low, 0.5 * high_slope - PENALTY * high) - 0.5 * np.outer(low_slope, high)
    to_last = np.outer(high, -PENALTY * low - 0.5 * low_slope) + 0.5 * np.outer(high_slope, low)
    one_axis = normed * normed * degree * (degree + 1) + 2.0 * (
        PENALTY * normed * normed - normed * slope
    )
    third = np.sqrt(1.5) / 3.0
    vertex = np.zeros((MODES, 2))
    vertex[0] = np.sqrt(0.5)
    vertex[1] = -third, third
    spread = np.stack(
        [
            vertex[:, 0] @ to_last,
            vertex[:, 1] @ to_last + vertex[:, 0] @ own,
            vertex[:, 1] @ own + vertex[:, 0] @ to_next,
            vertex[:, 1] @ to_next,
        ]
    )
    return normed, slope, own, one_axis, spread, third


NORMED, SLOPE, OWN, ONE_AXIS, SPREAD, THIRD = basis_tables()
ROOT_HALF = float(np.sqrt(0.5))


def diag(a, b, e):
    return float((ONE_AXIS[a] + ONE_AXIS[b] + ONE_AXIS[e]) / PENALTY)


def half_mask():
    return lax.broadcasted_iota(jnp.int32, (8, 128), 0) < 4


def row_in_half():
    return lax.broadcasted_iota(jnp.int32, (8, 128), 0) % 4


def lanes():
    return lax.broadcasted_iota(jnp.int32, (8, 128), 1)


def swap(value):
    return pltpu.roll(value, 4, 0)


class Pairs:
    def __init__(self):
        self.top = half_mask()
        self.known = {}

    def __call__(self, upper, lower):
        key = (float(upper), float(lower))
        if key[0] == key[1]:
            return jnp.float32(key[0])
        if key not in self.known:
            self.known[key] = jnp.where(self.top, jnp.float32(key[0]), jnp.float32(key[1]))
        return self.known[key]

    def once(self, upper, lower):
        if float(upper) == float(lower):
            return jnp.float32(upper)
        return jnp.where(self.top, jnp.float32(upper), jnp.float32(lower))


def total(terms):
    terms = list(terms)
    while len(terms) > 1:
        terms = [
            terms[k] + terms[k + 1] if k + 1 < len(terms) else terms[k]
            for k in range(0, len(terms), 2)
        ]
    return terms[0]


def keep_masks(orders, top):
    both = jnp.concatenate([orders, orders], axis=0)
    known = {}

    def get(upper, lower):
        if (upper, lower) not in known:
            if upper == lower:
                bound = jnp.int32(upper)
            else:
                bound = jnp.where(top, jnp.int32(upper), jnp.int32(lower))
            known[upper, lower] = (both >= bound).astype(jnp.float32)
        return known[upper, lower]

    return get


def odd_of(pair):
    return min(2 * pair + 1, MODES - 1)


def line_traces(line):
    even = total(float(NORMED[n]) * line[n] for n in range(0, MODES, 2))
    odd = total(float(NORMED[n]) * line[n] for n in range(1, MODES, 2))
    even_slope = total(float(SLOPE[n]) * line[n] for n in range(2, MODES, 2))
    odd_slope = total(float(SLOPE[n]) * line[n] for n in range(1, MODES, 2))
    return even + odd, even_slope + odd_slope, even - odd, odd_slope - even_slope


def x_turn():
    return lax.axis_index("gx") + lax.axis_index("gz")


def goes_up(turn):
    return jnp.full((8, 128), lax.rem(turn, 2), jnp.int32) == 0


def has_place(axis, distance):
    place = lax.axis_index(axis) + distance
    return jnp.where((place >= 0) & (place < lax.axis_size(axis)), 1.0, 0.0).astype(jnp.float32)


def trace_kernel(
    rhs_hbm, orders_hbm, first, x_a, x_b, orders, rhs, arrived,
):
    copies = [pltpu.make_async_copy(orders_hbm, orders, arrived.at[MODES])]
    for b in range(MODES):
        copies.append(pltpu.make_async_copy(rhs_hbm.at[:, b], rhs.at[:, b], arrived.at[b]))
    for copy in copies:
        copy.start()
    pairs = Pairs()
    top = pairs.top
    upward = goes_up(x_turn())
    copies[0].wait()
    keep = keep_masks(orders[0], top)
    for b in range(MODES):
        copies[1 + b].wait()
        for e in range(MODES):
            column = []
            for i in range(PAIRS):
                upper = rhs[2 * i, b, e, 0]
                lower = rhs[2 * i + 1, b, e, 0] if 2 * i + 1 < MODES else jnp.zeros_like(upper)
                cell = jnp.concatenate([upper, lower], axis=0)
                mask = keep(max(2 * i, b, e), max(odd_of(i), b, e))
                scale = pairs.once(
                    1.0 / (THETA * diag(2 * i, b, e)), 1.0 / (THETA * diag(odd_of(i), b, e))
                )
                cell = cell * mask * scale
                first[i, b, e] = cell
                column.append(cell)
            odd = [odd_of(i) if 2 * i + 1 < MODES else None for i in range(PAIRS)]
            value = total(
                pairs(NORMED[2 * i], NORMED[odd[i]] if odd[i] else 0.0) * column[i]
                for i in range(PAIRS)
            )
            slope = total(
                pairs(SLOPE[2 * i], SLOPE[odd[i]] if odd[i] else 0.0) * column[i]
                for i in range(PAIRS)
            )
            both_value = jnp.where(top, value + swap(value), swap(value) - value)
            both_slope = jnp.where(top, slope + swap(slope), slope - swap(slope))
            up = jnp.where(top, both_value, swap(both_slope))
            down = jnp.where(top, swap(both_value), both_slope)
            x_a[b * MODES + e] = jnp.where(upward, up, down)
            x_b[b * MODES + e] = jnp.where(upward, down, up)


def side_trace_kernel(first, y_a, y_b, z_a, z_b, y_low, y_high, z_low, z_high):
    row, lane = row_in_half(), lanes()
    y_up, z_up = goes_up(lax.axis_index("gy")), goes_up(lax.axis_index("gz"))
    packed_up = packed_down = None
    for kind in range(2):
        for i in range(PAIRS):
            for e in range(MODES):
                m = i * MODES + e
                q = m % 4
                line = [first[i, b, e] for b in range(MODES)]
                traces = line_traces(line)
                high, low = traces[kind], traces[2 + kind]
                y_high[kind, m] = high
                y_low[kind, m] = low
                up, down = pltpu.roll(high, 5 + q, 0), pltpu.roll(low, q, 0) if q else low
                packed_up = up if q == 0 else jnp.where(row == q, up, packed_up)
                packed_down = down if q == 0 else jnp.where(row == q, down, packed_down)
                if q == 3:
                    k = kind * 7 + m // 4
                    y_a[k] = jnp.where(y_up, packed_up, packed_down)
                    y_b[k] = jnp.where(y_up, packed_down, packed_up)
    packed_up = packed_down = jnp.zeros((8, 128), jnp.float32)
    for i in range(PAIRS):
        for b in range(MODES):
            m = i * MODES + b
            line = [first[i, b, e] for e in range(MODES)]
            traces = line_traces(line)
            for kind in range(2):
                high, low = traces[kind], traces[2 + kind]
                z_high[kind, m] = high
                z_low[kind, m] = low
                place = 2 * m + kind
                packed_up = jnp.where(lane == place, pltpu.roll(high, 1 + place, 1), packed_up)
                down = pltpu.roll(low, place, 1) if place else low
                packed_down = jnp.where(lane == place, down, packed_down)
    z_a[...] = jnp.where(z_up, packed_up, packed_down)
    z_b[...] = jnp.where(z_up, packed_down, packed_up)


def own_kernel(first, early, out, early_again):
    early_again[...] = early[...]
    pairs = Pairs()
    for b in range(MODES):
        for e in range(MODES):
            column = [first[i, b, e] for i in range(PAIRS)]
            for i in range(PAIRS):
                terms = []
                for j in range(PAIRS):
                    lower = OWN[2 * i + 1, 2 * j + 1] if max(i, j) < 3 else 0.0
                    terms.append(pairs(OWN[2 * i, 2 * j], lower) * column[j])
                out[i, b, e] = total(terms)
    for i in range(PAIRS):
        for b in range(MODES):
            line = [first[i, b, e] for e in range(MODES)]
            for n in range(MODES):
                out[i, b, n] += total(
                    float(OWN[n, k]) * line[k] for k in range(n % 2, MODES, 2)
                )
        for e in range(MODES):
            line = [first[i, b, e] for b in range(MODES)]
            for n in range(MODES):
                out[i, n, e] += total(
                    float(OWN[n, k]) * line[k] for k in range(n % 2, MODES, 2)
                )


def neighbour_line(low_value, low_slope, high_value, high_slope):
    plus, minus = high_value + low_value, high_value - low_value
    even = 0.5 * (low_slope - high_slope) - PENALTY * plus
    odd = -0.5 * (low_slope + high_slope) - PENALTY * minus
    return (even, 0.5 * plus), (odd, 0.5 * minus)


def vertex_pair(first_mode, second_mode):
    base, tilt = ROOT_HALF * first_mode, THIRD * second_mode
    return base - tilt, base + tilt


def sum_to_vertices(grid, pairs, row, lane):
    top = pairs.top
    rows = {}
    for (dy, dz), value in grid.items():
        rows.setdefault(dy, []).append((dz, value))
    result = [[[], []], [[], []]]
    for dy, entries in rows.items():
        inner, outer = [], []
        for dz, value in entries:
            if dz == 0:
                inner.append(value)
                continue
            moved = pltpu.roll(value, dz % 128, 1)
            inside = lane >= dz if dz > 0 else lane < 128 + dz
            inner.append(jnp.where(inside, moved, 0.0))
            outer.append(jnp.where(inside, 0.0, moved))
        for beyond, terms in ((0, inner), (1, outer)):
            if not terms:
                continue
            value = total(terms)
            if dy == 0:
                result[0][beyond].append(value)
                continue
            moved = pltpu.roll(value, dy % 8, 0)
            inside = row >= dy if dy > 0 else row < 4 + dy
            result[0][beyond].append(jnp.where(inside, moved, 0.0))
            result[1][beyond].append(jnp.where(inside, 0.0, swap(moved)))
    return [[total(result[r][z]) for z in range(2)] for r in range(2)]


def side_kernel(
    local, y_a, y_b, z_b, z_a, y_below, y_above, z_below, z_above, out
):
    row, lane = row_in_half(), lanes()
    y_even, z_even = goes_up(lax.axis_index("gy")), goes_up(lax.axis_index("gz"))
    y_has_low, y_has_high = has_place("gy", -1), has_place("gy", 1)
    z_has_low, z_has_high = has_place("gz", -1), has_place("gz", 1)
    y_low, y_high = [], []
    for k in range(FACE_ROWS):
        one, two = y_a[k], y_b[k]
        y_low.append(y_has_low * jnp.where(y_even, two, one))
        y_high.append(y_has_high * jnp.where(y_even, one, two))
    for i in range(PAIRS):
        for e in range(MODES):
            m = i * MODES + e
            q = m % 4
            seen = []
            for kind in range(2):
                halo = y_low[kind * 7 + m // 4]
                halo = pltpu.roll(halo, 8 - q, 0) if q else halo
                moved = pltpu.roll(y_below[kind, m], 1, 0)
                seen.append(jnp.where(row == 0, halo, moved))
            for kind in range(2):
                halo = y_high[kind * 7 + m // 4]
                halo = pltpu.roll(halo, 3 - q, 0) if q < 3 else halo
                moved = pltpu.roll(y_above[kind, m], 7, 0)
                seen.append(jnp.where(row == 3, halo, moved))
            parts = neighbour_line(*seen)
            for n in range(MODES):
                value, slope = parts[n % 2]
                add = float(NORMED[n]) * value
                add = add + float(SLOPE[n]) * slope if n else add
                out[i, n, e] = local[i, n, e] + add
    z_low_halo = z_has_low * jnp.where(z_even, z_b[...], z_a[...])
    z_high_halo = z_has_high * jnp.where(z_even, z_a[...], z_b[...])
    for i in range(PAIRS):
        for b in range(MODES):
            m = i * MODES + b
            seen = []
            for kind in range(2):
                place = 2 * m + kind
                halo = pltpu.roll(z_low_halo, 128 - place, 1) if place else z_low_halo
                moved = pltpu.roll(z_below[kind, m], 1, 1)
                seen.append(jnp.where(lane == 0, halo, moved))
            for kind in range(2):
                place = 2 * m + kind
                halo = pltpu.roll(z_high_halo, 127 - place, 1)
                moved = pltpu.roll(z_above[kind, m], 127, 1)
                seen.append(jnp.where(lane == 127, halo, moved))
            parts = neighbour_line(*seen)
            for e in range(MODES):
                value, slope = parts[e % 2]
                add = float(NORMED[e]) * value
                if e:
                    add = add + float(SLOPE[e]) * slope
                out[i, b, e] += add


def finish_kernel(first, local, orders, x_a, x_b, field, parts):
    pairs = Pairs()
    top = pairs.top
    row, lane = row_in_half(), lanes()
    keep = keep_masks(orders[0], top)
    has_low, has_high = has_place("gx", -1), has_place("gx", 1)
    upward = goes_up(x_turn())
    one_valid = jnp.where(upward, has_high, has_low)
    two_valid = jnp.where(upward, has_low, has_high)
    x_sign = jnp.where(upward, 1.0, -1.0)
    x_even = goes_up(lax.axis_index("gx"))
    for b in range(MODES):
        for e in range(MODES):
            one, two = one_valid * x_a[b * MODES + e], two_valid * x_b[b * MODES + e]
            plus, minus = one + two, swap(x_sign * (one - two))
            slope = 0.5 * jnp.where(top, plus, minus)
            value = (-2.0 * PENALTY) * slope - 0.5 * jnp.where(top, minus, plus)
            for i in range(PAIRS):
                last = 2 * i + 1 >= MODES
                k = odd_of(i)
                applied = local[i, b, e] + (
                    pairs(NORMED[2 * i], 0.0 if last else NORMED[k]) * value
                    + pairs(SLOPE[2 * i], 0.0 if last else SLOPE[k]) * slope
                )
                one = 2.0 * RHO_SECOND / (DELTA * PENALTY)
                scale = pairs.once(one / diag(2 * i, b, e), one / diag(odd_of(i), b, e))
                mask = keep(max(2 * i, b, e), max(odd_of(i), b, e))
                kappa = 1.0 + RHO_SECOND * RHO_FIRST + 2.0 * RHO_SECOND * THETA / DELTA
                after = kappa * first[i, b, e] - (mask * scale) * applied
                field[i, b, e] = after

    grid = {}

    def add(key, value):
        grid[key] = grid[key] + value if key in grid else value

    spread = -SPREAD / PENALTY
    for e in range(MODES):
        low, high = vertex_pair(field[0, 0, e], field[0, 1, e])
        for dz in range(-1, 3):
            add((0, dz), float(spread[dz + 1, e]) * low)
            add((1, dz), float(spread[dz + 1, e]) * high)
    for b in range(MODES):
        low, high = vertex_pair(field[0, b, 0], field[0, b, 1])
        for dy in range(-1, 3):
            add((dy, 0), float(spread[dy + 1, b]) * low)
            add((dy, 1), float(spread[dy + 1, b]) * high)
    force = [
        [
            pairs.once(THETA * diag(0, b, e), THETA * diag(1, b, e)) * first[0, b, e]
            for e in range(2)
        ]
        for b in range(2)
    ]
    force = [vertex_pair(force[0][e], force[1][e]) for e in range(2)]
    for dy in range(2):
        low, high = vertex_pair(force[0][dy], force[1][dy])
        add((dy, 0), low)
        add((dy, 1), high)
    kept, turned = pairs(ROOT_HALF, THIRD), pairs(-THIRD, ROOT_HALF)
    near = {key: kept * value + turned * swap(value) for key, value in grid.items()}
    outer = {}
    corners = []
    for i in range(PAIRS):
        line = [vertex_pair(field[i, 0, e], field[i, 1, e]) for e in range(2)]
        corners.append([vertex_pair(line[0][dy], line[1][dy]) for dy in range(2)])
    for dy in range(2):
        for dz in range(2):
            sums = []
            for dx in range(-1, 3):
                part = total(
                    pairs(
                        spread[dx + 1, 2 * i],
                        spread[dx + 1, 2 * i + 1] if 2 * i + 1 < MODES else 0.0,
                    )
                    * corners[i][dy][dz]
                    for i in range(PAIRS)
                )
                sums.append(part + swap(part))
            near[dy, dz] += jnp.where(top, sums[1], sums[2])
            outer[dy, dz] = jnp.where(top, sums[0], sums[3])
    near = sum_to_vertices(near, pairs, row, lane)
    outer = sum_to_vertices(outer, pairs, row, lane)
    for z in range(2):
        parts[0, z] = jnp.where(top, near[0][z], swap(near[1][z]))
        ahead = jnp.where(top, swap(near[0][z]), near[1][z])
        behind = jnp.where(top, outer[0][z], swap(outer[1][z]))
        parts[1, z] = jnp.where(x_even, ahead, behind)
        parts[2, z] = jnp.where(x_even, behind, ahead)
        parts[3, z] = jnp.where(top, swap(outer[0][z]), outer[1][z])


def unpack_kernel(field, here, smoothed, here_again):
    here_again[...] = here[...]
    for b in range(MODES):
        for e in range(MODES):
            for i in range(PAIRS):
                value = field[i, b, e]
                smoothed[2 * i, b, e, 0] = value[:4]
                if 2 * i + 1 < MODES:
                    smoothed[2 * i + 1, b, e, 0] = value[4:]


def column_kernel(chip, third, fetched, mated, column, blocks):
    count = lax.axis_size("gz")
    me = lax.axis_index("gz")
    core, place = lax.rem(me, 2), lax.div(me, 2)
    beside = place + 1 - 2 * lax.rem(place, 2)
    across = lax.rem(place + 2, 4)
    asked = beside + core * (across - beside)
    zero = jnp.zeros((8, 128), jnp.float32)
    blocks[0] = zero
    blocks[count + 1] = zero
    for source, sender, pair in (
        (place, core, chip),
        (asked, core, fetched),
        (beside + across - asked, 1 - core, mated),
        (3 - place, core, third),
    ):
        blocks[2 * source + sender + 1] = pair[0]
        blocks[2 * source + 2 - sender] = pair[1]
    lane = lax.broadcasted_iota(jnp.int32, (4, 128), 1)
    row = lax.broadcasted_iota(jnp.int32, (4, 128), 0)
    interior = (lax.axis_index("gx") > 0) & (lax.axis_index("gy") * 4 + row > 0)
    for k in range(count):
        value = (
            blocks[k + 1, :4]
            + jnp.where(lane < 2, blocks[k, 4:], 0.0)
            + jnp.where(lane == 127, blocks[k + 2, 4:], 0.0)
        )
        here = interior & (lane > 0) if k == 0 else interior
        column[0, :, k * 128 : (k + 1) * 128] = jnp.where(here, value, 0.0)


def shape(*dims):
    return jax.ShapeDtypeStruct(dims, jnp.float32)


def in_vmem(count):
    return [pl.BlockSpec(memory_space=pltpu.VMEM)] * count


def call(kernel, name, inputs, outputs, flops, scratch=(), in_hbm=False):
    size = sum(4 * int(np.prod(v.shape)) for v in (*inputs, *outputs))
    space = pltpu.HBM if in_hbm else pltpu.VMEM
    return pl.pallas_call(
        kernel,
        out_shape=outputs,
        in_specs=[pl.BlockSpec(memory_space=space)] * len(inputs),
        out_specs=[pl.BlockSpec(memory_space=pltpu.VMEM)] * len(outputs),
        scratch_shapes=list(scratch),
        name=name,
        cost_estimate=pl.CostEstimate(flops=flops, bytes_accessed=size, transcendentals=0),
        compiler_params=pltpu.CompilerParams(vmem_limit_bytes=24 * 1024 * 1024),
    )(*inputs)


def flip(value, axis, bits):
    return lax.ppermute(value, axis, [(i, i ^ bits) for i in range(lax.axis_size(axis))])


def exchange(value, partner):
    axes = ("gx", "gy", "gz")
    sizes = [lax.axis_size(name) for name in axes]
    route = [
        (source, int(np.ravel_multi_index(partner(list(place)), sizes)))
        for source, place in enumerate(np.ndindex(*sizes))
    ]
    return lax.ppermute(value, axes, route)


def second_of_pair(place, k, count, spare, bit):
    if place[k] in (0, count - 1):
        place[spare] ^= bit
    else:
        place[k] += 1 if place[k] % 2 else -1
    return place


def second_pairs(value, axis):
    k, count = ("gx", "gy", "gz").index(axis), lax.axis_size(axis)
    return exchange(value, lambda place: second_of_pair(place, k, count, 0 if k == 2 else 2, 1))


def x_pairs(value, turn):
    count = lax.axis_size("gx")

    def partner(place):
        if place[2] % 2 == turn:
            place[0] ^= 1
            return place
        return second_of_pair(place, 0, count, 1, 1)

    return exchange(value, partner)


def far_or_beside(value):
    def partner(place):
        place[0] ^= 2 if place[2] % 2 else 1
        return place

    return exchange(value, partner)


def both_y_sides(value):
    count = lax.axis_size("gy")

    def partner(place):
        if place[2] % 2:
            return second_of_pair(place, 1, count, 0, 1)
        place[1] ^= 1
        return place

    return exchange(value, partner)


def two_chips(value):
    def partner(place):
        place[2] ^= 4 if place[2] % 2 else 2
        return place

    return exchange(value, partner)


def inside(axis, distance):
    place = lax.axis_index(axis) + distance
    return ((place >= 0) & (place < lax.axis_size(axis))).astype(jnp.float32)


def per_device(rhs, orders):
    cells = (PAIRS, MODES, MODES, 8, 128)
    sides = (shape(2, 28, 8, 128),) * 4
    first, x_a, x_b, held = call(
        trace_kernel,
        "x_traces",
        tuple(pltpu.with_memory_space_constraint(v, pltpu.HBM) for v in (rhs, orders)),
        (
            shape(*cells), shape(49, 8, 128), shape(49, 8, 128),
            jax.ShapeDtypeStruct(orders.shape, jnp.int32),
        ),
        4_000_000,
        scratch=(pltpu.VMEM(rhs.shape, jnp.float32), pltpu.SemaphoreType.DMA((MODES + 1,))),
        in_hbm=True,
    )
    x_a, x_b = x_pairs(x_a, 0), x_pairs(x_b, 1)
    y_a, y_b, z_a, z_b, y_low, y_high, z_low, z_high = call(
        side_trace_kernel,
        "side_traces",
        (first,),
        (shape(FACE_ROWS, 8, 128),) * 2 + (shape(8, 128),) * 2 + sides,
        SIDE_COST,
    )
    y_a, y_b = flip(y_a, "gy", 1), second_pairs(y_b, "gy")
    z_b = second_pairs(z_b, "gz")
    z_a = flip(z_a, "gz", 1)
    local, y_a = call(
        own_kernel, "own_cells", (first, y_a), (shape(*cells), shape(FACE_ROWS, 8, 128)), OWN_COST
    )
    (local,) = call(
        side_kernel,
        "side_halo",
        (local, y_a, y_b, z_b, z_a, y_high, y_low, z_high, z_low),
        (shape(*cells),),
        HALO_COST,
    )
    field, parts = call(
        finish_kernel,
        "smooth_and_restrict",
        (first, local, held, x_a, x_b),
        (shape(*cells), shape(4, 2, 8, 128)),
        5_000_000,
    )
    count = lax.axis_size("gz")
    both = jnp.stack([parts, flip(parts, "gz", 1)])
    first_core = lax.axis_index("gz") % 2 == 0
    from_one = far_or_beside(jnp.where(first_core, both[:, 1], both[:, 3]))
    from_two = second_pairs(both[:, 2], "gx")
    smoothed, here = call(
        unpack_kernel,
        "unpack_modes",
        (field, both[:, 0]),
        (shape(*rhs.shape), shape(2, 2, 8, 128)),
        200_000,
    )
    sums = (
        jnp.where(first_core, 1.0, inside("gx", -2)) * from_one
        + jnp.where(first_core, 0.0, inside("gx", -1) * inside("gx", 1)) * from_two
        + jnp.where(first_core, 0.0, here)
    )
    chip = sums + flip(sums, "gz", 1)[::-1]
    from_beside = both_y_sides(chip[:, :, 4:].reshape(2, 8, 128)).reshape(2, 2, 4, 128)
    from_low = (lax.axis_index("gy") + lax.axis_index("gz")) % 2 == 1
    row = lax.broadcasted_iota(jnp.int32, (1, 1, 4, 1), 2)
    wanted = jnp.where(from_low, row < 2, row == 3)
    valid = jnp.where(from_low, inside("gy", -1), inside("gy", 1))
    edges = jnp.where(wanted, from_beside, 0.0) * valid
    edges = edges.reshape(2, 8, 128)
    mated = flip(edges, "gz", 1)
    owned = chip[:, :, :4].reshape(2, 8, 128) + edges + mated[::-1]
    third = flip(owned, "gz", 6)
    fetched = two_chips(owned)
    (column,) = call(
        column_kernel,
        "column",
        (owned, third, fetched, flip(fetched, "gz", 1)),
        (shape(1, 4, 128 * count),),
        20_000,
        scratch=(pltpu.VMEM((count + 2, 8, 128), jnp.float32),),
    )
    return smoothed, column


def solution(mesh):
    return jax.shard_map(
        per_device,
        mesh=mesh,
        in_specs=(P(None, None, None, "gx", "gy", "gz"), P("gx", "gy", "gz")),
        out_specs=(P(None, None, None, "gx", "gy", "gz"), P("gx", "gy", None)),
        check_vma=False,
    )
```

```python
import jax
import jax.numpy as jnp
import numpy as np
from jax import lax
from jax.experimental import pallas as pl
from jax.experimental.pallas import tpu as pltpu
from jax.sharding import PartitionSpec as P

PENALTY = 49.0
EIGEN_HIGH = 2.4
EIGEN_LOW = 0.24
THETA = 0.5 * (EIGEN_HIGH + EIGEN_LOW)
DELTA = 0.5 * (EIGEN_HIGH - EIGEN_LOW)
RHO_FIRST = DELTA / THETA
RHO_SECOND = 1.0 / (2.0 * THETA / DELTA - RHO_FIRST)
MODES = 7
PAIRS = 4
FACE_ROWS = 14
SIDE_COST = 4_000_000
OWN_COST = 1_400_000_000
HALO_COST = 4_000_000


def basis_tables():
    degree = np.arange(MODES)
    normed = np.sqrt((2.0 * degree + 1.0) / 2.0)
    smaller = np.minimum(degree[:, None], degree[None, :])
    parity = (degree[:, None] + degree[None, :]) % 2 == 0
    stiffness = np.where(parity, normed[:, None] * normed[None, :] * smaller * (smaller + 1), 0.0)
    signs = (-1.0) ** degree
    slope = normed * degree * (degree + 1) / 2.0
    high, high_slope = normed, slope
    low, low_slope = normed * signs, -slope * signs
    own = (
        stiffness
        + PENALTY * (np.outer(high, high) + np.outer(low, low))
        - 0.5 * (np.outer(high, high_slope) + np.outer(high_slope, high))
        + 0.5 * (np.outer(low, low_slope) + np.outer(low_slope, low))
    )
    own = np.where(parity, own, 0.0)
    to_next = np.outer(low, 0.5 * high_slope - PENALTY * high) - 0.5 * np.outer(low_slope, high)
    to_last = np.outer(high, -PENALTY * low - 0.5 * low_slope) + 0.5 * np.outer(high_slope, low)
    one_axis = normed * normed * degree * (degree + 1) + 2.0 * (
        PENALTY * normed * normed - normed * slope
    )
    third = np.sqrt(1.5) / 3.0
    vertex = np.zeros((MODES, 2))
    vertex[0] = np.sqrt(0.5)
    vertex[1] = -third, third
    spread = np.stack(
        [
            vertex[:, 0] @ to_last,
            vertex[:, 1] @ to_last + vertex[:, 0] @ own,
            vertex[:, 1] @ own + vertex[:, 0] @ to_next,
            vertex[:, 1] @ to_next,
        ]
    )
    return normed, slope, own, one_axis, spread, third


NORMED, SLOPE, OWN, ONE_AXIS, SPREAD, THIRD = basis_tables()
ROOT_HALF = float(np.sqrt(0.5))


def diag(a, b, e):
    return float((ONE_AXIS[a] + ONE_AXIS[b] + ONE_AXIS[e]) / PENALTY)


def half_mask():
    return lax.broadcasted_iota(jnp.int32, (8, 128), 0) < 4


def row_in_half():
    return lax.broadcasted_iota(jnp.int32, (8, 128), 0) % 4


def lanes():
    return lax.broadcasted_iota(jnp.int32, (8, 128), 1)


def swap(value):
    return pltpu.roll(value, 4, 0)


class Pairs:
    def __init__(self):
        self.top = half_mask()
        self.known = {}

    def __call__(self, upper, lower):
        key = (float(upper), float(lower))
        if key[0] == key[1]:
            return jnp.float32(key[0])
        if key not in self.known:
            self.known[key] = jnp.where(self.top, jnp.float32(key[0]), jnp.float32(key[1]))
        return self.known[key]

    def once(self, upper, lower):
        if float(upper) == float(lower):
            return jnp.float32(upper)
        return jnp.where(self.top, jnp.float32(upper), jnp.float32(lower))


def total(terms):
    terms = list(terms)
    while len(terms) > 1:
        terms = [
            terms[k] + terms[k + 1] if k + 1 < len(terms) else terms[k]
            for k in range(0, len(terms), 2)
        ]
    return terms[0]


def keep_masks(orders, top):
    both = jnp.concatenate([orders, orders], axis=0)
    known = {}

    def get(upper, lower):
        if (upper, lower) not in known:
            if upper == lower:
                bound = jnp.int32(upper)
            else:
                bound = jnp.where(top, jnp.int32(upper), jnp.int32(lower))
            known[upper, lower] = (both >= bound).astype(jnp.float32)
        return known[upper, lower]

    return get


def odd_of(pair):
    return min(2 * pair + 1, MODES - 1)


def line_traces(line):
    even = total(float(NORMED[n]) * line[n] for n in range(0, MODES, 2))
    odd = total(float(NORMED[n]) * line[n] for n in range(1, MODES, 2))
    even_slope = total(float(SLOPE[n]) * line[n] for n in range(2, MODES, 2))
    odd_slope = total(float(SLOPE[n]) * line[n] for n in range(1, MODES, 2))
    return even + odd, even_slope + odd_slope, even - odd, odd_slope - even_slope


def x_turn():
    return lax.axis_index("gx") + lax.axis_index("gz")


def goes_up(turn):
    return jnp.full((8, 128), lax.rem(turn, 2), jnp.int32) == 0


def has_place(axis, distance):
    place = lax.axis_index(axis) + distance
    return jnp.where((place >= 0) & (place < lax.axis_size(axis)), 1.0, 0.0).astype(jnp.float32)


def trace_kernel(
    rhs_hbm, orders_hbm, first, x_a, x_b, orders, rhs, arrived,
):
    copies = [pltpu.make_async_copy(orders_hbm, orders, arrived.at[MODES])]
    for b in range(MODES):
        copies.append(pltpu.make_async_copy(rhs_hbm.at[:, b], rhs.at[:, b], arrived.at[b]))
    for copy in copies:
        copy.start()
    pairs = Pairs()
    top = pairs.top
    upward = goes_up(x_turn())
    copies[0].wait()
    keep = keep_masks(orders[0], top)
    for b in range(MODES):
        copies[1 + b].wait()
        for e in range(MODES):
            column = []
            for i in range(PAIRS):
                upper = rhs[2 * i, b, e, 0]
                lower = rhs[2 * i + 1, b, e, 0] if 2 * i + 1 < MODES else jnp.zeros_like(upper)
                cell = jnp.concatenate([upper, lower], axis=0)
                mask = keep(max(2 * i, b, e), max(odd_of(i), b, e))
                scale = pairs.once(
                    1.0 / (THETA * diag(2 * i, b, e)), 1.0 / (THETA * diag(odd_of(i), b, e))
                )
                cell = cell * mask * scale
                first[i, b, e] = cell
                column.append(cell)
            odd = [odd_of(i) if 2 * i + 1 < MODES else None for i in range(PAIRS)]
            value = total(
                pairs(NORMED[2 * i], NORMED[odd[i]] if odd[i] else 0.0) * column[i]
                for i in range(PAIRS)
            )
            slope = total(
                pairs(SLOPE[2 * i], SLOPE[odd[i]] if odd[i] else 0.0) * column[i]
                for i in range(PAIRS)
            )
            both_value = jnp.where(top, value + swap(value), swap(value) - value)
            both_slope = jnp.where(top, slope + swap(slope), slope - swap(slope))
            up = jnp.where(top, both_value, swap(both_slope))
            down = jnp.where(top, swap(both_value), both_slope)
            x_a[b * MODES + e] = jnp.where(upward, up, down)
            x_b[b * MODES + e] = jnp.where(upward, down, up)


def side_trace_kernel(first, y_a, y_b, z_a, z_b, y_low, y_high, z_low, z_high):
    row, lane = row_in_half(), lanes()
    y_up, z_up = goes_up(lax.axis_index("gy")), goes_up(lax.axis_index("gz"))
    packed_up = packed_down = None
    for kind in range(2):
        for i in range(PAIRS):
            for e in range(MODES):
                m = i * MODES + e
                q = m % 4
                line = [first[i, b, e] for b in range(MODES)]
                traces = line_traces(line)
                high, low = traces[kind], traces[2 + kind]
                y_high[kind, m] = high
                y_low[kind, m] = low
                up, down = pltpu.roll(high, 5 + q, 0), pltpu.roll(low, q, 0) if q else low
                packed_up = up if q == 0 else jnp.where(row == q, up, packed_up)
                packed_down = down if q == 0 else jnp.where(row == q, down, packed_down)
                if q == 3:
                    k = kind * 7 + m // 4
                    y_a[k] = jnp.where(y_up, packed_up, packed_down)
                    y_b[k] = jnp.where(y_up, packed_down, packed_up)
    packed_up = packed_down = jnp.zeros((8, 128), jnp.float32)
    for i in range(PAIRS):
        for b in range(MODES):
            m = i * MODES + b
            line = [first[i, b, e] for e in range(MODES)]
            traces = line_traces(line)
            for kind in range(2):
                high, low = traces[kind], traces[2 + kind]
                z_high[kind, m] = high
                z_low[kind, m] = low
                place = 2 * m + kind
                packed_up = jnp.where(lane == place, pltpu.roll(high, 1 + place, 1), packed_up)
                down = pltpu.roll(low, place, 1) if place else low
                packed_down = jnp.where(lane == place, down, packed_down)
    z_a[...] = jnp.where(z_up, packed_up, packed_down)
    z_b[...] = jnp.where(z_up, packed_down, packed_up)


def own_kernel(first, early, out, early_again):
    early_again[...] = early[...]
    pairs = Pairs()
    for b in range(MODES):
        for e in range(MODES):
            column = [first[i, b, e] for i in range(PAIRS)]
            for i in range(PAIRS):
                terms = []
                for j in range(PAIRS):
                    lower = OWN[2 * i + 1, 2 * j + 1] if max(i, j) < 3 else 0.0
                    terms.append(pairs(OWN[2 * i, 2 * j], lower) * column[j])
                out[i, b, e] = total(terms)
    for i in range(PAIRS):
        for b in range(MODES):
            line = [first[i, b, e] for e in range(MODES)]
            for n in range(MODES):
                out[i, b, n] += total(
                    float(OWN[n, k]) * line[k] for k in range(n % 2, MODES, 2)
                )
        for e in range(MODES):
            line = [first[i, b, e] for b in range(MODES)]
            for n in range(MODES):
                out[i, n, e] += total(
                    float(OWN[n, k]) * line[k] for k in range(n % 2, MODES, 2)
                )


def neighbour_line(low_value, low_slope, high_value, high_slope):
    plus, minus = high_value + low_value, high_value - low_value
    even = 0.5 * (low_slope - high_slope) - PENALTY * plus
    odd = -0.5 * (low_slope + high_slope) - PENALTY * minus
    return (even, 0.5 * plus), (odd, 0.5 * minus)


def vertex_pair(first_mode, second_mode):
    base, tilt = ROOT_HALF * first_mode, THIRD * second_mode
    return base - tilt, base + tilt


def sum_to_vertices(grid, pairs, row, lane):
    top = pairs.top
    rows = {}
    for (dy, dz), value in grid.items():
        rows.setdefault(dy, []).append((dz, value))
    result = [[[], []], [[], []]]
    for dy, entries in rows.items():
        inner, outer = [], []
        for dz, value in entries:
            if dz == 0:
                inner.append(value)
                continue
            moved = pltpu.roll(value, dz % 128, 1)
            inside = lane >= dz if dz > 0 else lane < 128 + dz
            inner.append(jnp.where(inside, moved, 0.0))
            outer.append(jnp.where(inside, 0.0, moved))
        for beyond, terms in ((0, inner), (1, outer)):
            if not terms:
                continue
            value = total(terms)
            if dy == 0:
                result[0][beyond].append(value)
                continue
            moved = pltpu.roll(value, dy % 8, 0)
            inside = row >= dy if dy > 0 else row < 4 + dy
            result[0][beyond].append(jnp.where(inside, moved, 0.0))
            result[1][beyond].append(jnp.where(inside, 0.0, swap(moved)))
    return [[total(result[r][z]) for z in range(2)] for r in range(2)]


def side_kernel(
    local, y_a, y_b, z_b, z_a, y_below, y_above, z_below, z_above, out
):
    row, lane = row_in_half(), lanes()
    y_even, z_even = goes_up(lax.axis_index("gy")), goes_up(lax.axis_index("gz"))
    y_has_low, y_has_high = has_place("gy", -1), has_place("gy", 1)
    z_has_low, z_has_high = has_place("gz", -1), has_place("gz", 1)
    y_low, y_high = [], []
    for k in range(FACE_ROWS):
        one, two = y_a[k], y_b[k]
        y_low.append(y_has_low * jnp.where(y_even, two, one))
        y_high.append(y_has_high * jnp.where(y_even, one, two))
    for i in range(PAIRS):
        for e in range(MODES):
            m = i * MODES + e
            q = m % 4
            seen = []
            for kind in range(2):
                halo = y_low[kind * 7 + m // 4]
                halo = pltpu.roll(halo, 8 - q, 0) if q else halo
                moved = pltpu.roll(y_below[kind, m], 1, 0)
                seen.append(jnp.where(row == 0, halo, moved))
            for kind in range(2):
                halo = y_high[kind * 7 + m // 4]
                halo = pltpu.roll(halo, 3 - q, 0) if q < 3 else halo
                moved = pltpu.roll(y_above[kind, m], 7, 0)
                seen.append(jnp.where(row == 3, halo, moved))
            parts = neighbour_line(*seen)
            for n in range(MODES):
                value, slope = parts[n % 2]
                add = float(NORMED[n]) * value
                add = add + float(SLOPE[n]) * slope if n else add
                out[i, n, e] = local[i, n, e] + add
    z_low_halo = z_has_low * jnp.where(z_even, z_b[...], z_a[...])
    z_high_halo = z_has_high * jnp.where(z_even, z_a[...], z_b[...])
    for i in range(PAIRS):
        for b in range(MODES):
            m = i * MODES + b
            seen = []
            for kind in range(2):
                place = 2 * m + kind
                halo = pltpu.roll(z_low_halo, 128 - place, 1) if place else z_low_halo
                moved = pltpu.roll(z_below[kind, m], 1, 1)
                seen.append(jnp.where(lane == 0, halo, moved))
            for kind in range(2):
                place = 2 * m + kind
                halo = pltpu.roll(z_high_halo, 127 - place, 1)
                moved = pltpu.roll(z_above[kind, m], 127, 1)
                seen.append(jnp.where(lane == 127, halo, moved))
            parts = neighbour_line(*seen)
            for e in range(MODES):
                value, slope = parts[e % 2]
                add = float(NORMED[e]) * value
                if e:
                    add = add + float(SLOPE[e]) * slope
                out[i, b, e] += add


def finish_kernel(first, local, orders, x_a, x_b, field, parts):
    pairs = Pairs()
    top = pairs.top
    row, lane = row_in_half(), lanes()
    keep = keep_masks(orders[0], top)
    has_low, has_high = has_place("gx", -1), has_place("gx", 1)
    upward = goes_up(x_turn())
    one_valid = jnp.where(upward, has_high, has_low)
    two_valid = jnp.where(upward, has_low, has_high)
    x_sign = jnp.where(upward, 1.0, -1.0)
    x_even = goes_up(lax.axis_index("gx"))
    for b in range(MODES):
        for e in range(MODES):
            one, two = one_valid * x_a[b * MODES + e], two_valid * x_b[b * MODES + e]
            plus, minus = one + two, swap(x_sign * (one - two))
            slope = 0.5 * jnp.where(top, plus, minus)
            value = (-2.0 * PENALTY) * slope - 0.5 * jnp.where(top, minus, plus)
            for i in range(PAIRS):
                last = 2 * i + 1 >= MODES
                k = odd_of(i)
                applied = local[i, b, e] + (
                    pairs(NORMED[2 * i], 0.0 if last else NORMED[k]) * value
                    + pairs(SLOPE[2 * i], 0.0 if last else SLOPE[k]) * slope
                )
                one = 2.0 * RHO_SECOND / (DELTA * PENALTY)
                scale = pairs.once(one / diag(2 * i, b, e), one / diag(odd_of(i), b, e))
                mask = keep(max(2 * i, b, e), max(odd_of(i), b, e))
                kappa = 1.0 + RHO_SECOND * RHO_FIRST + 2.0 * RHO_SECOND * THETA / DELTA
                after = kappa * first[i, b, e] - (mask * scale) * applied
                field[i, b, e] = after

    grid = {}

    def add(key, value):
        grid[key] = grid[key] + value if key in grid else value

    spread = -SPREAD / PENALTY
    for e in range(MODES):
        low, high = vertex_pair(field[0, 0, e], field[0, 1, e])
        for dz in range(-1, 3):
            add((0, dz), float(spread[dz + 1, e]) * low)
            add((1, dz), float(spread[dz + 1, e]) * high)
    for b in range(MODES):
        low, high = vertex_pair(field[0, b, 0], field[0, b, 1])
        for dy in range(-1, 3):
            add((dy, 0), float(spread[dy + 1, b]) * low)
            add((dy, 1), float(spread[dy + 1, b]) * high)
    force = [
        [
            pairs.once(THETA * diag(0, b, e), THETA * diag(1, b, e)) * first[0, b, e]
            for e in range(2)
        ]
        for b in range(2)
    ]
    force = [vertex_pair(force[0][e], force[1][e]) for e in range(2)]
    for dy in range(2):
        low, high = vertex_pair(force[0][dy], force[1][dy])
        add((dy, 0), low)
        add((dy, 1), high)
    kept, turned = pairs(ROOT_HALF, THIRD), pairs(-THIRD, ROOT_HALF)
    near = {key: kept * value + turned * swap(value) for key, value in grid.items()}
    outer = {}
    corners = []
    for i in range(PAIRS):
        line = [vertex_pair(field[i, 0, e], field[i, 1, e]) for e in range(2)]
        corners.append([vertex_pair(line[0][dy], line[1][dy]) for dy in range(2)])
    for dy in range(2):
        for dz in range(2):
            sums = []
            for dx in range(-1, 3):
                part = total(
                    pairs(
                        spread[dx + 1, 2 * i],
                        spread[dx + 1, 2 * i + 1] if 2 * i + 1 < MODES else 0.0,
                    )
                    * corners[i][dy][dz]
                    for i in range(PAIRS)
                )
                sums.append(part + swap(part))
            near[dy, dz] += jnp.where(top, sums[1], sums[2])
            outer[dy, dz] = jnp.where(top, sums[0], sums[3])
    near = sum_to_vertices(near, pairs, row, lane)
    outer = sum_to_vertices(outer, pairs, row, lane)
    for z in range(2):
        parts[0, z] = jnp.where(top, near[0][z], swap(near[1][z]))
        ahead = jnp.where(top, swap(near[0][z]), near[1][z])
        behind = jnp.where(top, outer[0][z], swap(outer[1][z]))
        parts[1, z] = jnp.where(x_even, ahead, behind)
        parts[2, z] = jnp.where(x_even, behind, ahead)
        parts[3, z] = jnp.where(top, swap(outer[0][z]), outer[1][z])


def unpack_kernel(field, here, smoothed, here_again):
    here_again[...] = here[...]
    for b in range(MODES):
        for e in range(MODES):
            for i in range(PAIRS):
                value = field[i, b, e]
                smoothed[2 * i, b, e, 0] = value[:4]
                if 2 * i + 1 < MODES:
                    smoothed[2 * i + 1, b, e, 0] = value[4:]


def column_kernel(chip, third, fetched, mated, column, blocks):
    count = lax.axis_size("gz")
    me = lax.axis_index("gz")
    core, place = lax.rem(me, 2), lax.div(me, 2)
    beside = place + 1 - 2 * lax.rem(place, 2)
    across = lax.rem(place + 2, 4)
    asked = beside + core * (across - beside)
    zero = jnp.zeros((8, 128), jnp.float32)
    blocks[0] = zero
    blocks[count + 1] = zero
    for source, sender, pair in (
        (place, core, chip),
        (asked, core, fetched),
        (beside + across - asked, 1 - core, mated),
        (3 - place, core, third),
    ):
        blocks[2 * source + sender + 1] = pair[0]
        blocks[2 * source + 2 - sender] = pair[1]
    lane = lax.broadcasted_iota(jnp.int32, (4, 128), 1)
    row = lax.broadcasted_iota(jnp.int32, (4, 128), 0)
    interior = (lax.axis_index("gx") > 0) & (lax.axis_index("gy") * 4 + row > 0)
    for k in range(count):
        value = (
            blocks[k + 1, :4]
            + jnp.where(lane < 2, blocks[k, 4:], 0.0)
            + jnp.where(lane == 127, blocks[k + 2, 4:], 0.0)
        )
        here = interior & (lane > 0) if k == 0 else interior
        column[0, :, k * 128 : (k + 1) * 128] = jnp.where(here, value, 0.0)


def shape(*dims):
    return jax.ShapeDtypeStruct(dims, jnp.float32)


def in_vmem(count):
    return [pl.BlockSpec(memory_space=pltpu.VMEM)] * count


def call(kernel, name, inputs, outputs, flops, scratch=(), in_hbm=False):
    size = sum(4 * int(np.prod(v.shape)) for v in (*inputs, *outputs))
    space = pltpu.HBM if in_hbm else pltpu.VMEM
    return pl.pallas_call(
        kernel,
        out_shape=outputs,
        in_specs=[pl.BlockSpec(memory_space=space)] * len(inputs),
        out_specs=[pl.BlockSpec(memory_space=pltpu.VMEM)] * len(outputs),
        scratch_shapes=list(scratch),
        name=name,
        cost_estimate=pl.CostEstimate(flops=flops, bytes_accessed=size, transcendentals=0),
        compiler_params=pltpu.CompilerParams(vmem_limit_bytes=24 * 1024 * 1024),
    )(*inputs)


def flip(value, axis, bits):
    return lax.ppermute(value, axis, [(i, i ^ bits) for i in range(lax.axis_size(axis))])


def exchange(value, partner):
    axes = ("gx", "gy", "gz")
    sizes = [lax.axis_size(name) for name in axes]
    route = [
        (source, int(np.ravel_multi_index(partner(list(place)), sizes)))
        for source, place in enumerate(np.ndindex(*sizes))
    ]
    return lax.ppermute(value, axes, route)


def second_of_pair(place, k, count, spare, bit):
    if place[k] in (0, count - 1):
        place[spare] ^= bit
    else:
        place[k] += 1 if place[k] % 2 else -1
    return place


def second_pairs(value, axis):
    k, count = ("gx", "gy", "gz").index(axis), lax.axis_size(axis)
    return exchange(value, lambda place: second_of_pair(place, k, count, 0 if k == 2 else 2, 1))


def x_pairs(value, turn):
    count = lax.axis_size("gx")

    def partner(place):
        if place[2] % 2 == turn:
            place[0] ^= 1
            return place
        return second_of_pair(place, 0, count, 1, 1)

    return exchange(value, partner)


def far_or_beside(value):
    def partner(place):
        place[0] ^= 2 if place[2] % 2 else 1
        return place

    return exchange(value, partner)


def both_y_sides(value):
    count = lax.axis_size("gy")

    def partner(place):
        if place[2] % 2:
            return second_of_pair(place, 1, count, 0, 1)
        place[1] ^= 1
        return place

    return exchange(value, partner)


def two_chips(value):
    def partner(place):
        place[2] ^= 4 if place[2] % 2 else 2
        return place

    return exchange(value, partner)


def inside(axis, distance):
    place = lax.axis_index(axis) + distance
    return ((place >= 0) & (place < lax.axis_size(axis))).astype(jnp.float32)


def per_device(rhs, orders):
    cells = (PAIRS, MODES, MODES, 8, 128)
    sides = (shape(2, 28, 8, 128),) * 4
    first, x_a, x_b, held = call(
        trace_kernel,
        "x_traces",
        tuple(pltpu.with_memory_space_constraint(v, pltpu.HBM) for v in (rhs, orders)),
        (
            shape(*cells), shape(49, 8, 128), shape(49, 8, 128),
            jax.ShapeDtypeStruct(orders.shape, jnp.int32),
        ),
        4_000_000,
        scratch=(pltpu.VMEM(rhs.shape, jnp.float32), pltpu.SemaphoreType.DMA((MODES + 1,))),
        in_hbm=True,
    )
    x_a, x_b = x_pairs(x_a, 0), x_pairs(x_b, 1)
    y_a, y_b, z_a, z_b, y_low, y_high, z_low, z_high = call(
        side_trace_kernel,
        "side_traces",
        (first,),
        (shape(FACE_ROWS, 8, 128),) * 2 + (shape(8, 128),) * 2 + sides,
        SIDE_COST,
    )
    y_a, y_b = flip(y_a, "gy", 1), second_pairs(y_b, "gy")
    z_b = second_pairs(z_b, "gz")
    z_a = flip(z_a, "gz", 1)
    local, y_a = call(
        own_kernel, "own_cells", (first, y_a), (shape(*cells), shape(FACE_ROWS, 8, 128)), OWN_COST
    )
    (local,) = call(
        side_kernel,
        "side_halo",
        (local, y_a, y_b, z_b, z_a, y_high, y_low, z_high, z_low),
        (shape(*cells),),
        HALO_COST,
    )
    field, parts = call(
        finish_kernel,
        "smooth_and_restrict",
        (first, local, held, x_a, x_b),
        (shape(*cells), shape(4, 2, 8, 128)),
        5_000_000,
    )
    count = lax.axis_size("gz")
    both = jnp.stack([parts, flip(parts, "gz", 1)])
    first_core = lax.axis_index("gz") % 2 == 0
    from_two = second_pairs(both[:, 2], "gx")
    from_one = far_or_beside(jnp.where(first_core, both[:, 1], both[:, 3]))
    smoothed, here = call(
        unpack_kernel,
        "unpack_modes",
        (field, both[:, 0]),
        (shape(*rhs.shape), shape(2, 2, 8, 128)),
        200_000,
    )
    sums = (
        jnp.where(first_core, 0.0, inside("gx", -1) * inside("gx", 1)) * from_two
        + jnp.where(first_core, 1.0, inside("gx", -2)) * from_one
        + jnp.where(first_core, 0.0, here)
    )
    chip = sums + flip(sums, "gz", 1)[::-1]
    from_beside = both_y_sides(chip[:, :, 4:].reshape(2, 8, 128)).reshape(2, 2, 4, 128)
    from_low = (lax.axis_index("gy") + lax.axis_index("gz")) % 2 == 1
    row = lax.broadcasted_iota(jnp.int32, (1, 1, 4, 1), 2)
    wanted = jnp.where(from_low, row < 2, row == 3)
    valid = jnp.where(from_low, inside("gy", -1), inside("gy", 1))
    edges = jnp.where(wanted, from_beside, 0.0) * valid
    edges = edges.reshape(2, 8, 128)
    mated = flip(edges, "gz", 1)
    owned = chip[:, :, :4].reshape(2, 8, 128) + edges + mated[::-1]
    third = flip(owned, "gz", 6)
    fetched = two_chips(owned)
    (column,) = call(
        column_kernel,
        "column",
        (owned, third, fetched, flip(fetched, "gz", 1)),
        (shape(1, 4, 128 * count),),
        20_000,
        scratch=(pltpu.VMEM((count + 2, 8, 128), jnp.float32),),
    )
    return smoothed, column


def solution(mesh):
    return jax.shard_map(
        per_device,
        mesh=mesh,
        in_specs=(P(None, None, None, "gx", "gy", "gz"), P("gx", "gy", "gz")),
        out_specs=(P(None, None, None, "gx", "gy", "gz"), P("gx", "gy", None)),
        check_vma=False,
    )
```

```python
import jax
import jax.numpy as jnp
import numpy as np
from jax import lax
from jax.experimental import pallas as pl
from jax.experimental.pallas import tpu as pltpu
from jax.sharding import PartitionSpec as P

PENALTY = 49.0
EIGEN_HIGH = 2.4
EIGEN_LOW = 0.24
THETA = 0.5 * (EIGEN_HIGH + EIGEN_LOW)
DELTA = 0.5 * (EIGEN_HIGH - EIGEN_LOW)
RHO_FIRST = DELTA / THETA
RHO_SECOND = 1.0 / (2.0 * THETA / DELTA - RHO_FIRST)
MODES = 7
PAIRS = 4
FACE_ROWS = 14
SIDE_COST = 4_000_000
OWN_COST = 1_400_000_000
HALO_COST = 4_000_000


def basis_tables():
    degree = np.arange(MODES)
    normed = np.sqrt((2.0 * degree + 1.0) / 2.0)
    smaller = np.minimum(degree[:, None], degree[None, :])
    parity = (degree[:, None] + degree[None, :]) % 2 == 0
    stiffness = np.where(parity, normed[:, None] * normed[None, :] * smaller * (smaller + 1), 0.0)
    signs = (-1.0) ** degree
    slope = normed * degree * (degree + 1) / 2.0
    high, high_slope = normed, slope
    low, low_slope = normed * signs, -slope * signs
    own = (
        stiffness
        + PENALTY * (np.outer(high, high) + np.outer(low, low))
        - 0.5 * (np.outer(high, high_slope) + np.outer(high_slope, high))
        + 0.5 * (np.outer(low, low_slope) + np.outer(low_slope, low))
    )
    own = np.where(parity, own, 0.0)
    to_next = np.outer(low, 0.5 * high_slope - PENALTY * high) - 0.5 * np.outer(low_slope, high)
    to_last = np.outer(high, -PENALTY * low - 0.5 * low_slope) + 0.5 * np.outer(high_slope, low)
    one_axis = normed * normed * degree * (degree + 1) + 2.0 * (
        PENALTY * normed * normed - normed * slope
    )
    third = np.sqrt(1.5) / 3.0
    vertex = np.zeros((MODES, 2))
    vertex[0] = np.sqrt(0.5)
    vertex[1] = -third, third
    spread = np.stack(
        [
            vertex[:, 0] @ to_last,
            vertex[:, 1] @ to_last + vertex[:, 0] @ own,
            vertex[:, 1] @ own + vertex[:, 0] @ to_next,
            vertex[:, 1] @ to_next,
        ]
    )
    return normed, slope, own, one_axis, spread, third


NORMED, SLOPE, OWN, ONE_AXIS, SPREAD, THIRD = basis_tables()
ROOT_HALF = float(np.sqrt(0.5))


def diag(a, b, e):
    return float((ONE_AXIS[a] + ONE_AXIS[b] + ONE_AXIS[e]) / PENALTY)


def half_mask():
    return lax.broadcasted_iota(jnp.int32, (8, 128), 0) < 4


def row_in_half():
    return lax.broadcasted_iota(jnp.int32, (8, 128), 0) % 4


def lanes():
    return lax.broadcasted_iota(jnp.int32, (8, 128), 1)


def swap(value):
    return pltpu.roll(value, 4, 0)


class Pairs:
    def __init__(self):
        self.top = half_mask()
        self.known = {}

    def __call__(self, upper, lower):
        key = (float(upper), float(lower))
        if key[0] == key[1]:
            return jnp.float32(key[0])
        if key not in self.known:
            self.known[key] = jnp.where(self.top, jnp.float32(key[0]), jnp.float32(key[1]))
        return self.known[key]

    def once(self, upper, lower):
        if float(upper) == float(lower):
            return jnp.float32(upper)
        return jnp.where(self.top, jnp.float32(upper), jnp.float32(lower))


def total(terms):
    terms = list(terms)
    while len(terms) > 1:
        terms = [
            terms[k] + terms[k + 1] if k + 1 < len(terms) else terms[k]
            for k in range(0, len(terms), 2)
        ]
    return terms[0]


def keep_masks(orders, top):
    both = jnp.concatenate([orders, orders], axis=0)
    known = {}

    def get(upper, lower):
        if (upper, lower) not in known:
            if upper == lower:
                bound = jnp.int32(upper)
            else:
                bound = jnp.where(top, jnp.int32(upper), jnp.int32(lower))
            known[upper, lower] = (both >= bound).astype(jnp.float32)
        return known[upper, lower]

    return get


def odd_of(pair):
    return min(2 * pair + 1, MODES - 1)


def line_traces(line):
    even = total(float(NORMED[n]) * line[n] for n in range(0, MODES, 2))
    odd = total(float(NORMED[n]) * line[n] for n in range(1, MODES, 2))
    even_slope = total(float(SLOPE[n]) * line[n] for n in range(2, MODES, 2))
    odd_slope = total(float(SLOPE[n]) * line[n] for n in range(1, MODES, 2))
    return even + odd, even_slope + odd_slope, even - odd, odd_slope - even_slope


def x_turn():
    return lax.axis_index("gx") + lax.axis_index("gz")


def goes_up(turn):
    return jnp.full((8, 128), lax.rem(turn, 2), jnp.int32) == 0


def has_place(axis, distance):
    place = lax.axis_index(axis) + distance
    return jnp.where((place >= 0) & (place < lax.axis_size(axis)), 1.0, 0.0).astype(jnp.float32)


def trace_kernel(
    rhs_hbm, orders_hbm, first, x_a, x_b, orders, rhs, arrived,
):
    copies = [pltpu.make_async_copy(orders_hbm, orders, arrived.at[MODES])]
    for b in range(MODES):
        copies.append(pltpu.make_async_copy(rhs_hbm.at[:, b], rhs.at[:, b], arrived.at[b]))
    for copy in copies:
        copy.start()
    pairs = Pairs()
    top = pairs.top
    upward = goes_up(x_turn())
    copies[0].wait()
    keep = keep_masks(orders[0], top)
    for b in range(MODES):
        copies[1 + b].wait()
        for e in range(MODES):
            column = []
            for i in range(PAIRS):
                upper = rhs[2 * i, b, e, 0]
                lower = rhs[2 * i + 1, b, e, 0] if 2 * i + 1 < MODES else jnp.zeros_like(upper)
                cell = jnp.concatenate([upper, lower], axis=0)
                mask = keep(max(2 * i, b, e), max(odd_of(i), b, e))
                scale = pairs.once(
                    1.0 / (THETA * diag(2 * i, b, e)), 1.0 / (THETA * diag(odd_of(i), b, e))
                )
                cell = cell * mask * scale
                first[i, b, e] = cell
                column.append(cell)
            odd = [odd_of(i) if 2 * i + 1 < MODES else None for i in range(PAIRS)]
            value = total(
                pairs(NORMED[2 * i], NORMED[odd[i]] if odd[i] else 0.0) * column[i]
                for i in range(PAIRS)
            )
            slope = total(
                pairs(SLOPE[2 * i], SLOPE[odd[i]] if odd[i] else 0.0) * column[i]
                for i in range(PAIRS)
            )
            both_value = jnp.where(top, value + swap(value), swap(value) - value)
            both_slope = jnp.where(top, slope + swap(slope), slope - swap(slope))
            up = jnp.where(top, both_value, swap(both_slope))
            down = jnp.where(top, swap(both_value), both_slope)
            x_a[b * MODES + e] = jnp.where(upward, up, down)
            x_b[b * MODES + e] = jnp.where(upward, down, up)


def side_trace_kernel(first, y_a, y_b, z_a, z_b, y_low, y_high, z_low, z_high):
    row, lane = row_in_half(), lanes()
    y_up, z_up = goes_up(lax.axis_index("gy")), goes_up(lax.axis_index("gz"))
    packed_up = packed_down = None
    for kind in range(2):
        for i in range(PAIRS):
            for e in range(MODES):
                m = i * MODES + e
                q = m % 4
                line = [first[i, b, e] for b in range(MODES)]
                traces = line_traces(line)
                high, low = traces[kind], traces[2 + kind]
                y_high[kind, m] = high
                y_low[kind, m] = low
                up, down = pltpu.roll(high, 5 + q, 0), pltpu.roll(low, q, 0) if q else low
                packed_up = up if q == 0 else jnp.where(row == q, up, packed_up)
                packed_down = down if q == 0 else jnp.where(row == q, down, packed_down)
                if q == 3:
                    k = kind * 7 + m // 4
                    y_a[k] = jnp.where(y_up, packed_up, packed_down)
                    y_b[k] = jnp.where(y_up, packed_down, packed_up)
    packed_up = packed_down = jnp.zeros((8, 128), jnp.float32)
    for i in range(PAIRS):
        for b in range(MODES):
            m = i * MODES + b
            line = [first[i, b, e] for e in range(MODES)]
            traces = line_traces(line)
            for kind in range(2):
                high, low = traces[kind], traces[2 + kind]
                z_high[kind, m] = high
                z_low[kind, m] = low
                place = 2 * m + kind
                packed_up = jnp.where(lane == place, pltpu.roll(high, 1 + place, 1), packed_up)
                down = pltpu.roll(low, place, 1) if place else low
                packed_down = jnp.where(lane == place, down, packed_down)
    z_a[...] = jnp.where(z_up, packed_up, packed_down)
    z_b[...] = jnp.where(z_up, packed_down, packed_up)


def own_kernel(first, early, out, early_again):
    early_again[...] = early[...]
    pairs = Pairs()
    for b in range(MODES):
        for e in range(MODES):
            column = [first[i, b, e] for i in range(PAIRS)]
            for i in range(PAIRS):
                terms = []
                for j in range(PAIRS):
                    lower = OWN[2 * i + 1, 2 * j + 1] if max(i, j) < 3 else 0.0
                    terms.append(pairs(OWN[2 * i, 2 * j], lower) * column[j])
                out[i, b, e] = total(terms)
    for i in range(PAIRS):
        for b in range(MODES):
            line = [first[i, b, e] for e in range(MODES)]
            for n in range(MODES):
                out[i, b, n] += total(
                    float(OWN[n, k]) * line[k] for k in range(n % 2, MODES, 2)
                )
        for e in range(MODES):
            line = [first[i, b, e] for b in range(MODES)]
            for n in range(MODES):
                out[i, n, e] += total(
                    float(OWN[n, k]) * line[k] for k in range(n % 2, MODES, 2)
                )


def neighbour_line(low_value, low_slope, high_value, high_slope):
    plus, minus = high_value + low_value, high_value - low_value
    even = 0.5 * (low_slope - high_slope) - PENALTY * plus
    odd = -0.5 * (low_slope + high_slope) - PENALTY * minus
    return (even, 0.5 * plus), (odd, 0.5 * minus)


def vertex_pair(first_mode, second_mode):
    base, tilt = ROOT_HALF * first_mode, THIRD * second_mode
    return base - tilt, base + tilt


def sum_to_vertices(grid, pairs, row, lane):
    top = pairs.top
    rows = {}
    for (dy, dz), value in grid.items():
        rows.setdefault(dy, []).append((dz, value))
    result = [[[], []], [[], []]]
    for dy, entries in rows.items():
        inner, outer = [], []
        for dz, value in entries:
            if dz == 0:
                inner.append(value)
                continue
            moved = pltpu.roll(value, dz % 128, 1)
            inside = lane >= dz if dz > 0 else lane < 128 + dz
            inner.append(jnp.where(inside, moved, 0.0))
            outer.append(jnp.where(inside, 0.0, moved))
        for beyond, terms in ((0, inner), (1, outer)):
            if not terms:
                continue
            value = total(terms)
            if dy == 0:
                result[0][beyond].append(value)
                continue
            moved = pltpu.roll(value, dy % 8, 0)
            inside = row >= dy if dy > 0 else row < 4 + dy
            result[0][beyond].append(jnp.where(inside, moved, 0.0))
            result[1][beyond].append(jnp.where(inside, 0.0, swap(moved)))
    return [[total(result[r][z]) for z in range(2)] for r in range(2)]


def side_kernel(
    local, y_a, y_b, z_b, z_a, y_below, y_above, z_below, z_above, out
):
    row, lane = row_in_half(), lanes()
    y_even, z_even = goes_up(lax.axis_index("gy")), goes_up(lax.axis_index("gz"))
    y_has_low, y_has_high = has_place("gy", -1), has_place("gy", 1)
    z_has_low, z_has_high = has_place("gz", -1), has_place("gz", 1)
    y_low, y_high = [], []
    for k in range(FACE_ROWS):
        one, two = y_a[k], y_b[k]
        y_low.append(y_has_low * jnp.where(y_even, two, one))
        y_high.append(y_has_high * jnp.where(y_even, one, two))
    for i in range(PAIRS):
        for e in range(MODES):
            m = i * MODES + e
            q = m % 4
            seen = []
            for kind in range(2):
                halo = y_low[kind * 7 + m // 4]
                halo = pltpu.roll(halo, 8 - q, 0) if q else halo
                moved = pltpu.roll(y_below[kind, m], 1, 0)
                seen.append(jnp.where(row == 0, halo, moved))
            for kind in range(2):
                halo = y_high[kind * 7 + m // 4]
                halo = pltpu.roll(halo, 3 - q, 0) if q < 3 else halo
                moved = pltpu.roll(y_above[kind, m], 7, 0)
                seen.append(jnp.where(row == 3, halo, moved))
            parts = neighbour_line(*seen)
            for n in range(MODES):
                value, slope = parts[n % 2]
                add = float(NORMED[n]) * value
                add = add + float(SLOPE[n]) * slope if n else add
                out[i, n, e] = local[i, n, e] + add
    z_low_halo = z_has_low * jnp.where(z_even, z_b[...], z_a[...])
    z_high_halo = z_has_high * jnp.where(z_even, z_a[...], z_b[...])
    for i in range(PAIRS):
        for b in range(MODES):
            m = i * MODES + b
            seen = []
            for kind in range(2):
                place = 2 * m + kind
                halo = pltpu.roll(z_low_halo, 128 - place, 1) if place else z_low_halo
                moved = pltpu.roll(z_below[kind, m], 1, 1)
                seen.append(jnp.where(lane == 0, halo, moved))
            for kind in range(2):
                place = 2 * m + kind
                halo = pltpu.roll(z_high_halo, 127 - place, 1)
                moved = pltpu.roll(z_above[kind, m], 127, 1)
                seen.append(jnp.where(lane == 127, halo, moved))
            parts = neighbour_line(*seen)
            for e in range(MODES):
                value, slope = parts[e % 2]
                add = float(NORMED[e]) * value
                if e:
                    add = add + float(SLOPE[e]) * slope
                out[i, b, e] += add


def finish_kernel(first, local, orders, x_a, x_b, field, parts):
    pairs = Pairs()
    top = pairs.top
    row, lane = row_in_half(), lanes()
    keep = keep_masks(orders[0], top)
    has_low, has_high = has_place("gx", -1), has_place("gx", 1)
    upward = goes_up(x_turn())
    one_valid = jnp.where(upward, has_high, has_low)
    two_valid = jnp.where(upward, has_low, has_high)
    x_sign = jnp.where(upward, 1.0, -1.0)
    x_even = goes_up(lax.axis_index("gx"))
    for b in range(MODES):
        for e in range(MODES):
            one, two = one_valid * x_a[b * MODES + e], two_valid * x_b[b * MODES + e]
            plus, minus = one + two, swap(x_sign * (one - two))
            slope = 0.5 * jnp.where(top, plus, minus)
            value = (-2.0 * PENALTY) * slope - 0.5 * jnp.where(top, minus, plus)
            for i in range(PAIRS):
                last = 2 * i + 1 >= MODES
                k = odd_of(i)
                applied = local[i, b, e] + (
                    pairs(NORMED[2 * i], 0.0 if last else NORMED[k]) * value
                    + pairs(SLOPE[2 * i], 0.0 if last else SLOPE[k]) * slope
                )
                one = 2.0 * RHO_SECOND / (DELTA * PENALTY)
                scale = pairs.once(one / diag(2 * i, b, e), one / diag(odd_of(i), b, e))
                mask = keep(max(2 * i, b, e), max(odd_of(i), b, e))
                kappa = 1.0 + RHO_SECOND * RHO_FIRST + 2.0 * RHO_SECOND * THETA / DELTA
                after = kappa * first[i, b, e] - (mask * scale) * applied
                field[i, b, e] = after

    grid = {}

    def add(key, value):
        grid[key] = grid[key] + value if key in grid else value

    spread = -SPREAD / PENALTY
    for e in range(MODES):
        low, high = vertex_pair(field[0, 0, e], field[0, 1, e])
        for dz in range(-1, 3):
            add((0, dz), float(spread[dz + 1, e]) * low)
            add((1, dz), float(spread[dz + 1, e]) * high)
    for b in range(MODES):
        low, high = vertex_pair(field[0, b, 0], field[0, b, 1])
        for dy in range(-1, 3):
            add((dy, 0), float(spread[dy + 1, b]) * low)
            add((dy, 1), float(spread[dy + 1, b]) * high)
    force = [
        [
            pairs.once(THETA * diag(0, b, e), THETA * diag(1, b, e)) * first[0, b, e]
            for e in range(2)
        ]
        for b in range(2)
    ]
    force = [vertex_pair(force[0][e], force[1][e]) for e in range(2)]
    for dy in range(2):
        low, high = vertex_pair(force[0][dy], force[1][dy])
        add((dy, 0), low)
        add((dy, 1), high)
    kept, turned = pairs(ROOT_HALF, THIRD), pairs(-THIRD, ROOT_HALF)
    near = {key: kept * value + turned * swap(value) for key, value in grid.items()}
    outer = {}
    corners = []
    for i in range(PAIRS):
        line = [vertex_pair(field[i, 0, e], field[i, 1, e]) for e in range(2)]
        corners.append([vertex_pair(line[0][dy], line[1][dy]) for dy in range(2)])
    for dy in range(2):
        for dz in range(2):
            sums = []
            for dx in range(-1, 3):
                part = total(
                    pairs(
                        spread[dx + 1, 2 * i],
                        spread[dx + 1, 2 * i + 1] if 2 * i + 1 < MODES else 0.0,
                    )
                    * corners[i][dy][dz]
                    for i in range(PAIRS)
                )
                sums.append(part + swap(part))
            near[dy, dz] += jnp.where(top, sums[1], sums[2])
            outer[dy, dz] = jnp.where(top, sums[0], sums[3])
    near = sum_to_vertices(near, pairs, row, lane)
    outer = sum_to_vertices(outer, pairs, row, lane)
    for z in range(2):
        parts[0, z] = jnp.where(top, near[0][z], swap(near[1][z]))
        ahead = jnp.where(top, swap(near[0][z]), near[1][z])
        behind = jnp.where(top, outer[0][z], swap(outer[1][z]))
        parts[1, z] = jnp.where(x_even, ahead, behind)
        parts[2, z] = jnp.where(x_even, behind, ahead)
        parts[3, z] = jnp.where(top, swap(outer[0][z]), outer[1][z])


def unpack_kernel(field, here, smoothed, here_again):
    here_again[...] = here[...]
    for b in range(MODES):
        for e in range(MODES):
            for i in range(PAIRS):
                value = field[i, b, e]
                smoothed[2 * i, b, e, 0] = value[:4]
                if 2 * i + 1 < MODES:
                    smoothed[2 * i + 1, b, e, 0] = value[4:]


def column_kernel(chip, third, fetched, mated, column, blocks):
    count = lax.axis_size("gz")
    me = lax.axis_index("gz")
    core, place = lax.rem(me, 2), lax.div(me, 2)
    beside = place + 1 - 2 * lax.rem(place, 2)
    across = lax.rem(place + 2, 4)
    mirrored = 3 - place
    asked = mirrored + core * (across - mirrored)
    zero = jnp.zeros((8, 128), jnp.float32)
    blocks[0] = zero
    blocks[count + 1] = zero
    for source, sender, pair in (
        (place, core, chip),
        (asked, core, fetched),
        (mirrored + across - asked, 1 - core, mated),
        (beside, core, third),
    ):
        blocks[2 * source + sender + 1] = pair[0]
        blocks[2 * source + 2 - sender] = pair[1]
    lane = lax.broadcasted_iota(jnp.int32, (4, 128), 1)
    row = lax.broadcasted_iota(jnp.int32, (4, 128), 0)
    interior = (lax.axis_index("gx") > 0) & (lax.axis_index("gy") * 4 + row > 0)
    for k in range(count):
        value = (
            blocks[k + 1, :4]
            + jnp.where(lane < 2, blocks[k, 4:], 0.0)
            + jnp.where(lane == 127, blocks[k + 2, 4:], 0.0)
        )
        here = interior & (lane > 0) if k == 0 else interior
        column[0, :, k * 128 : (k + 1) * 128] = jnp.where(here, value, 0.0)


def shape(*dims):
    return jax.ShapeDtypeStruct(dims, jnp.float32)


def in_vmem(count):
    return [pl.BlockSpec(memory_space=pltpu.VMEM)] * count


def call(kernel, name, inputs, outputs, flops, scratch=(), in_hbm=False):
    size = sum(4 * int(np.prod(v.shape)) for v in (*inputs, *outputs))
    space = pltpu.HBM if in_hbm else pltpu.VMEM
    return pl.pallas_call(
        kernel,
        out_shape=outputs,
        in_specs=[pl.BlockSpec(memory_space=space)] * len(inputs),
        out_specs=[pl.BlockSpec(memory_space=pltpu.VMEM)] * len(outputs),
        scratch_shapes=list(scratch),
        name=name,
        cost_estimate=pl.CostEstimate(flops=flops, bytes_accessed=size, transcendentals=0),
        compiler_params=pltpu.CompilerParams(vmem_limit_bytes=24 * 1024 * 1024),
    )(*inputs)


def flip(value, axis, bits):
    return lax.ppermute(value, axis, [(i, i ^ bits) for i in range(lax.axis_size(axis))])


def exchange(value, partner):
    axes = ("gx", "gy", "gz")
    sizes = [lax.axis_size(name) for name in axes]
    route = [
        (source, int(np.ravel_multi_index(partner(list(place)), sizes)))
        for source, place in enumerate(np.ndindex(*sizes))
    ]
    return lax.ppermute(value, axes, route)


def second_of_pair(place, k, count, spare, bit):
    if place[k] in (0, count - 1):
        place[spare] ^= bit
    else:
        place[k] += 1 if place[k] % 2 else -1
    return place


def second_pairs(value, axis):
    k, count = ("gx", "gy", "gz").index(axis), lax.axis_size(axis)
    return exchange(value, lambda place: second_of_pair(place, k, count, 0 if k == 2 else 2, 1))


def x_pairs(value, turn):
    count = lax.axis_size("gx")

    def partner(place):
        if place[2] % 2 == turn:
            place[0] ^= 1
            return place
        return second_of_pair(place, 0, count, 1, 1)

    return exchange(value, partner)


def far_or_beside(value):
    def partner(place):
        place[0] ^= 2 if place[2] % 2 else 1
        return place

    return exchange(value, partner)


def both_y_sides(value):
    count = lax.axis_size("gy")

    def partner(place):
        if place[2] % 2:
            return second_of_pair(place, 1, count, 0, 1)
        place[1] ^= 1
        return place

    return exchange(value, partner)


def two_chips(value):
    def partner(place):
        place[2] ^= 4 if place[2] % 2 else 6
        return place

    return exchange(value, partner)


def inside(axis, distance):
    place = lax.axis_index(axis) + distance
    return ((place >= 0) & (place < lax.axis_size(axis))).astype(jnp.float32)


def per_device(rhs, orders):
    cells = (PAIRS, MODES, MODES, 8, 128)
    sides = (shape(2, 28, 8, 128),) * 4
    first, x_a, x_b, held = call(
        trace_kernel,
        "x_traces",
        tuple(pltpu.with_memory_space_constraint(v, pltpu.HBM) for v in (rhs, orders)),
        (
            shape(*cells), shape(49, 8, 128), shape(49, 8, 128),
            jax.ShapeDtypeStruct(orders.shape, jnp.int32),
        ),
        4_000_000,
        scratch=(pltpu.VMEM(rhs.shape, jnp.float32), pltpu.SemaphoreType.DMA((MODES + 1,))),
        in_hbm=True,
    )
    x_a, x_b = x_pairs(x_a, 0), x_pairs(x_b, 1)
    y_a, y_b, z_a, z_b, y_low, y_high, z_low, z_high = call(
        side_trace_kernel,
        "side_traces",
        (first,),
        (shape(FACE_ROWS, 8, 128),) * 2 + (shape(8, 128),) * 2 + sides,
        SIDE_COST,
    )
    y_a, y_b = flip(y_a, "gy", 1), second_pairs(y_b, "gy")
    z_b = second_pairs(z_b, "gz")
    z_a = flip(z_a, "gz", 1)
    local, y_a = call(
        own_kernel, "own_cells", (first, y_a), (shape(*cells), shape(FACE_ROWS, 8, 128)), OWN_COST
    )
    (local,) = call(
        side_kernel,
        "side_halo",
        (local, y_a, y_b, z_b, z_a, y_high, y_low, z_high, z_low),
        (shape(*cells),),
        HALO_COST,
    )
    field, parts = call(
        finish_kernel,
        "smooth_and_restrict",
        (first, local, held, x_a, x_b),
        (shape(*cells), shape(4, 2, 8, 128)),
        5_000_000,
    )
    count = lax.axis_size("gz")
    both = jnp.stack([parts, flip(parts, "gz", 1)])
    first_core = lax.axis_index("gz") % 2 == 0
    from_two = second_pairs(both[:, 2], "gx")
    from_one = far_or_beside(jnp.where(first_core, both[:, 1], both[:, 3]))
    smoothed, here = call(
        unpack_kernel,
        "unpack_modes",
        (field, both[:, 0]),
        (shape(*rhs.shape), shape(2, 2, 8, 128)),
        200_000,
    )
    sums = (
        jnp.where(first_core, 0.0, inside("gx", -1) * inside("gx", 1)) * from_two
        + jnp.where(first_core, 1.0, inside("gx", -2)) * from_one
        + jnp.where(first_core, 0.0, here)
    )
    chip = sums + flip(sums, "gz", 1)[::-1]
    from_beside = both_y_sides(chip[:, :, 4:].reshape(2, 8, 128)).reshape(2, 2, 4, 128)
    from_low = (lax.axis_index("gy") + lax.axis_index("gz")) % 2 == 1
    row = lax.broadcasted_iota(jnp.int32, (1, 1, 4, 1), 2)
    wanted = jnp.where(from_low, row < 2, row == 3)
    valid = jnp.where(from_low, inside("gy", -1), inside("gy", 1))
    edges = jnp.where(wanted, from_beside, 0.0) * valid
    edges = edges.reshape(2, 8, 128)
    mated = flip(edges, "gz", 1)
    owned = chip[:, :, :4].reshape(2, 8, 128) + edges + mated[::-1]
    third = flip(owned, "gz", 2)
    fetched = two_chips(owned)
    (column,) = call(
        column_kernel,
        "column",
        (owned, third, fetched, flip(fetched, "gz", 1)),
        (shape(1, 4, 128 * count),),
        20_000,
        scratch=(pltpu.VMEM((count + 2, 8, 128), jnp.float32),),
    )
    return smoothed, column


def solution(mesh):
    return jax.shard_map(
        per_device,
        mesh=mesh,
        in_specs=(P(None, None, None, "gx", "gy", "gz"), P("gx", "gy", "gz")),
        out_specs=(P(None, None, None, "gx", "gy", "gz"), P("gx", "gy", None)),
        check_vma=False,
    )
```

```python
import jax
import jax.numpy as jnp
import numpy as np
from jax import lax
from jax.experimental import pallas as pl
from jax.experimental.pallas import tpu as pltpu
from jax.sharding import PartitionSpec as P

PENALTY = 49.0
EIGEN_HIGH = 2.4
EIGEN_LOW = 0.24
THETA = 0.5 * (EIGEN_HIGH + EIGEN_LOW)
DELTA = 0.5 * (EIGEN_HIGH - EIGEN_LOW)
RHO_FIRST = DELTA / THETA
RHO_SECOND = 1.0 / (2.0 * THETA / DELTA - RHO_FIRST)
MODES = 7
PAIRS = 4
FACE_ROWS = 14
SIDE_COST = 4_000_000
OWN_COST = 1_400_000_000
HALO_COST = 4_000_000


def basis_tables():
    degree = np.arange(MODES)
    normed = np.sqrt((2.0 * degree + 1.0) / 2.0)
    smaller = np.minimum(degree[:, None], degree[None, :])
    parity = (degree[:, None] + degree[None, :]) % 2 == 0
    stiffness = np.where(parity, normed[:, None] * normed[None, :] * smaller * (smaller + 1), 0.0)
    signs = (-1.0) ** degree
    slope = normed * degree * (degree + 1) / 2.0
    high, high_slope = normed, slope
    low, low_slope = normed * signs, -slope * signs
    own = (
        stiffness
        + PENALTY * (np.outer(high, high) + np.outer(low, low))
        - 0.5 * (np.outer(high, high_slope) + np.outer(high_slope, high))
        + 0.5 * (np.outer(low, low_slope) + np.outer(low_slope, low))
    )
    own = np.where(parity, own, 0.0)
    to_next = np.outer(low, 0.5 * high_slope - PENALTY * high) - 0.5 * np.outer(low_slope, high)
    to_last = np.outer(high, -PENALTY * low - 0.5 * low_slope) + 0.5 * np.outer(high_slope, low)
    one_axis = normed * normed * degree * (degree + 1) + 2.0 * (
        PENALTY * normed * normed - normed * slope
    )
    third = np.sqrt(1.5) / 3.0
    vertex = np.zeros((MODES, 2))
    vertex[0] = np.sqrt(0.5)
    vertex[1] = -third, third
    spread = np.stack(
        [
            vertex[:, 0] @ to_last,
            vertex[:, 1] @ to_last + vertex[:, 0] @ own,
            vertex[:, 1] @ own + vertex[:, 0] @ to_next,
            vertex[:, 1] @ to_next,
        ]
    )
    return normed, slope, own, one_axis, spread, third


NORMED, SLOPE, OWN, ONE_AXIS, SPREAD, THIRD = basis_tables()
ROOT_HALF = float(np.sqrt(0.5))


def diag(a, b, e):
    return float((ONE_AXIS[a] + ONE_AXIS[b] + ONE_AXIS[e]) / PENALTY)


def half_mask():
    return lax.broadcasted_iota(jnp.int32, (8, 128), 0) < 4


def row_in_half():
    return lax.broadcasted_iota(jnp.int32, (8, 128), 0) % 4


def lanes():
    return lax.broadcasted_iota(jnp.int32, (8, 128), 1)


def swap(value):
    return pltpu.roll(value, 4, 0)


class Pairs:
    def __init__(self):
        self.top = half_mask()
        self.known = {}

    def __call__(self, upper, lower):
        key = (float(upper), float(lower))
        if key[0] == key[1]:
            return jnp.float32(key[0])
        if key not in self.known:
            self.known[key] = jnp.where(self.top, jnp.float32(key[0]), jnp.float32(key[1]))
        return self.known[key]

    def once(self, upper, lower):
        if float(upper) == float(lower):
            return jnp.float32(upper)
        return jnp.where(self.top, jnp.float32(upper), jnp.float32(lower))


def total(terms):
    terms = list(terms)
    while len(terms) > 1:
        terms = [
            terms[k] + terms[k + 1] if k + 1 < len(terms) else terms[k]
            for k in range(0, len(terms), 2)
        ]
    return terms[0]


def keep_masks(orders, top):
    both = jnp.concatenate([orders, orders], axis=0)
    known = {}

    def get(upper, lower):
        if (upper, lower) not in known:
            if upper == lower:
                bound = jnp.int32(upper)
            else:
                bound = jnp.where(top, jnp.int32(upper), jnp.int32(lower))
            known[upper, lower] = (both >= bound).astype(jnp.float32)
        return known[upper, lower]

    return get


def odd_of(pair):
    return min(2 * pair + 1, MODES - 1)


def line_traces(line):
    even = total(float(NORMED[n]) * line[n] for n in range(0, MODES, 2))
    odd = total(float(NORMED[n]) * line[n] for n in range(1, MODES, 2))
    even_slope = total(float(SLOPE[n]) * line[n] for n in range(2, MODES, 2))
    odd_slope = total(float(SLOPE[n]) * line[n] for n in range(1, MODES, 2))
    return even + odd, even_slope + odd_slope, even - odd, odd_slope - even_slope


def x_turn():
    return lax.axis_index("gx") + lax.axis_index("gz")


def goes_up(turn):
    return jnp.full((8, 128), lax.rem(turn, 2), jnp.int32) == 0


def has_place(axis, distance):
    place = lax.axis_index(axis) + distance
    return jnp.where((place >= 0) & (place < lax.axis_size(axis)), 1.0, 0.0).astype(jnp.float32)


def trace_kernel(
    rhs_hbm, orders_hbm, first, x_a, x_b, orders, rhs, arrived,
):
    copies = [pltpu.make_async_copy(orders_hbm, orders, arrived.at[MODES])]
    for b in range(MODES):
        copies.append(pltpu.make_async_copy(rhs_hbm.at[:, b], rhs.at[:, b], arrived.at[b]))
    for copy in copies:
        copy.start()
    pairs = Pairs()
    top = pairs.top
    upward = goes_up(x_turn())
    copies[0].wait()
    keep = keep_masks(orders[0], top)
    for b in range(MODES):
        copies[1 + b].wait()
        for e in range(MODES):
            column = []
            for i in range(PAIRS):
                upper = rhs[2 * i, b, e, 0]
                lower = rhs[2 * i + 1, b, e, 0] if 2 * i + 1 < MODES else jnp.zeros_like(upper)
                cell = jnp.concatenate([upper, lower], axis=0)
                mask = keep(max(2 * i, b, e), max(odd_of(i), b, e))
                scale = pairs.once(
                    1.0 / (THETA * diag(2 * i, b, e)), 1.0 / (THETA * diag(odd_of(i), b, e))
                )
                cell = cell * mask * scale
                first[i, b, e] = cell
                column.append(cell)
            odd = [odd_of(i) if 2 * i + 1 < MODES else None for i in range(PAIRS)]
            value = total(
                pairs(NORMED[2 * i], NORMED[odd[i]] if odd[i] else 0.0) * column[i]
                for i in range(PAIRS)
            )
            slope = total(
                pairs(SLOPE[2 * i], SLOPE[odd[i]] if odd[i] else 0.0) * column[i]
                for i in range(PAIRS)
            )
            both_value = jnp.where(top, value + swap(value), swap(value) - value)
            both_slope = jnp.where(top, slope + swap(slope), slope - swap(slope))
            up = jnp.where(top, both_value, swap(both_slope))
            down = jnp.where(top, swap(both_value), both_slope)
            x_a[b * MODES + e] = jnp.where(upward, up, down)
            x_b[b * MODES + e] = jnp.where(upward, down, up)


def side_trace_kernel(first, y_a, y_b, z_a, z_b, y_low, y_high, z_low, z_high):
    row, lane = row_in_half(), lanes()
    y_up, z_up = goes_up(lax.axis_index("gy")), goes_up(lax.axis_index("gz"))
    packed_up = packed_down = None
    for kind in range(2):
        for i in range(PAIRS):
            for e in range(MODES):
                m = i * MODES + e
                q = m % 4
                line = [first[i, b, e] for b in range(MODES)]
                traces = line_traces(line)
                high, low = traces[kind], traces[2 + kind]
                y_high[kind, m] = high
                y_low[kind, m] = low
                up, down = pltpu.roll(high, 5 + q, 0), pltpu.roll(low, q, 0) if q else low
                packed_up = up if q == 0 else jnp.where(row == q, up, packed_up)
                packed_down = down if q == 0 else jnp.where(row == q, down, packed_down)
                if q == 3:
                    k = kind * 7 + m // 4
                    y_a[k] = jnp.where(y_up, packed_up, packed_down)
                    y_b[k] = jnp.where(y_up, packed_down, packed_up)
    packed_up = packed_down = jnp.zeros((8, 128), jnp.float32)
    for i in range(PAIRS):
        for b in range(MODES):
            m = i * MODES + b
            line = [first[i, b, e] for e in range(MODES)]
            traces = line_traces(line)
            for kind in range(2):
                high, low = traces[kind], traces[2 + kind]
                z_high[kind, m] = high
                z_low[kind, m] = low
                place = 2 * m + kind
                packed_up = jnp.where(lane == place, pltpu.roll(high, 1 + place, 1), packed_up)
                down = pltpu.roll(low, place, 1) if place else low
                packed_down = jnp.where(lane == place, down, packed_down)
    z_a[...] = jnp.where(z_up, packed_up, packed_down)
    z_b[...] = jnp.where(z_up, packed_down, packed_up)


def own_kernel(first, early, out, early_again):
    early_again[...] = early[...]
    pairs = Pairs()
    for b in range(MODES):
        for e in range(MODES):
            column = [first[i, b, e] for i in range(PAIRS)]
            for i in range(PAIRS):
                terms = []
                for j in range(PAIRS):
                    lower = OWN[2 * i + 1, 2 * j + 1] if max(i, j) < 3 else 0.0
                    terms.append(pairs(OWN[2 * i, 2 * j], lower) * column[j])
                out[i, b, e] = total(terms)
    for i in range(PAIRS):
        for b in range(MODES):
            line = [first[i, b, e] for e in range(MODES)]
            for n in range(MODES):
                out[i, b, n] += total(
                    float(OWN[n, k]) * line[k] for k in range(n % 2, MODES, 2)
                )
        for e in range(MODES):
            line = [first[i, b, e] for b in range(MODES)]
            for n in range(MODES):
                out[i, n, e] += total(
                    float(OWN[n, k]) * line[k] for k in range(n % 2, MODES, 2)
                )


def neighbour_line(low_value, low_slope, high_value, high_slope):
    plus, minus = high_value + low_value, high_value - low_value
    even = 0.5 * (low_slope - high_slope) - PENALTY * plus
    odd = -0.5 * (low_slope + high_slope) - PENALTY * minus
    return (even, 0.5 * plus), (odd, 0.5 * minus)


def vertex_pair(first_mode, second_mode):
    base, tilt = ROOT_HALF * first_mode, THIRD * second_mode
    return base - tilt, base + tilt


def sum_to_vertices(grid, pairs, row, lane):
    top = pairs.top
    rows = {}
    for (dy, dz), value in grid.items():
        rows.setdefault(dy, []).append((dz, value))
    result = [[[], []], [[], []]]
    for dy, entries in rows.items():
        inner, outer = [], []
        for dz, value in entries:
            if dz == 0:
                inner.append(value)
                continue
            moved = pltpu.roll(value, dz % 128, 1)
            inside = lane >= dz if dz > 0 else lane < 128 + dz
            inner.append(jnp.where(inside, moved, 0.0))
            outer.append(jnp.where(inside, 0.0, moved))
        for beyond, terms in ((0, inner), (1, outer)):
            if not terms:
                continue
            value = total(terms)
            if dy == 0:
                result[0][beyond].append(value)
                continue
            moved = pltpu.roll(value, dy % 8, 0)
            inside = row >= dy if dy > 0 else row < 4 + dy
            result[0][beyond].append(jnp.where(inside, moved, 0.0))
            result[1][beyond].append(jnp.where(inside, 0.0, swap(moved)))
    return [[total(result[r][z]) for z in range(2)] for r in range(2)]


def side_kernel(
    local, y_a, y_b, z_b, z_a, y_below, y_above, z_below, z_above, out
):
    row, lane = row_in_half(), lanes()
    y_even, z_even = goes_up(lax.axis_index("gy")), goes_up(lax.axis_index("gz"))
    y_has_low, y_has_high = has_place("gy", -1), has_place("gy", 1)
    z_has_low, z_has_high = has_place("gz", -1), has_place("gz", 1)
    y_low, y_high = [], []
    for k in range(FACE_ROWS):
        one, two = y_a[k], y_b[k]
        y_low.append(y_has_low * jnp.where(y_even, two, one))
        y_high.append(y_has_high * jnp.where(y_even, one, two))
    for i in range(PAIRS):
        for e in range(MODES):
            m = i * MODES + e
            q = m % 4
            seen = []
            for kind in range(2):
                halo = y_low[kind * 7 + m // 4]
                halo = pltpu.roll(halo, 8 - q, 0) if q else halo
                moved = pltpu.roll(y_below[kind, m], 1, 0)
                seen.append(jnp.where(row == 0, halo, moved))
            for kind in range(2):
                halo = y_high[kind * 7 + m // 4]
                halo = pltpu.roll(halo, 3 - q, 0) if q < 3 else halo
                moved = pltpu.roll(y_above[kind, m], 7, 0)
                seen.append(jnp.where(row == 3, halo, moved))
            parts = neighbour_line(*seen)
            for n in range(MODES):
                value, slope = parts[n % 2]
                add = float(NORMED[n]) * value
                add = add + float(SLOPE[n]) * slope if n else add
                out[i, n, e] = local[i, n, e] + add
    z_low_halo = z_has_low * jnp.where(z_even, z_b[...], z_a[...])
    z_high_halo = z_has_high * jnp.where(z_even, z_a[...], z_b[...])
    for i in range(PAIRS):
        for b in range(MODES):
            m = i * MODES + b
            seen = []
            for kind in range(2):
                place = 2 * m + kind
                halo = pltpu.roll(z_low_halo, 128 - place, 1) if place else z_low_halo
                moved = pltpu.roll(z_below[kind, m], 1, 1)
                seen.append(jnp.where(lane == 0, halo, moved))
            for kind in range(2):
                place = 2 * m + kind
                halo = pltpu.roll(z_high_halo, 127 - place, 1)
                moved = pltpu.roll(z_above[kind, m], 127, 1)
                seen.append(jnp.where(lane == 127, halo, moved))
            parts = neighbour_line(*seen)
            for e in range(MODES):
                value, slope = parts[e % 2]
                add = float(NORMED[e]) * value
                if e:
                    add = add + float(SLOPE[e]) * slope
                out[i, b, e] += add


def finish_kernel(first, local, orders, x_a, x_b, field, here, parts):
    pairs = Pairs()
    top = pairs.top
    row, lane = row_in_half(), lanes()
    keep = keep_masks(orders[0], top)
    has_low, has_high = has_place("gx", -1), has_place("gx", 1)
    upward = goes_up(x_turn())
    one_valid = jnp.where(upward, has_high, has_low)
    two_valid = jnp.where(upward, has_low, has_high)
    x_sign = jnp.where(upward, 1.0, -1.0)
    x_even = goes_up(lax.axis_index("gx"))
    for b in range(MODES):
        for e in range(MODES):
            one, two = one_valid * x_a[b * MODES + e], two_valid * x_b[b * MODES + e]
            plus, minus = one + two, swap(x_sign * (one - two))
            slope = 0.5 * jnp.where(top, plus, minus)
            value = (-2.0 * PENALTY) * slope - 0.5 * jnp.where(top, minus, plus)
            for i in range(PAIRS):
                last = 2 * i + 1 >= MODES
                k = odd_of(i)
                applied = local[i, b, e] + (
                    pairs(NORMED[2 * i], 0.0 if last else NORMED[k]) * value
                    + pairs(SLOPE[2 * i], 0.0 if last else SLOPE[k]) * slope
                )
                one = 2.0 * RHO_SECOND / (DELTA * PENALTY)
                scale = pairs.once(one / diag(2 * i, b, e), one / diag(odd_of(i), b, e))
                mask = keep(max(2 * i, b, e), max(odd_of(i), b, e))
                kappa = 1.0 + RHO_SECOND * RHO_FIRST + 2.0 * RHO_SECOND * THETA / DELTA
                after = kappa * first[i, b, e] - (mask * scale) * applied
                field[i, b, e] = after

    grid = {}

    def add(key, value):
        grid[key] = grid[key] + value if key in grid else value

    spread = -SPREAD / PENALTY
    for e in range(MODES):
        low, high = vertex_pair(field[0, 0, e], field[0, 1, e])
        for dz in range(-1, 3):
            add((0, dz), float(spread[dz + 1, e]) * low)
            add((1, dz), float(spread[dz + 1, e]) * high)
    for b in range(MODES):
        low, high = vertex_pair(field[0, b, 0], field[0, b, 1])
        for dy in range(-1, 3):
            add((dy, 0), float(spread[dy + 1, b]) * low)
            add((dy, 1), float(spread[dy + 1, b]) * high)
    force = [
        [
            pairs.once(THETA * diag(0, b, e), THETA * diag(1, b, e)) * first[0, b, e]
            for e in range(2)
        ]
        for b in range(2)
    ]
    force = [vertex_pair(force[0][e], force[1][e]) for e in range(2)]
    for dy in range(2):
        low, high = vertex_pair(force[0][dy], force[1][dy])
        add((dy, 0), low)
        add((dy, 1), high)
    kept, turned = pairs(ROOT_HALF, THIRD), pairs(-THIRD, ROOT_HALF)
    near = {key: kept * value + turned * swap(value) for key, value in grid.items()}
    outer = {}
    corners = []
    for i in range(PAIRS):
        line = [vertex_pair(field[i, 0, e], field[i, 1, e]) for e in range(2)]
        corners.append([vertex_pair(line[0][dy], line[1][dy]) for dy in range(2)])
    for dy in range(2):
        for dz in range(2):
            sums = []
            for dx in range(-1, 3):
                part = total(
                    pairs(
                        spread[dx + 1, 2 * i],
                        spread[dx + 1, 2 * i + 1] if 2 * i + 1 < MODES else 0.0,
                    )
                    * corners[i][dy][dz]
                    for i in range(PAIRS)
                )
                sums.append(part + swap(part))
            near[dy, dz] += jnp.where(top, sums[1], sums[2])
            outer[dy, dz] = jnp.where(top, sums[0], sums[3])
    near = sum_to_vertices(near, pairs, row, lane)
    outer = sum_to_vertices(outer, pairs, row, lane)
    for z in range(2):
        here[z] = jnp.where(top, near[0][z], swap(near[1][z]))
        ahead = jnp.where(top, swap(near[0][z]), near[1][z])
        behind = jnp.where(top, outer[0][z], swap(outer[1][z]))
        parts[0, z] = jnp.where(x_even, ahead, behind)
        parts[1, z] = jnp.where(x_even, behind, ahead)
        parts[2, z] = jnp.where(top, swap(outer[0][z]), outer[1][z])


def unpack_kernel(field, here, smoothed, here_again):
    here_again[...] = here[...]
    for b in range(MODES):
        for e in range(MODES):
            for i in range(PAIRS):
                value = field[i, b, e]
                smoothed[2 * i, b, e, 0] = value[:4]
                if 2 * i + 1 < MODES:
                    smoothed[2 * i + 1, b, e, 0] = value[4:]


def column_kernel(chip, third, fetched, mated, column, blocks):
    count = lax.axis_size("gz")
    me = lax.axis_index("gz")
    core, place = lax.rem(me, 2), lax.div(me, 2)
    beside = place + 1 - 2 * lax.rem(place, 2)
    across = lax.rem(place + 2, 4)
    asked = beside + core * (across - beside)
    zero = jnp.zeros((8, 128), jnp.float32)
    blocks[0] = zero
    blocks[count + 1] = zero
    for source, sender, pair in (
        (place, core, chip),
        (asked, core, fetched),
        (beside + across - asked, 1 - core, mated),
        (3 - place, core, third),
    ):
        blocks[2 * source + sender + 1] = pair[0]
        blocks[2 * source + 2 - sender] = pair[1]
    lane = lax.broadcasted_iota(jnp.int32, (4, 128), 1)
    row = lax.broadcasted_iota(jnp.int32, (4, 128), 0)
    interior = (lax.axis_index("gx") > 0) & (lax.axis_index("gy") * 4 + row > 0)
    for k in range(count):
        value = (
            blocks[k + 1, :4]
            + jnp.where(lane < 2, blocks[k, 4:], 0.0)
            + jnp.where(lane == 127, blocks[k + 2, 4:], 0.0)
        )
        here = interior & (lane > 0) if k == 0 else interior
        column[0, :, k * 128 : (k + 1) * 128] = jnp.where(here, value, 0.0)


def shape(*dims):
    return jax.ShapeDtypeStruct(dims, jnp.float32)


def in_vmem(count):
    return [pl.BlockSpec(memory_space=pltpu.VMEM)] * count


def call(kernel, name, inputs, outputs, flops, scratch=(), in_hbm=False):
    size = sum(4 * int(np.prod(v.shape)) for v in (*inputs, *outputs))
    space = pltpu.HBM if in_hbm else pltpu.VMEM
    return pl.pallas_call(
        kernel,
        out_shape=outputs,
        in_specs=[pl.BlockSpec(memory_space=space)] * len(inputs),
        out_specs=[pl.BlockSpec(memory_space=pltpu.VMEM)] * len(outputs),
        scratch_shapes=list(scratch),
        name=name,
        cost_estimate=pl.CostEstimate(flops=flops, bytes_accessed=size, transcendentals=0),
        compiler_params=pltpu.CompilerParams(vmem_limit_bytes=24 * 1024 * 1024),
    )(*inputs)


def flip(value, axis, bits):
    return lax.ppermute(value, axis, [(i, i ^ bits) for i in range(lax.axis_size(axis))])


def exchange(value, partner):
    axes = ("gx", "gy", "gz")
    sizes = [lax.axis_size(name) for name in axes]
    route = [
        (source, int(np.ravel_multi_index(partner(list(place)), sizes)))
        for source, place in enumerate(np.ndindex(*sizes))
    ]
    return lax.ppermute(value, axes, route)


def second_of_pair(place, k, count, spare, bit):
    if place[k] in (0, count - 1):
        place[spare] ^= bit
    else:
        place[k] += 1 if place[k] % 2 else -1
    return place


def second_pairs(value, axis):
    k, count = ("gx", "gy", "gz").index(axis), lax.axis_size(axis)
    return exchange(value, lambda place: second_of_pair(place, k, count, 0 if k == 2 else 2, 1))


def x_pairs(value, turn):
    count = lax.axis_size("gx")

    def partner(place):
        if place[2] % 2 == turn:
            place[0] ^= 1
            return place
        return second_of_pair(place, 0, count, 1, 1)

    return exchange(value, partner)


def far_or_beside(value):
    def partner(place):
        place[0] ^= 2 if place[2] % 2 else 1
        return place

    return exchange(value, partner)


def both_y_sides(value):
    count = lax.axis_size("gy")

    def partner(place):
        if place[2] % 2:
            return second_of_pair(place, 1, count, 0, 1)
        place[1] ^= 1
        return place

    return exchange(value, partner)


def two_chips(value):
    def partner(place):
        place[2] ^= 4 if place[2] % 2 else 2
        return place

    return exchange(value, partner)


def inside(axis, distance):
    place = lax.axis_index(axis) + distance
    return ((place >= 0) & (place < lax.axis_size(axis))).astype(jnp.float32)


def per_device(rhs, orders):
    cells = (PAIRS, MODES, MODES, 8, 128)
    sides = (shape(2, 28, 8, 128),) * 4
    first, x_a, x_b, held = call(
        trace_kernel,
        "x_traces",
        tuple(pltpu.with_memory_space_constraint(v, pltpu.HBM) for v in (rhs, orders)),
        (
            shape(*cells), shape(49, 8, 128), shape(49, 8, 128),
            jax.ShapeDtypeStruct(orders.shape, jnp.int32),
        ),
        4_000_000,
        scratch=(pltpu.VMEM(rhs.shape, jnp.float32), pltpu.SemaphoreType.DMA((MODES + 1,))),
        in_hbm=True,
    )
    x_a, x_b = x_pairs(x_a, 0), x_pairs(x_b, 1)
    y_a, y_b, z_a, z_b, y_low, y_high, z_low, z_high = call(
        side_trace_kernel,
        "side_traces",
        (first,),
        (shape(FACE_ROWS, 8, 128),) * 2 + (shape(8, 128),) * 2 + sides,
        SIDE_COST,
    )
    y_a, y_b = flip(y_a, "gy", 1), second_pairs(y_b, "gy")
    z_b = second_pairs(z_b, "gz")
    z_a = flip(z_a, "gz", 1)
    local, y_a = call(
        own_kernel, "own_cells", (first, y_a), (shape(*cells), shape(FACE_ROWS, 8, 128)), OWN_COST
    )
    (local,) = call(
        side_kernel,
        "side_halo",
        (local, y_a, y_b, z_b, z_a, y_high, y_low, z_high, z_low),
        (shape(*cells),),
        HALO_COST,
    )
    field, here, parts = call(
        finish_kernel,
        "smooth_and_restrict",
        (first, local, held, x_a, x_b),
        (shape(*cells), shape(2, 8, 128), shape(3, 2, 8, 128)),
        5_000_000,
    )
    count = lax.axis_size("gz")
    both = jnp.stack([parts, flip(parts, "gz", 1)])
    first_core = lax.axis_index("gz") % 2 == 0
    from_two = second_pairs(both[:, 1], "gx")
    from_one = far_or_beside(jnp.where(first_core, both[:, 0], both[:, 2]))
    smoothed, here = call(
        unpack_kernel,
        "unpack_modes",
        (field, here),
        (shape(*rhs.shape), shape(2, 8, 128)),
        200_000,
    )
    sums = (
        jnp.where(first_core, 0.0, inside("gx", -1) * inside("gx", 1)) * from_two
        + jnp.where(first_core, 1.0, inside("gx", -2)) * from_one
        + jnp.stack([here, jnp.zeros_like(here)])
    )
    chip = sums + flip(sums, "gz", 1)[::-1]
    from_beside = both_y_sides(chip[:, :, 4:].reshape(2, 8, 128)).reshape(2, 2, 4, 128)
    from_low = (lax.axis_index("gy") + lax.axis_index("gz")) % 2 == 1
    row = lax.broadcasted_iota(jnp.int32, (1, 1, 4, 1), 2)
    wanted = jnp.where(from_low, row < 2, row == 3)
    valid = jnp.where(from_low, inside("gy", -1), inside("gy", 1))
    edges = jnp.where(wanted, from_beside, 0.0) * valid
    edges = edges.reshape(2, 8, 128)
    mated = flip(edges, "gz", 1)
    owned = chip[:, :, :4].reshape(2, 8, 128) + edges + mated[::-1]
    third = flip(owned, "gz", 6)
    fetched = two_chips(owned)
    (column,) = call(
        column_kernel,
        "column",
        (owned, third, fetched, flip(fetched, "gz", 1)),
        (shape(1, 4, 128 * count),),
        20_000,
        scratch=(pltpu.VMEM((count + 2, 8, 128), jnp.float32),),
    )
    return smoothed, column


def solution(mesh):
    return jax.shard_map(
        per_device,
        mesh=mesh,
        in_specs=(P(None, None, None, "gx", "gy", "gz"), P("gx", "gy", "gz")),
        out_specs=(P(None, None, None, "gx", "gy", "gz"), P("gx", "gy", None)),
        check_vma=False,
    )
```
